32 devices in a mesh: member: 8 (over z, y), tile: 4 (over x, core).
Axes of the slice: x: 2, y: 2, z: 4, core: 2. Of those that a mesh axis runs over, the one named last changes fastest.
Arguments:
- realization_array: float32 [8, 4, 256, 512], P('member', None, 'tile'), may hold values from -6 to 6
- water_depth: float32 [256, 512], P('tile'), may hold values from 0.5 to 4
- wet_mask: int32 [256, 512], P('tile'), may hold values 0 or 1
- obs_cell: int32 [16384], P('tile'), may hold values from 0 to 32767, as said below
- obs_value: float32 [16384], P('tile'), may hold values from -8 to 8
- obs_error: float32 [16384], P('tile'), may hold values from 0.05 to 0.5
- celer_gain: float32 [16384], P('tile'), may hold values from 0.5 to 2
- obs_list: int32 [4, 128, 64], P('tile', 'member'), may hold values from 3584 to 8639, as said below
- obs_count: int32 [4, 128], P('tile', 'member'), may hold values from 32 to 64, as said below
Outputs:
- analysis: float32 [8, 4, 256, 512], P('member', None, 'tile')
The draws below stay inside these ranges and needn't reach their ends.
Inputs may be any that keep to these rules, and one draw needn't show every extreme that they name: `obs_cell`: observation o of a tile lies in cells o * S to o * S + S - 1 of that tile, S = 8. `obs_list`: the entries of one patch's list are distinct and name only observations of existing tiles. `obs_count`: some patch has a full list.
All inputs are finite; a program needn't handle non-finite values. No bound on the sum of `wet_mask` on one device may be relied on, other than what follows from the above.
Results may differ from the reference program's by a relative error of at most 0.0003.
Values sent between devices are 32-bit elements; how exact they have to be, the bound alone decides.
No kernel may reach another device: no remote copies, remote signals or barrier semaphores. Data moves between devices by JAX's collectives and lax.ppermute only.
A program may use at most 128 MiB of HBM per device.

```python
import math
import jax
import jax.numpy as jnp
from jax import lax

PANEL_LINES = 64
MESH_SPAN_NORTH = 512
OBS_TILE = 4096
OBS_PATCH = 64
REGION_POINTS = 256
STEPS = 4
NS_ITERS = 14
MEMBERS = 8
SHEET_PANELS = 4
NX = 256
OBS = 16384
REGIONS_IN_PANEL = 128


def draw_obs_cell(key, part):
    key = jax.random.fold_in(key, 11)
    spacing = PANEL_LINES * MESH_SPAN_NORTH // OBS_TILE
    order = jnp.arange(OBS, dtype=jnp.int32) % OBS_TILE
    jitter = jax.random.randint(key, (OBS,), 0, spacing, dtype=jnp.int32)
    return order * spacing + jitter


def draw_obs_list(key, part):
    key = jax.random.fold_in(key, 23)
    radius = OBS_TILE // 8
    tile_iota = jnp.arange(SHEET_PANELS, dtype=jnp.int32)[:, None]
    patch_iota = jnp.arange(REGIONS_IN_PANEL, dtype=jnp.int32)[None, :]
    row_index = patch_iota * REGION_POINTS // MESH_SPAN_NORTH
    centre = OBS_TILE + row_index * OBS_TILE // PANEL_LINES
    lowest = jnp.where(tile_iota == 0, OBS_TILE, 0)
    highest = jnp.where(tile_iota == SHEET_PANELS - 1, 2 * OBS_TILE - 2 * radius, 3 * OBS_TILE - 2 * radius)
    start = jnp.clip(centre - radius, lowest, highest)
    position = jnp.arange(2 * radius, dtype=jnp.int32)
    scores = jax.random.randint(key, (SHEET_PANELS, REGIONS_IN_PANEL, 2 * radius), 0, 2 ** 16, dtype=jnp.int32)
    scores = scores * (2 * radius) + position
    ends = (position == 0) | (position == 2 * radius - 1)
    scores = scores + jnp.where(ends, 2 ** 28, 0).astype(jnp.int32)
    offsets = jax.lax.top_k(scores, OBS_PATCH)[1].astype(jnp.int32)
    return start[:, :, None] + offsets


def draw_obs_count(key, part):
    key = jax.random.fold_in(key, 37)
    first, second = jax.random.split(key)
    counts = jax.random.randint(first, (SHEET_PANELS * REGIONS_IN_PANEL,), OBS_PATCH // 2, OBS_PATCH + 1, dtype=jnp.int32)
    chosen = jax.random.randint(second, (), 0, SHEET_PANELS * REGIONS_IN_PANEL, dtype=jnp.int32)
    counts = jnp.where(jnp.arange(SHEET_PANELS * REGIONS_IN_PANEL, dtype=jnp.int32) == chosen, OBS_PATCH, counts)
    return counts.reshape(SHEET_PANELS, REGIONS_IN_PANEL)


def place_ends(values, own_key, least, largest):
    longest = values.shape.index(max(values.shape))
    spots = []
    for shift in (0, 1):
        where = [jax.random.randint(jax.random.fold_in(own_key, axis), (), 0, length) for axis, length in enumerate(values.shape)]
        where[longest] = (where[longest] + shift) % values.shape[longest]
        spots.append(tuple(where))
    return values.at[spots[0]].set(least).at[spots[1]].set(largest)


def levels(rng, shape, cuts, least, top_value):
    loudness, own = 1.0, jax.random.fold_in(rng, 6)
    for axis_at, shards_of in cuts:
        draws = jnp.exp(jax.random.uniform(jax.random.fold_in(own, axis_at), (shards_of,), jnp.float32, least / len(cuts), top_value / len(cuts)))
        loudness = loudness * jnp.repeat(draws, shape[axis_at] // shards_of).reshape([-1 if axis == axis_at else 1 for axis in range(len(shape))])
    return loudness


def bell_draw(rng, extent, scale, bound, pieces=(), kind=jnp.bfloat16):
    entries = scale * jax.random.normal(rng, extent, jnp.float32)
    if pieces:
        entries = entries * levels(rng, extent, pieces, -0.22, 0.18)
    return jnp.clip(entries, -bound, bound).astype(kind)


def setup_inputs(seed: int = 0) -> dict:
    arg_keys = jax.random.split(jax.random.key(seed), 10)
    realization_array = bell_draw(arg_keys[0], (MEMBERS, 4, NX, MESH_SPAN_NORTH), 1.0, 6.0, ((0, 8), (2, 4)), jnp.float32)
    water_depth = jnp.clip(jnp.exp(math.log(4.0) - 2.0794415 * jax.random.uniform(arg_keys[1], (NX, MESH_SPAN_NORTH), jnp.float32) ** levels(arg_keys[1], (NX, MESH_SPAN_NORTH), ((0, 4),), -0.2, 0.2)), 0.5, 4.0)
    wet_mask = place_ends((jax.random.randint(arg_keys[2], (NX, MESH_SPAN_NORTH), 0, 8) < 7).astype(jnp.int32), jax.random.fold_in(arg_keys[2], 1), 0, 1)
    obs_cell = draw_obs_cell(jax.random.fold_in(arg_keys[9], 71), 0)
    obs_value = bell_draw(arg_keys[4], (OBS,), 1.5, 8.0, ((0, 4),), jnp.float32)
    obs_error = jnp.clip(jnp.exp(math.log(0.5) - 2.3025851 * jax.random.uniform(arg_keys[5], (OBS,), jnp.float32) ** levels(arg_keys[5], (OBS,), ((0, 4),), -0.2, 0.2)), 0.05, 0.5)
    celer_gain = jnp.clip(jnp.exp(math.log(2.0) - 1.3862944 * jax.random.uniform(arg_keys[6], (OBS,), jnp.float32) ** levels(arg_keys[6], (OBS,), ((0, 4),), -0.2, 0.2)), 0.5, 2.0)
    obs_list = draw_obs_list(jax.random.fold_in(arg_keys[9], 71), 0)
    obs_count = draw_obs_count(jax.random.fold_in(arg_keys[9], 71), 0)
    return dict(realization_array=realization_array, water_depth=water_depth, wet_mask=wet_mask, obs_cell=obs_cell, obs_value=obs_value, obs_error=obs_error, celer_gain=celer_gain, obs_list=obs_list, obs_count=obs_count)


FRICTION = 0.98
PRESSURE = 0.25
DIVERGE = 0.25
FORCING = 0.05
UPWIND = 0.4
DAMPING = 0.02
HIGH = lax.Precision.HIGHEST

def along_y(field):
    padded = jnp.pad(field, ((0, 0), (1, 1)))
    return (padded[:, 2:], padded[:, :-2])

def advance(water_elevation, eastward_velocity, northward_velocity, swell_intensity, water_depth, wet_float):
    level_pad = jnp.pad(water_elevation, ((1, 1), (0, 0)))
    new_x = wet_float * (FRICTION * eastward_velocity - PRESSURE * (level_pad[2:] - level_pad[:-2]))
    level_up, level_down = along_y(water_elevation)
    new_y = wet_float * (FRICTION * northward_velocity - PRESSURE * (level_up - level_down))
    flux_x = jnp.pad(water_depth * new_x, ((1, 1), (0, 0)))
    flux_up, flux_down = along_y(water_depth * new_y)
    new_surface = wet_float * (water_elevation - DIVERGE * (flux_x[2:] - flux_x[:-2] + flux_up - flux_down) + FORCING * swell_intensity)
    energy_pad = jnp.pad(swell_intensity, ((1, 0), (0, 0)))
    new_energy = wet_float * (swell_intensity - UPWIND * (swell_intensity - energy_pad[:-1]) - DAMPING * swell_intensity)
    return (new_surface, new_x, new_y, new_energy)

def mat_mul(left, right):
    return jnp.matmul(left, right, precision=HIGH)

def mix_weights(gram, proj):
    count = gram.shape[-1]
    eye = jnp.eye(count, dtype=jnp.float32)
    amat = gram + (count - 1.0) * eye
    trace_sum = jnp.trace(amat, axis1=1, axis2=2)
    current = amat / trace_sum[:, None, None]
    inverse = jnp.broadcast_to(eye, amat.shape)
    for sweep in range(NS_ITERS):
        factor = 1.5 * eye - 0.5 * mat_mul(inverse, current)
        current = mat_mul(current, factor)
        inverse = mat_mul(factor, inverse)
    root = inverse / jnp.sqrt(trace_sum)[:, None, None]
    covar = mat_mul(root, root)
    wbar = jnp.einsum('pkl,pl->pk', covar, proj, precision=HIGH)
    wtot = jnp.sqrt(count - 1.0) * root + wbar[:, :, None]
    return wtot - lax.optimization_barrier(jnp.mean(wtot, axis=1, keepdims=True)) + 1.0 / count

def reference(realization_array, water_depth, wet_mask, obs_cell, obs_value, obs_error, celer_gain, obs_list, obs_count):
    wet_float = wet_mask.astype(jnp.float32)

    def integrate_realization(state):
        water_elevation, eastward_velocity, northward_velocity, swell_intensity = (state[0], state[1], state[2], state[3])
        for sweep in range(STEPS):
            water_elevation, eastward_velocity, northward_velocity, swell_intensity = advance(water_elevation, eastward_velocity, northward_velocity, swell_intensity, water_depth, wet_float)
        return jnp.stack([water_elevation, eastward_velocity, northward_velocity, swell_intensity])
    predicted_fields = lax.map(integrate_realization, realization_array)
    realization_pile = predicted_fields.shape[0]
    elevation_panels = predicted_fields[:, 0].reshape(realization_pile, SHEET_PANELS, PANEL_LINES * MESH_SPAN_NORTH)
    cells = obs_cell.reshape(SHEET_PANELS, OBS_TILE)
    equivalents = jnp.take_along_axis(elevation_panels, cells[None], axis=2) * celer_gain.reshape(SHEET_PANELS, OBS_TILE)[None]
    equivalents = equivalents.reshape(realization_pile, OBS)
    tile_iota = jnp.arange(SHEET_PANELS, dtype=jnp.int32)[:, None, None]
    global_idx = (tile_iota * OBS_TILE - OBS_TILE + obs_list).astype(jnp.int32)
    picked = equivalents[:, global_idx]
    value = obs_value[global_idx]
    error = obs_error[global_idx]
    patch_iota = jnp.arange(REGIONS_IN_PANEL, dtype=jnp.int32)
    row_index = patch_iota * REGION_POINTS // MESH_SPAN_NORTH
    centre = OBS_TILE + row_index * OBS_TILE // PANEL_LINES
    radius = OBS_TILE // 8
    dist = (obs_list - centre[None, :, None]).astype(jnp.float32) / radius
    live = jnp.arange(OBS_PATCH, dtype=jnp.int32)[None, None, :] < obs_count[:, :, None]
    precision = jnp.where(live, 1.0 / ((1.0 + 4.0 * dist * dist) * error), 0.0)
    mean_eq = lax.optimization_barrier(jnp.mean(picked, axis=0))
    spread = picked - mean_eq[None]
    gram = jnp.einsum('ktpo,ltpo->tpkl', spread * precision[None], spread, precision=HIGH)
    proj = jnp.einsum('ktpo,tpo->tpk', spread, precision * (value - mean_eq), precision=HIGH)
    mix = mix_weights(gram.reshape(SHEET_PANELS * REGIONS_IN_PANEL, realization_pile, realization_pile), proj.reshape(SHEET_PANELS * REGIONS_IN_PANEL, realization_pile))
    mix = mix.reshape(SHEET_PANELS, REGIONS_IN_PANEL, realization_pile, realization_pile)
    panel_sequence = predicted_fields.reshape(realization_pile, 4, SHEET_PANELS, REGIONS_IN_PANEL, REGION_POINTS)
    analysis = jnp.einsum('kftpc,tpkm->mftpc', panel_sequence, mix, precision=HIGH)
    return analysis.reshape(realization_pile, 4, NX, MESH_SPAN_NORTH)
```

```python
import functools

import jax
import jax.numpy as jnp
from jax import lax
from jax.experimental import pallas as pl
from jax.experimental.pallas import tpu as pltpu
from jax.sharding import PartitionSpec as P

REGION_POINTS = 256
STEPS = 4
NS_ITERS = 14
CELLS_PER_OBS = 8
LANES = 128

FRICTION = 0.98
PRESSURE = 0.25
DIVERGE = 0.25
FORCING = 0.05
UPWIND = 0.4
DAMPING = 0.02
HIGH = lax.Precision.HIGHEST

PAD = 8


def iota(shape, dim):
    return lax.broadcasted_iota(jnp.int32, shape, dim)


def forecast_kernel(
    sizes,
    state_ref,
    depth_ref,
    mask_ref,
    cell_ref,
    gain_ref,
    low_ref,
    high_ref,
    out_ref,
    s_ref,
    u_ref,
    v_ref,
    e_ref,
    h_ref,
    w_ref,
    flux_ref,
    part_ref,
    cell_win,
    gain_win,
    level_ref,
):
    members, own_rows, halo, obs_halo = sizes
    rows, width = depth_ref.shape
    total = rows + 2 * halo
    first = PAD + halo
    fields = (s_ref, u_ref, v_ref, e_ref, h_ref, w_ref)
    for i, field in enumerate(fields):
        field[PAD : PAD + halo, :] = low_ref[i * halo : (i + 1) * halo, :]
        field[first + rows : first + rows + halo, :] = high_ref[i * halo : (i + 1) * halo, :]
        if i < 4:
            field[first : first + rows, :] = state_ref[i]
    h_ref[first : first + rows, :] = depth_ref[...]
    w_ref[first : first + rows, :] = mask_ref[...].astype(jnp.float32)
    edge = jnp.zeros((PAD, width), jnp.float32)
    for field in (s_ref, e_ref, flux_ref):
        field[0:PAD, :] = edge
        field[PAD + total : PAD + total + PAD, :] = edge

    column = iota((8, width), 1)
    not_first = column > 0
    not_last = column < width - 1

    def next_col(x):
        return jnp.where(not_last, pltpu.roll(x, width - 1, 1), 0.0)

    def prev_col(x):
        return jnp.where(not_first, pltpu.roll(x, 1, 1), 0.0)

    for step in range(STEPS):
        for block in range(total // 8):
            r = PAD + 8 * block
            here = pl.ds(r, 8)
            s, e, w, h = s_ref[here, :], e_ref[here, :], w_ref[here, :], h_ref[here, :]
            slope = s_ref[pl.ds(r + 1, 8), :] - s_ref[pl.ds(r - 1, 8), :]
            u = w * (FRICTION * u_ref[here, :] - PRESSURE * slope)
            u_ref[here, :] = u
            flux_ref[here, :] = h * u
            v = w * (FRICTION * v_ref[here, :] - PRESSURE * (next_col(s) - prev_col(s)))
            v_ref[here, :] = v
            flux = h * v
            part_ref[here, :] = s - DIVERGE * (next_col(flux) - prev_col(flux)) + FORCING * e
        for block in reversed(range(total // 8)):
            r = PAD + 8 * block
            here = pl.ds(r, 8)
            w = w_ref[here, :]
            rise = flux_ref[pl.ds(r + 1, 8), :] - flux_ref[pl.ds(r - 1, 8), :]
            s_ref[here, :] = w * (part_ref[here, :] - DIVERGE * rise)
            e = e_ref[here, :]
            e_ref[here, :] = w * (e - UPWIND * (e - e_ref[pl.ds(r - 1, 8), :]) - DAMPING * e)

    span = obs_halo // LANES
    inner = cell_ref.shape[0]
    window = inner + 2 * span
    base = 6 * halo
    for j, (win, own) in enumerate(((cell_win, cell_ref), (gain_win, gain_ref))):
        win[span : span + inner, :] = own[...].astype(jnp.float32)
        for i in range(span):
            lanes = slice(i * LANES, (i + 1) * LANES)
            win[i : i + 1, :] = low_ref[base + j : base + j + 1, lanes]
            win[span + inner + i : span + inner + i + 1, :] = high_ref[base + j : base + j + 1, lanes]
    cell = cell_win[0:window, :]
    half = width // CELLS_PER_OBS
    top = first - obs_halo // half
    equiv = jnp.zeros((window, LANES), jnp.float32)
    lane_cell = (iota((window, LANES), 1) % CELLS_PER_OBS).astype(jnp.float32)
    group = LANES // CELLS_PER_OBS
    for q in range(width // LANES):
        level_ref[...] = s_ref[top : top + 2 * window, q * LANES : (q + 1) * LANES]
        for parity in range(2):
            shift = parity * half + q * group
            spread = (iota((LANES, LANES), 0) == iota((LANES, LANES), 1) // CELLS_PER_OBS + shift).astype(jnp.float32)
            gather = (iota((LANES, LANES), 1) == iota((LANES, LANES), 0) // CELLS_PER_OBS + shift).astype(jnp.float32)
            offset = jnp.dot(cell, spread, preferred_element_type=jnp.float32, precision=HIGH)
            level = level_ref[pl.ds(parity, window, stride=2), :]
            chosen = jnp.where(jnp.abs(offset - lane_cell) < 0.5, level, 0.0)
            equiv = equiv + jnp.dot(chosen, gather, preferred_element_type=jnp.float32, precision=HIGH)
    equiv = equiv * gain_win[0:window, :]

    pieces = width // LANES
    for j in range(members):
        source = first + j * own_rows
        for i in range(4):
            for q in range(pieces):
                target = (i * pieces + q) * own_rows
                out_ref[j, target : target + own_rows, :] = fields[i][
                    source : source + own_rows, q * LANES : (q + 1) * LANES
                ]
        out_ref[j, 4 * pieces * own_rows : 4 * pieces * own_rows + window, :] = equiv


def group_matmul(left, right, starts, members):
    total = None
    for k in range(members):
        column = jnp.take_along_axis(left, starts + k, axis=1, mode="promise_in_bounds")
        term = column * right[k : k + 1, :]
        total = term if total is None else total + term
    return total


def analysis_kernel(
    sizes,
    recv_ref,
    spot_ref,
    damp_ref,
    live_ref,
    value_ref,
    error_ref,
    low_ref,
    high_ref,
    out_ref,
    value_win,
    error_win,
    table_ref,
):
    members, own_rows, halo, obs_halo, pieces = sizes
    stride = recv_ref.shape[0] // members
    body_rows = 4 * pieces * own_rows
    span = obs_halo // LANES
    inner = value_ref.shape[0]
    window = inner + 2 * span
    base = 6 * halo + 2
    for j, (win, own) in enumerate(((value_win, value_ref), (error_win, error_ref))):
        win[span : span + inner, :] = own[...]
        for i in range(span):
            lanes = slice(i * LANES, (i + 1) * LANES)
            win[i : i + 1, :] = low_ref[base + j : base + j + 1, lanes]
            win[span + inner + i : span + inner + i + 1, :] = high_ref[base + j : base + j + 1, lanes]

    spot = spot_ref[...]
    pairs = spot.shape[0]
    row, lane = spot // LANES, spot % LANES
    rows_of = [jnp.broadcast_to(row[i : i + 1, :], (members, LANES)) for i in range(pairs)]
    lanes_of = [jnp.broadcast_to(lane[i : i + 1, :], (members, LANES)) for i in range(pairs)]
    picked = [jnp.zeros((members, LANES), jnp.float32) for i in range(pairs)]
    value = jnp.zeros((pairs, LANES), jnp.float32)
    error = jnp.zeros((pairs, LANES), jnp.float32)
    for r in range(window):
        source = recv_ref[pl.ds(body_rows + r, members, stride=stride), :]
        for i in range(pairs):
            got = jnp.take_along_axis(source, lanes_of[i], axis=1, mode="promise_in_bounds")
            picked[i] = jnp.where(rows_of[i] == r, got, picked[i])
        hit = row == r
        for name, win in (("value", value_win), ("error", error_win)):
            line = jnp.broadcast_to(win[r : r + 1, :], (pairs, LANES))
            got = jnp.take_along_axis(line, lane, axis=1, mode="promise_in_bounds")
            if name == "value":
                value = jnp.where(hit, got, value)
            else:
                error = jnp.where(hit, got, error)
    precision = jnp.where(live_ref[...] > 0.0, 1.0 / (damp_ref[...] * error), 0.0)

    left_half = iota((members, LANES), 1) < LANES // 2
    weighted, spreads, innovations = [], [], []
    for i in range(pairs):
        mean = jnp.sum(picked[i], axis=0, keepdims=True) * (1.0 / members)
        spread = picked[i] - mean
        scaled = spread * precision[i : i + 1, :]
        innovation = jnp.broadcast_to(value[i : i + 1, :] - mean, (members, LANES))
        weighted += [jnp.where(left_half, scaled, 0.0), jnp.where(left_half, 0.0, scaled)]
        spreads += [spread, spread]
        innovations += [innovation, innovation]
    every = lax.dot_general(
        jnp.concatenate(weighted, axis=0),
        jnp.concatenate(spreads + innovations, axis=0),
        (((1,), (1,)), ((), ())),
        preferred_element_type=jnp.float32,
        precision=HIGH,
    )
    lane_at = iota((members, LANES), 1)
    patch_at = lane_at // members
    gram = jnp.zeros((members, LANES), jnp.float32)
    proj = jnp.zeros((members, LANES), jnp.float32)
    for p in range(2 * pairs):
        mine = patch_at == p
        block = every[p * members : (p + 1) * members, :]
        gram = jnp.where(mine, block[:, :LANES], gram)
        proj = jnp.where(mine, block[:, LANES:], proj)

    starts = lane_at - lane_at % members
    eye = (lane_at % members == iota((members, LANES), 0)).astype(jnp.float32)
    amat = gram + (members - 1.0) * eye
    trace = group_matmul(
        jnp.broadcast_to(jnp.sum(amat * eye, axis=0, keepdims=True), (members, LANES)),
        jnp.ones((members, LANES), jnp.float32),
        starts,
        members,
    )

    def iterate(sweep, carry):
        current, inverse = carry
        factor = 1.5 * eye - 0.5 * group_matmul(inverse, current, starts, members)
        return (
            group_matmul(current, factor, starts, members),
            group_matmul(factor, inverse, starts, members),
        )

    current, inverse = lax.fori_loop(0, NS_ITERS, iterate, (amat / trace, eye), unroll=members <= 8)
    root = inverse / jnp.sqrt(trace)
    wbar = group_matmul(root, group_matmul(root, proj, starts, members), starts, members)
    wtot = ((members - 1.0) ** 0.5) * root + wbar
    mix = wtot - jnp.sum(wtot, axis=0, keepdims=True) * (1.0 / members) + 1.0 / members
    table_ref[...] = mix.T

    def analyse(m, carry):
        for side in range(2):
            coefs = table_ref[pl.ds(side * members + m, own_rows, stride=2 * members), :]
            columns = [
                jnp.broadcast_to(coefs[:, k : k + 1], (own_rows, LANES)) for k in range(members)
            ]
            for i in range(4):
                for q in range(side * pieces // 2, (side + 1) * pieces // 2):
                    start = (i * pieces + q) * own_rows
                    total = None
                    for k in range(members):
                        term = columns[k] * recv_ref[pl.ds(k * stride + start, own_rows), :]
                        total = term if total is None else total + term
                    out_ref[m, i, :, q * LANES : (q + 1) * LANES] = total
        return carry

    if members <= 8:
        for m in range(members):
            analyse(m, 0)
    else:
        lax.fori_loop(0, members, analyse, 0)


def exchange(low, high):
    count = lax.axis_size("tile")
    forward = [(i, i + 1) for i in range(count - 1)]
    backward = [(target, source) for source, target in forward]
    return lax.ppermute(low, "tile", forward), lax.ppermute(high, "tile", backward)


def vmem_specs(count):
    return [pl.BlockSpec(memory_space=pltpu.VMEM)] * count


def body(
    realization_array,
    water_depth,
    wet_mask,
    obs_cell,
    obs_value,
    obs_error,
    celer_gain,
    obs_list,
    obs_count,
):
    members = lax.axis_size("member")
    rows, width = water_depth.shape
    obs_tile = obs_cell.shape[0]
    radius = obs_tile // 8
    halo = radius * CELLS_PER_OBS // width + 2 * STEPS
    per_dev, slots = obs_list.shape[1:]
    own_rows = per_dev * REGION_POINTS // width
    pieces = width // LANES
    state = realization_array[0]
    wet_float = wet_mask.astype(jnp.float32)
    offset = (obs_cell % CELLS_PER_OBS).astype(jnp.float32)

    def edge(rows_of, obs_of):
        grid = jnp.concatenate([state, water_depth[None], wet_float[None]], axis=0)[:, rows_of, :]
        obs = jnp.stack([x[obs_of] for x in (offset, celer_gain, obs_value, obs_error)])
        return jnp.concatenate(
            [grid.reshape(6 * halo, width), obs.reshape(4 * radius // width, width)], axis=0
        )

    low, high = exchange(
        edge(slice(rows - halo, rows), slice(obs_tile - radius, obs_tile)),
        edge(slice(0, halo), slice(0, radius)),
    )

    window = (obs_tile + 2 * radius) // LANES
    packet = 4 * pieces * own_rows + window
    grid = (rows + 2 * halo + 2 * PAD, width)
    panel = (obs_tile // LANES, LANES)
    sends = pl.pallas_call(
        functools.partial(forecast_kernel, (members, own_rows, halo, radius)),
        out_shape=jax.ShapeDtypeStruct((members, packet, LANES), jnp.float32),
        in_specs=vmem_specs(7),
        out_specs=pl.BlockSpec(memory_space=pltpu.VMEM),
        scratch_shapes=[pltpu.VMEM(grid, jnp.float32)] * 8
        + [pltpu.VMEM((window, LANES), jnp.float32)] * 2
        + [pltpu.VMEM((2 * window, LANES), jnp.float32)],
        compiler_params=pltpu.CompilerParams(vmem_limit_bytes=24 * 2**20),
        name="forecast",
    )(
        state,
        water_depth,
        wet_mask,
        offset.reshape(panel),
        celer_gain.reshape(panel),
        low,
        high,
    )
    received = lax.all_to_all(sends, "member", split_axis=0, concat_axis=0, tiled=True)

    pairs = per_dev * slots // LANES
    patch_index = lax.axis_index("member") * per_dev + jnp.arange(per_dev, dtype=jnp.int32)
    row_index = patch_index * REGION_POINTS // width
    centre = obs_tile + row_index * obs_tile // rows
    dist = (obs_list[0] - centre[:, None]).astype(jnp.float32) / radius
    damp = 1.0 + 4.0 * dist * dist
    live = jnp.arange(slots, dtype=jnp.int32)[None, :] < obs_count[0][:, None]
    spot = obs_list[0] - (obs_tile - radius)
    analysed = pl.pallas_call(
        functools.partial(analysis_kernel, (members, own_rows, halo, radius, pieces)),
        out_shape=jax.ShapeDtypeStruct((members, 4, own_rows, width), jnp.float32),
        in_specs=vmem_specs(8),
        out_specs=pl.BlockSpec(memory_space=pltpu.VMEM),
        scratch_shapes=[pltpu.VMEM((window, LANES), jnp.float32)] * 2
        + [pltpu.VMEM((LANES, members), jnp.float32)],
        compiler_params=pltpu.CompilerParams(vmem_limit_bytes=24 * 2**20),
        name="analysis",
    )(
        received.reshape(members * packet, LANES),
        spot.reshape(pairs, LANES),
        damp.reshape(pairs, LANES),
        live.astype(jnp.float32).reshape(pairs, LANES),
        obs_value.reshape(panel),
        obs_error.reshape(panel),
        low,
        high,
    )
    result = lax.all_to_all(analysed, "member", split_axis=0, concat_axis=0, tiled=True)
    return jnp.transpose(result, (1, 0, 2, 3)).reshape(1, 4, rows, width)


def solution(mesh):
    return jax.shard_map(
        body,
        mesh=mesh,
        in_specs=(
            P("member", None, "tile", None),
            P("tile", None),
            P("tile", None),
            P("tile"),
            P("tile"),
            P("tile"),
            P("tile"),
            P("tile", "member", None),
            P("tile", "member"),
        ),
        out_specs=P("member", None, "tile", None),
        check_vma=False,
    )
```

```python
import functools

import jax
import jax.numpy as jnp
from jax import lax
from jax.experimental import pallas as pl
from jax.experimental.pallas import tpu as pltpu
from jax.sharding import PartitionSpec as P

REGION_POINTS = 256
STEPS = 4
NS_ITERS = 14
CELLS_PER_OBS = 8
LANES = 128

FRICTION = 0.98
PRESSURE = 0.25
DIVERGE = 0.25
FORCING = 0.05
UPWIND = 0.4
DAMPING = 0.02
HIGH = lax.Precision.HIGHEST

PAD = 8


def iota(shape, dim):
    return lax.broadcasted_iota(jnp.int32, shape, dim)


def edge_kernel(halo, *refs):
    grids, obs, outs = refs[:3], refs[3:7], refs[7:9]
    wet_ref, cell_ref, sems = refs[9:]
    rows = grids[1].shape[0]
    inner = obs[0].shape[0]
    even = lax.axis_index("tile") % 2 == 0
    copies = []

    def fetch(source, target):
        copies.append(pltpu.make_async_copy(source, target, sems.at[len(copies)]))
        copies[-1].start()

    for side, out in enumerate(outs):
        is_last = even if side == 0 else jnp.logical_not(even)
        start = pl.multiple_of(jnp.where(is_last, rows - halo, 0), 8)
        for i in range(6):
            source = (grids[0].at[i] if i < 4 else grids[i - 3]).at[pl.ds(start, halo), :]
            fetch(source, out.at[pl.ds(i * halo, halo), :] if i < 5 else wet_ref.at[side])
        start = pl.multiple_of(jnp.where(is_last, inner - 8, 0), 8)
        for j in range(4):
            target = out.at[pl.ds(6 * halo, 8), pl.ds(j * LANES, LANES)] if j else cell_ref.at[side]
            fetch(obs[j].at[pl.ds(start, 8), :], target)
    for copy in copies:
        copy.wait()
    for side, out in enumerate(outs):
        out[5 * halo : 6 * halo, :] = wet_ref[side].astype(jnp.float32)
        out[6 * halo : 6 * halo + 8, 0:LANES] = (cell_ref[side] % CELLS_PER_OBS).astype(jnp.float32)


def side_by_side(x, pairs):
    return jnp.concatenate([x[:pairs], x[pairs:]], axis=1)


def window_parts(win, own, near_ref, far_ref, base, j, even):
    inner = own.shape[0]
    span = (win.shape[0] - inner) // 2
    lanes = slice(j * LANES, (j + 1) * LANES)
    near, far = near_ref[base : base + 8, lanes], far_ref[base : base + 8, lanes]
    win[0:span, :] = jnp.where(even, far, near)[8 - span :, :]
    win[span : span + inner, :] = own
    win[span + inner :, :] = jnp.where(even, near, far)[:span, :]


def forecast_kernel(
    sizes,
    state_ref,
    depth_ref,
    mask_ref,
    cell_ref,
    gain_ref,
    near_ref,
    far_ref,
    out_ref,
    equiv_ref,
    s_ref,
    u_ref,
    v_ref,
    e_ref,
    h_ref,
    w_ref,
    flux_ref,
    part_ref,
    cell_win,
    gain_win,
):
    members, own_rows, halo, obs_halo = sizes
    even = lax.axis_index("tile") % 2 == 0
    rows, width = depth_ref.shape
    pieces = width // LANES
    total = rows + 2 * halo
    first = PAD + halo
    own = pl.ds(first, rows)
    fields = (s_ref, u_ref, v_ref, e_ref, h_ref, w_ref)
    near_at = pl.multiple_of(jnp.where(even, first + rows, PAD), 8)
    far_at = pl.multiple_of(jnp.where(even, PAD, first + rows), 8)
    edge = jnp.zeros((PAD, LANES), jnp.float32)
    for q in range(pieces):
        lanes = slice(q * LANES, (q + 1) * LANES)
        for i, field in enumerate(fields):
            field[q, pl.ds(near_at, halo), :] = near_ref[i * halo : (i + 1) * halo, lanes]
            field[q, pl.ds(far_at, halo), :] = far_ref[i * halo : (i + 1) * halo, lanes]
            if i < 4:
                field[q, own, :] = state_ref[i, :, lanes]
        h_ref[q, own, :] = depth_ref[:, lanes]
        w_ref[q, own, :] = mask_ref[:, lanes].astype(jnp.float32)
        for field in (s_ref, e_ref, flux_ref):
            field[q, 0:PAD, :] = edge
            field[q, PAD + total : PAD + total + PAD, :] = edge

    lane = iota((8, LANES), 1)
    at_first, at_last = lane == 0, lane == LANES - 1

    def across(x):
        ahead = [pltpu.roll(piece, LANES - 1, 1) for piece in x] + [0.0]
        behind = [0.0] + [pltpu.roll(piece, 1, 1) for piece in x]
        return [
            jnp.where(at_last, ahead[q + 1], ahead[q]) - jnp.where(at_first, behind[q], behind[q + 1])
            for q in range(pieces)
        ]

    for step in range(STEPS):
        for block in range(total // 8):
            r = PAD + 8 * block
            here, below, above = pl.ds(r, 8), pl.ds(r + 1, 8), pl.ds(r - 1, 8)
            s = [s_ref[q, here, :] for q in range(pieces)]
            slope = across(s)
            flux = []
            for q in range(pieces):
                w, h = w_ref[q, here, :], h_ref[q, here, :]
                u = w * (FRICTION * u_ref[q, here, :] - PRESSURE * (s_ref[q, below, :] - s_ref[q, above, :]))
                u_ref[q, here, :] = u
                flux_ref[q, here, :] = h * u
                v = w * (FRICTION * v_ref[q, here, :] - PRESSURE * slope[q])
                v_ref[q, here, :] = v
                flux.append(h * v)
            rise = across(flux)
            for q in range(pieces):
                part_ref[q, here, :] = s[q] - DIVERGE * rise[q] + FORCING * e_ref[q, here, :]
        for block in reversed(range(total // 8)):
            r = PAD + 8 * block
            here, below, above = pl.ds(r, 8), pl.ds(r + 1, 8), pl.ds(r - 1, 8)
            for q in range(pieces):
                w = w_ref[q, here, :]
                rise = flux_ref[q, below, :] - flux_ref[q, above, :]
                s_ref[q, here, :] = w * (part_ref[q, here, :] - DIVERGE * rise)
                e = e_ref[q, here, :]
                e_ref[q, here, :] = w * (e - UPWIND * (e - e_ref[q, above, :]) - DAMPING * e)

    window = cell_win.shape[0]
    base = 6 * halo
    offsets = (cell_ref[...] % CELLS_PER_OBS).astype(jnp.float32)
    window_parts(cell_win, offsets, near_ref, far_ref, base, 0, even)
    window_parts(gain_win, gain_ref[...], near_ref, far_ref, base, 1, even)
    half = width // CELLS_PER_OBS
    top = first - obs_halo // half
    column = iota((LANES, 2 * width), 1)
    cell_at = column // (2 * LANES) * LANES + column % LANES
    parity = column // LANES % 2
    spread = jnp.where(
        iota((LANES, 2 * width), 0) == parity * half + cell_at // CELLS_PER_OBS, 1.0, 0.0
    ).astype(jnp.bfloat16)
    offset = jnp.dot(cell_win[...].astype(jnp.bfloat16), spread, preferred_element_type=jnp.float32)
    level = jnp.concatenate(
        [s_ref[q, pl.ds(top + side, window, stride=2), :] for q in range(pieces) for side in range(2)], axis=1
    )
    place = (iota((window, 2 * width), 1) % CELLS_PER_OBS).astype(jnp.float32)
    rest = jnp.where(jnp.abs(offset - place) < 0.5, level, 0.0)
    equiv = jnp.zeros((window, LANES), jnp.float32)
    parts = []
    for i in range(3):
        parts.append(rest.astype(jnp.bfloat16))
        rest = rest - parts[-1].astype(jnp.float32)
    for part in reversed(parts):
        equiv = equiv + lax.dot_general(
            part, spread, (((1,), (1,)), ((), ())), preferred_element_type=jnp.float32
        )
    equiv_ref[...] = equiv * gain_win[...]

    for j in range(members):
        source = first + j * own_rows
        for i in range(4):
            for q in range(pieces):
                target = (i * pieces + q) * own_rows
                out_ref[j, target : target + own_rows, :] = fields[i][q, source : source + own_rows, :]


def group_columns(left, starts, members):
    return [jnp.take_along_axis(left, starts + k, axis=1, mode="promise_in_bounds") for k in range(members)]


def group_matmul(columns, right):
    terms = [column * right[k : k + 1, :] for k, column in enumerate(columns)]
    while len(terms) > 1:
        terms = [a + b for a, b in zip(terms[::2], terms[1::2])]
    return terms[0]


def relative(index, members):
    bits = members.bit_length() - 1
    return sum(((index >> i) & 1) << (bits - 1 - i) for i in range(bits))


def weight_kernel(
    sizes,
    equiv_ref,
    spot_ref,
    damp_ref,
    live_ref,
    value_ref,
    error_ref,
    near_ref,
    far_ref,
    mix_ref,
    value_win,
    error_win,
):
    members, halo = sizes
    window = value_win.shape[0]
    even = lax.axis_index("tile") % 2 == 0
    window_parts(value_win, value_ref[...], near_ref, far_ref, 6 * halo, 2, even)
    window_parts(error_win, error_ref[...], near_ref, far_ref, 6 * halo, 3, even)

    spot = spot_ref[...]
    pairs = spot.shape[0]
    row, lane = spot // LANES, spot % LANES
    rows_of = [jnp.broadcast_to(row[i : i + 1, :], (members, LANES)) for i in range(pairs)]
    lanes_of = [jnp.broadcast_to(lane[i : i + 1, :], (members, LANES)) for i in range(pairs)]
    picked = [jnp.zeros((members, LANES), jnp.float32) for i in range(pairs)]
    value = jnp.zeros((pairs, LANES), jnp.float32)
    error = jnp.zeros((pairs, LANES), jnp.float32)
    for r in range(window):
        source = equiv_ref[pl.ds(r, members, stride=window), :]
        for i in range(pairs):
            got = jnp.take_along_axis(source, lanes_of[i], axis=1, mode="promise_in_bounds")
            picked[i] = jnp.where(rows_of[i] == r, got, picked[i])
        hit = row == r
        line = jnp.broadcast_to(value_win[r : r + 1, :], spot.shape)
        value = jnp.where(hit, jnp.take_along_axis(line, lane, axis=1, mode="promise_in_bounds"), value)
        line = jnp.broadcast_to(error_win[r : r + 1, :], spot.shape)
        error = jnp.where(hit, jnp.take_along_axis(line, lane, axis=1, mode="promise_in_bounds"), error)
    precision = jnp.where(live_ref[...] > 0.0, 1.0 / (damp_ref[...] * error), 0.0)

    left_half = iota((members, LANES), 1) < LANES // 2
    weighted, spreads, innovations = [], [], []
    for i in range(pairs):
        mean = jnp.sum(picked[i], axis=0, keepdims=True) * (1.0 / members)
        spread = picked[i] - mean
        scaled = spread * precision[i : i + 1, :]
        innovation = jnp.broadcast_to(value[i : i + 1, :] - mean, (members, LANES))
        weighted.append(scaled)
        spreads.append(spread)
        innovations.append(innovation)
    every = lax.dot_general(
        jnp.concatenate(
            [jnp.where(left_half, x, 0.0) for x in weighted] + [jnp.where(left_half, 0.0, x) for x in weighted],
            axis=0,
        ),
        jnp.concatenate(spreads + spreads + innovations + innovations, axis=0),
        (((1,), (1,)), ((), ())),
        preferred_element_type=jnp.float32,
        precision=HIGH,
    )
    lane_at = iota((members, LANES), 1)
    patch_at = lane_at // members
    gram = jnp.zeros((members, LANES), jnp.float32)
    proj = jnp.zeros((members, LANES), jnp.float32)
    for p in range(2 * pairs):
        mine = patch_at == p
        block = every[p * members : (p + 1) * members, :]
        gram = jnp.where(mine, block[:, :LANES], gram)
        proj = jnp.where(mine, block[:, LANES:], proj)

    starts = lane_at - lane_at % members
    eye = (lane_at % members == iota((members, LANES), 0)).astype(jnp.float32)
    amat = gram + (members - 1.0) * eye
    diagonal = jnp.broadcast_to(jnp.sum(amat * eye, axis=0, keepdims=True), (members, LANES))
    trace = functools.reduce(jnp.add, group_columns(diagonal, starts, members))

    def iterate(sweep, carry):
        product, inverse = carry
        columns = group_columns(product, starts, members)
        square = group_matmul(columns, product)
        cube = group_matmul(columns, square)
        return (
            2.25 * product - 1.5 * square + 0.25 * cube,
            1.5 * inverse - 0.5 * group_matmul(columns, inverse),
        )

    product, inverse = lax.fori_loop(0, NS_ITERS, iterate, (amat / trace, eye), unroll=members <= 8)
    root = inverse / jnp.sqrt(trace)
    columns = group_columns(root, starts, members)
    wbar = group_matmul(columns, group_matmul(columns, proj))
    wtot = ((members - 1.0) ** 0.5) * root + wbar
    mix = wtot - jnp.sum(wtot, axis=0, keepdims=True) * (1.0 / members) + 1.0 / members
    mix_ref[...] = mix


def mix_kernel(sizes, recv_ref, mix_ref, out_ref, table_ref):
    members, own_rows, pieces = sizes
    stride = recv_ref.shape[0] // members
    me = lax.axis_index("member")
    table_ref[...] = mix_ref[...].T
    bases = [pl.multiple_of((me ^ relative(k, members)) * stride, 8) for k in range(members)]

    def analyse(m, carry):
        target = me ^ relative(m, members)
        for side in range(2):
            coefs = table_ref[pl.ds(side * members + m, own_rows, stride=2 * members), :]
            columns = [
                jnp.broadcast_to(coefs[:, k : k + 1], (own_rows, LANES)) for k in range(members)
            ]
            for i in range(4):
                for q in range(side * pieces // 2, (side + 1) * pieces // 2):
                    start = (i * pieces + q) * own_rows
                    total = None
                    for k in range(members):
                        term = columns[k] * recv_ref[pl.ds(bases[k] + start, own_rows), :]
                        total = term if total is None else total + term
                    out_ref[target, i, :, q * LANES : (q + 1) * LANES] = total
        return carry

    if members <= 8:
        for m in range(members):
            analyse(m, 0)
    else:
        lax.fori_loop(0, members, analyse, 0)


def gather_members(block):
    members = lax.axis_size("member")
    held = block[None]
    distance = members // 2
    while distance:
        pairs = [(i, i ^ distance) for i in range(members)]
        held = jnp.concatenate([held, lax.ppermute(held, "member", pairs)], axis=0)
        distance //= 2
    return held


def swaps(near, far):
    count = lax.axis_size("tile")

    def pairs(start):
        twos = [(i, i + 1) for i in range(start, count - 1, 2)]
        return twos + [(b, a) for a, b in twos]

    far = lax.ppermute(far, "tile", pairs(1))
    near = lax.ppermute(near, "tile", pairs(0))
    return near, far


def vmem_specs(count):
    return [pl.BlockSpec(memory_space=pltpu.VMEM)] * count


def body(
    realization_array,
    water_depth,
    wet_mask,
    obs_cell,
    obs_value,
    obs_error,
    celer_gain,
    obs_list,
    obs_count,
):
    members = lax.axis_size("member")
    rows, width = water_depth.shape
    obs_tile = obs_cell.shape[0]
    radius = obs_tile // 8
    halo = radius * CELLS_PER_OBS // width + 2 * STEPS
    per_dev, slots = obs_list.shape[1:]
    own_rows = per_dev * REGION_POINTS // width
    pieces = width // LANES
    state = realization_array[0]
    panel = (obs_tile // LANES, LANES)
    pairs = per_dev * slots // LANES
    edges = pl.pallas_call(
        functools.partial(edge_kernel, halo),
        out_shape=[jax.ShapeDtypeStruct((6 * halo + 8, width), jnp.float32)] * 2,
        in_specs=[pl.BlockSpec(memory_space=pl.ANY)] * 7,
        out_specs=vmem_specs(2),
        scratch_shapes=[
            pltpu.VMEM((2, halo, width), jnp.int32),
            pltpu.VMEM((2, 8, LANES), jnp.int32),
            pltpu.SemaphoreType.DMA((20,)),
        ],
        name="edges",
    )(
        state,
        water_depth,
        wet_mask,
        obs_cell.reshape(panel),
        celer_gain.reshape(panel),
        obs_value.reshape(panel),
        obs_error.reshape(panel),
    )
    near, far = swaps(*edges)

    window = (obs_tile + 2 * radius) // LANES
    packet = 4 * pieces * own_rows
    grid = (pieces, rows + 2 * halo + 2 * PAD, LANES)
    sends, equiv = pl.pallas_call(
        functools.partial(forecast_kernel, (members, own_rows, halo, radius)),
        out_shape=[
            jax.ShapeDtypeStruct((members, packet, LANES), jnp.float32),
            jax.ShapeDtypeStruct((window, LANES), jnp.float32),
        ],
        in_specs=vmem_specs(7),
        out_specs=vmem_specs(2),
        scratch_shapes=[pltpu.VMEM(grid, jnp.float32)] * 8 + [pltpu.VMEM((window, LANES), jnp.float32)] * 2,
        compiler_params=pltpu.CompilerParams(vmem_limit_bytes=24 * 2**20),
        name="forecast",
    )(
        state,
        water_depth,
        wet_mask,
        obs_cell.reshape(panel),
        celer_gain.reshape(panel),
        near,
        far,
    )
    received = lax.all_to_all(sends, "member", split_axis=0, concat_axis=0, tiled=True)
    equivs = gather_members(equiv)

    patch_index = lax.axis_index("member") * per_dev + jnp.arange(per_dev, dtype=jnp.int32)
    row_index = patch_index * REGION_POINTS // width
    centre = obs_tile + row_index * obs_tile // rows
    dist = (obs_list[0] - centre[:, None]).astype(jnp.float32) / radius
    damp = 1.0 + 4.0 * dist * dist
    live = jnp.arange(slots, dtype=jnp.int32)[None, :] < obs_count[0][:, None]
    spot = side_by_side(obs_list[0] - (obs_tile - radius), pairs)
    mix = pl.pallas_call(
        functools.partial(weight_kernel, (members, halo)),
        out_shape=jax.ShapeDtypeStruct((members, LANES), jnp.float32),
        in_specs=vmem_specs(8),
        out_specs=vmem_specs(1)[0],
        scratch_shapes=[pltpu.VMEM((window, LANES), jnp.float32)] * 2,
        compiler_params=pltpu.CompilerParams(vmem_limit_bytes=24 * 2**20),
        name="weights",
    )(
        equivs.reshape(members * window, LANES),
        spot,
        side_by_side(damp, pairs),
        side_by_side(live.astype(jnp.float32), pairs),
        obs_value.reshape(panel),
        obs_error.reshape(panel),
        near,
        far,
    )
    analysed = pl.pallas_call(
        functools.partial(mix_kernel, (members, own_rows, pieces)),
        out_shape=jax.ShapeDtypeStruct((members, 4, own_rows, width), jnp.float32),
        in_specs=vmem_specs(2),
        out_specs=vmem_specs(1)[0],
        scratch_shapes=[pltpu.VMEM((LANES, members), jnp.float32)],
        compiler_params=pltpu.CompilerParams(vmem_limit_bytes=24 * 2**20),
        name="mix",
    )(received.reshape(members * packet, LANES), mix)
    result = lax.all_to_all(analysed, "member", split_axis=0, concat_axis=0, tiled=True)
    return jnp.transpose(result, (1, 0, 2, 3)).reshape(1, 4, rows, width)


def solution(mesh):
    return jax.shard_map(
        body,
        mesh=mesh,
        in_specs=(
            P("member", None, "tile", None),
            P("tile", None),
            P("tile", None),
            P("tile"),
            P("tile"),
            P("tile"),
            P("tile"),
            P("tile", "member", None),
            P("tile", "member"),
        ),
        out_specs=P("member", None, "tile", None),
        check_vma=False,
    )
```

```python
import functools

import jax
import jax.numpy as jnp
from jax import lax
from jax.experimental import pallas as pl
from jax.experimental.pallas import tpu as pltpu
from jax.sharding import PartitionSpec as P

REGION_POINTS = 256
STEPS = 4
NS_ITERS = 14
CELLS_PER_OBS = 8
LANES = 128

FRICTION = 0.98
PRESSURE = 0.25
DIVERGE = 0.25
FORCING = 0.05
UPWIND = 0.4
DAMPING = 0.02
HIGH = lax.Precision.HIGHEST

PAD = 8
PACKED = 2


def iota(shape, dim):
    return lax.broadcasted_iota(jnp.int32, shape, dim)


def edge_kernel(halo, *refs):
    grids, obs, outs = refs[:3], refs[3:7], refs[7:9]
    wet_ref, cell_ref, sems = refs[9:]
    rows = grids[1].shape[0]
    inner = obs[0].shape[0]
    even = lax.axis_index("tile") % 2 == 0
    copies = []

    def fetch(source, target):
        copies.append(pltpu.make_async_copy(source, target, sems.at[len(copies)]))
        copies[-1].start()

    for side, out in enumerate(outs):
        is_last = even if side == 0 else jnp.logical_not(even)
        start = pl.multiple_of(jnp.where(is_last, rows - halo, 0), 8)
        for i in range(6):
            source = (grids[0].at[i] if i < 4 else grids[i - 3]).at[pl.ds(start, halo), :]
            fetch(source, out.at[pl.ds(i * halo, halo), :] if i < 5 else wet_ref.at[side])
        start = pl.multiple_of(jnp.where(is_last, inner - 8, 0), 8)
        for j in range(4):
            target = out.at[pl.ds(6 * halo, 8), pl.ds(j * LANES, LANES)] if j else cell_ref.at[side]
            fetch(obs[j].at[pl.ds(start, 8), :], target)
    for copy in copies:
        copy.wait()
    for side, out in enumerate(outs):
        out[5 * halo : 6 * halo, :] = wet_ref[side].astype(jnp.float32)
        out[6 * halo : 6 * halo + 8, 0:LANES] = (cell_ref[side] % CELLS_PER_OBS).astype(jnp.float32)


def side_by_side(x, pairs):
    return jnp.concatenate([x[:pairs], x[pairs:]], axis=1)


def window_parts(win, own, near_ref, far_ref, base, j, even):
    inner = own.shape[0]
    span = (win.shape[0] - inner) // 2
    lanes = slice(j * LANES, (j + 1) * LANES)
    near, far = near_ref[base : base + 8, lanes], far_ref[base : base + 8, lanes]
    win[0:span, :] = jnp.where(even, far, near)[8 - span :, :]
    win[span : span + inner, :] = own
    win[span + inner :, :] = jnp.where(even, near, far)[:span, :]


def forecast_kernel(
    sizes,
    state_ref,
    depth_ref,
    mask_ref,
    cell_ref,
    gain_ref,
    near_ref,
    far_ref,
    *refs,
):
    members, own_rows, halo, obs_halo = sizes
    out_ref, rest_refs, scratch = refs[0], refs[1 : members + 1], refs[members + 1 :]
    s_ref, u_ref, v_ref, e_ref, h_ref, w_ref, flux_ref, part_ref, cell_win, gain_win = scratch
    even = lax.axis_index("tile") % 2 == 0
    rows, width = depth_ref.shape
    pieces = width // LANES
    total = rows + 2 * halo
    first = PAD + halo
    own = pl.ds(first, rows)
    fields = (s_ref, u_ref, v_ref, e_ref, h_ref, w_ref)
    near_at = pl.multiple_of(jnp.where(even, first + rows, PAD), 8)
    far_at = pl.multiple_of(jnp.where(even, PAD, first + rows), 8)
    edge = jnp.zeros((PAD, LANES), jnp.float32)
    for q in range(pieces):
        lanes = slice(q * LANES, (q + 1) * LANES)
        for i, field in enumerate(fields):
            field[q, pl.ds(near_at, halo), :] = near_ref[i * halo : (i + 1) * halo, lanes]
            field[q, pl.ds(far_at, halo), :] = far_ref[i * halo : (i + 1) * halo, lanes]
            if i < 4:
                field[q, own, :] = state_ref[i, :, lanes]
        h_ref[q, own, :] = depth_ref[:, lanes]
        w_ref[q, own, :] = mask_ref[:, lanes].astype(jnp.float32)
        for field in (s_ref, e_ref, flux_ref):
            field[q, 0:PAD, :] = edge
            field[q, PAD + total : PAD + total + PAD, :] = edge

    lane = iota((8, LANES), 1)
    at_first, at_last = lane == 0, lane == LANES - 1

    def across(x):
        ahead = [pltpu.roll(piece, LANES - 1, 1) for piece in x] + [0.0]
        behind = [0.0] + [pltpu.roll(piece, 1, 1) for piece in x]
        return [
            jnp.where(at_last, ahead[q + 1], ahead[q]) - jnp.where(at_first, behind[q], behind[q + 1])
            for q in range(pieces)
        ]

    for step in range(STEPS):
        for block in range(total // 8):
            r = PAD + 8 * block
            here, below, above = pl.ds(r, 8), pl.ds(r + 1, 8), pl.ds(r - 1, 8)
            s = [s_ref[q, here, :] for q in range(pieces)]
            slope = across(s)
            flux = []
            for q in range(pieces):
                w, h = w_ref[q, here, :], h_ref[q, here, :]
                u = w * (FRICTION * u_ref[q, here, :] - PRESSURE * (s_ref[q, below, :] - s_ref[q, above, :]))
                u_ref[q, here, :] = u
                flux_ref[q, here, :] = h * u
                v = w * (FRICTION * v_ref[q, here, :] - PRESSURE * slope[q])
                v_ref[q, here, :] = v
                flux.append(h * v)
            rise = across(flux)
            for q in range(pieces):
                part_ref[q, here, :] = s[q] - DIVERGE * rise[q] + FORCING * e_ref[q, here, :]
        for block in reversed(range(total // 8)):
            r = PAD + 8 * block
            here, below, above = pl.ds(r, 8), pl.ds(r + 1, 8), pl.ds(r - 1, 8)
            for q in range(pieces):
                w = w_ref[q, here, :]
                rise = flux_ref[q, below, :] - flux_ref[q, above, :]
                s_ref[q, here, :] = w * (part_ref[q, here, :] - DIVERGE * rise)
                e = e_ref[q, here, :]
                e_ref[q, here, :] = w * (e - UPWIND * (e - e_ref[q, above, :]) - DAMPING * e)

    window = cell_win.shape[0]
    base = 6 * halo
    offsets = (cell_ref[...] % CELLS_PER_OBS).astype(jnp.float32)
    window_parts(cell_win, offsets, near_ref, far_ref, base, 0, even)
    window_parts(gain_win, gain_ref[...], near_ref, far_ref, base, 1, even)
    half = width // CELLS_PER_OBS
    top = first - obs_halo // half
    column = iota((LANES, 2 * width), 1)
    cell_at = column // (2 * LANES) * LANES + column % LANES
    parity = column // LANES % 2
    spread = jnp.where(
        iota((LANES, 2 * width), 0) == parity * half + cell_at // CELLS_PER_OBS, 1.0, 0.0
    ).astype(jnp.bfloat16)
    offset = jnp.dot(cell_win[...].astype(jnp.bfloat16), spread, preferred_element_type=jnp.float32)
    level = jnp.concatenate(
        [s_ref[q, pl.ds(top + side, window, stride=2), :] for q in range(pieces) for side in range(2)], axis=1
    )
    place = (iota((window, 2 * width), 1) % CELLS_PER_OBS).astype(jnp.float32)
    rest = jnp.where(jnp.abs(offset - place) < 0.5, level, 0.0)
    equiv = jnp.zeros((window, LANES), jnp.float32)
    parts = []
    for i in range(3):
        parts.append(rest.astype(jnp.bfloat16))
        rest = rest - parts[-1].astype(jnp.float32)
    for part in reversed(parts):
        equiv = equiv + lax.dot_general(
            part, spread, (((1,), (1,)), ((), ())), preferred_element_type=jnp.float32
        )
    equiv = equiv * gain_win[...]

    me = lax.axis_index("member")
    for j in range(members):
        source = first + j * own_rows
        for i in range(PACKED):
            for q in range(pieces):
                target = (i * pieces + q) * own_rows
                out_ref[j, target : target + own_rows, :] = fields[i][q, source : source + own_rows, :]
        body_rows = PACKED * pieces * own_rows
        out_ref[j, body_rows : body_rows + window, :] = equiv
        source = pl.multiple_of(first + (me ^ j) * own_rows, min(own_rows, 8))
        for i in range(PACKED, 4):
            for q in range(pieces):
                target = ((i - PACKED) * pieces + q) * own_rows
                rest_refs[j][target : target + own_rows, :] = fields[i][q, pl.ds(source, own_rows), :]


def group_columns(left, starts, members):
    return [jnp.take_along_axis(left, starts + k, axis=1, mode="promise_in_bounds") for k in range(members)]


def group_matmul(columns, right):
    terms = [column * right[k : k + 1, :] for k, column in enumerate(columns)]
    while len(terms) > 1:
        terms = [a + b for a, b in zip(terms[::2], terms[1::2])]
    return terms[0]


def weight_kernel(
    sizes,
    recv_ref,
    spot_ref,
    damp_ref,
    live_ref,
    value_ref,
    error_ref,
    near_ref,
    far_ref,
    mix_ref,
    value_win,
    error_win,
):
    members, halo = sizes
    window = value_win.shape[0]
    stride = recv_ref.shape[0] // members
    even = lax.axis_index("tile") % 2 == 0
    window_parts(value_win, value_ref[...], near_ref, far_ref, 6 * halo, 2, even)
    window_parts(error_win, error_ref[...], near_ref, far_ref, 6 * halo, 3, even)

    spot = spot_ref[...]
    pairs = spot.shape[0]
    row, lane = spot // LANES, spot % LANES
    rows_of = [jnp.broadcast_to(row[i : i + 1, :], (members, LANES)) for i in range(pairs)]
    lanes_of = [jnp.broadcast_to(lane[i : i + 1, :], (members, LANES)) for i in range(pairs)]
    picked = [jnp.zeros((members, LANES), jnp.float32) for i in range(pairs)]
    value = jnp.zeros((pairs, LANES), jnp.float32)
    error = jnp.zeros((pairs, LANES), jnp.float32)
    for r in range(window):
        source = recv_ref[pl.ds(stride - window + r, members, stride=stride), :]
        for i in range(pairs):
            got = jnp.take_along_axis(source, lanes_of[i], axis=1, mode="promise_in_bounds")
            picked[i] = jnp.where(rows_of[i] == r, got, picked[i])
        hit = row == r
        line = jnp.broadcast_to(value_win[r : r + 1, :], spot.shape)
        value = jnp.where(hit, jnp.take_along_axis(line, lane, axis=1, mode="promise_in_bounds"), value)
        line = jnp.broadcast_to(error_win[r : r + 1, :], spot.shape)
        error = jnp.where(hit, jnp.take_along_axis(line, lane, axis=1, mode="promise_in_bounds"), error)
    precision = jnp.where(live_ref[...] > 0.0, 1.0 / (damp_ref[...] * error), 0.0)

    left_half = iota((members, LANES), 1) < LANES // 2
    weighted, spreads, innovations = [], [], []
    for i in range(pairs):
        mean = jnp.sum(picked[i], axis=0, keepdims=True) * (1.0 / members)
        spread = picked[i] - mean
        scaled = spread * precision[i : i + 1, :]
        innovation = jnp.broadcast_to(value[i : i + 1, :] - mean, (members, LANES))
        weighted.append(scaled)
        spreads.append(spread)
        innovations.append(innovation)
    every = lax.dot_general(
        jnp.concatenate(
            [jnp.where(left_half, x, 0.0) for x in weighted] + [jnp.where(left_half, 0.0, x) for x in weighted],
            axis=0,
        ),
        jnp.concatenate(spreads + spreads + innovations + innovations, axis=0),
        (((1,), (1,)), ((), ())),
        preferred_element_type=jnp.float32,
        precision=HIGH,
    )
    lane_at = iota((members, LANES), 1)
    patch_at = lane_at // members
    gram = jnp.zeros((members, LANES), jnp.float32)
    proj = jnp.zeros((members, LANES), jnp.float32)
    for p in range(2 * pairs):
        mine = patch_at == p
        block = every[p * members : (p + 1) * members, :]
        gram = jnp.where(mine, block[:, :LANES], gram)
        proj = jnp.where(mine, block[:, LANES:], proj)

    starts = lane_at - lane_at % members
    eye = (lane_at % members == iota((members, LANES), 0)).astype(jnp.float32)
    amat = gram + (members - 1.0) * eye
    diagonal = jnp.broadcast_to(jnp.sum(amat * eye, axis=0, keepdims=True), (members, LANES))
    trace = functools.reduce(jnp.add, group_columns(diagonal, starts, members))

    def iterate(sweep, carry):
        product, inverse = carry
        columns = group_columns(product, starts, members)
        square = group_matmul(columns, product)
        cube = group_matmul(columns, square)
        return (
            2.25 * product - 1.5 * square + 0.25 * cube,
            1.5 * inverse - 0.5 * group_matmul(columns, inverse),
        )

    product, inverse = lax.fori_loop(0, NS_ITERS, iterate, (amat / trace, eye), unroll=members <= 8)
    root = inverse / jnp.sqrt(trace)
    columns = group_columns(root, starts, members)
    wbar = group_matmul(columns, group_matmul(columns, proj))
    wtot = ((members - 1.0) ** 0.5) * root + wbar
    mix = wtot - jnp.sum(wtot, axis=0, keepdims=True) * (1.0 / members) + 1.0 / members
    mix_ref[...] = mix


def mix_kernel(sizes, recv_ref, mix_ref, *refs):
    members, own_rows, pieces = sizes
    rest_refs, (out_ref, table_ref) = refs[:members], refs[members:]
    stride = recv_ref.shape[0] // members
    me = lax.axis_index("member")
    order = (iota((members, members), 0) == iota((members, members), 1) ^ me).astype(jnp.float32)
    table_ref[...] = lax.dot_general(
        mix_ref[...], order, (((0,), (0,)), ((), ())), preferred_element_type=jnp.float32, precision=HIGH
    )
    bases = [pl.multiple_of((me ^ d) * stride, 8) for d in range(members)]

    def analyse(m, carry):
        for side in range(2):
            coefs = table_ref[pl.ds(side * members + m, own_rows, stride=2 * members), :]
            columns = [jnp.broadcast_to(coefs[:, d : d + 1], (own_rows, LANES)) for d in range(members)]
            for i in range(4):
                for q in range(side * pieces // 2, (side + 1) * pieces // 2):
                    total = None
                    for d in range(members):
                        if i < PACKED:
                            start = (i * pieces + q) * own_rows
                            block = recv_ref[pl.ds(bases[d] + start, own_rows), :]
                        else:
                            start = ((i - PACKED) * pieces + q) * own_rows
                            block = rest_refs[d][start : start + own_rows, :]
                        term = columns[d] * block
                        total = term if total is None else total + term
                    out_ref[m, i, :, q * LANES : (q + 1) * LANES] = total
        return carry

    if members <= 8:
        for m in range(members):
            analyse(m, 0)
    else:
        lax.fori_loop(0, members, analyse, 0)


def trade(blocks):
    members = len(blocks)
    held = list(blocks)
    for d in reversed(range(1, members)):
        held[d] = lax.ppermute(blocks[d], "member", [(i, i ^ d) for i in range(members)])
    return held


def swaps(near, far):
    count = lax.axis_size("tile")

    def pairs(start):
        twos = [(i, i + 1) for i in range(start, count - 1, 2)]
        return twos + [(b, a) for a, b in twos]

    far = lax.ppermute(far, "tile", pairs(1))
    near = lax.ppermute(near, "tile", pairs(0))
    return near, far


def vmem_specs(count):
    return [pl.BlockSpec(memory_space=pltpu.VMEM)] * count


def body(
    realization_array,
    water_depth,
    wet_mask,
    obs_cell,
    obs_value,
    obs_error,
    celer_gain,
    obs_list,
    obs_count,
):
    members = lax.axis_size("member")
    rows, width = water_depth.shape
    obs_tile = obs_cell.shape[0]
    radius = obs_tile // 8
    halo = radius * CELLS_PER_OBS // width + 2 * STEPS
    per_dev, slots = obs_list.shape[1:]
    own_rows = per_dev * REGION_POINTS // width
    pieces = width // LANES
    state = realization_array[0]
    panel = (obs_tile // LANES, LANES)
    pairs = per_dev * slots // LANES
    edges = pl.pallas_call(
        functools.partial(edge_kernel, halo),
        out_shape=[jax.ShapeDtypeStruct((6 * halo + 8, width), jnp.float32)] * 2,
        in_specs=[pl.BlockSpec(memory_space=pl.ANY)] * 7,
        out_specs=vmem_specs(2),
        scratch_shapes=[
            pltpu.VMEM((2, halo, width), jnp.int32),
            pltpu.VMEM((2, 8, LANES), jnp.int32),
            pltpu.SemaphoreType.DMA((20,)),
        ],
        name="edges",
    )(
        state,
        water_depth,
        wet_mask,
        obs_cell.reshape(panel),
        celer_gain.reshape(panel),
        obs_value.reshape(panel),
        obs_error.reshape(panel),
    )
    near, far = swaps(*edges)

    window = (obs_tile + 2 * radius) // LANES
    packet = PACKED * pieces * own_rows + window
    grid = (pieces, rows + 2 * halo + 2 * PAD, LANES)
    sends, *rest = pl.pallas_call(
        functools.partial(forecast_kernel, (members, own_rows, halo, radius)),
        out_shape=[
            jax.ShapeDtypeStruct((members, packet, LANES), jnp.float32),
        ]
        + [jax.ShapeDtypeStruct(((4 - PACKED) * pieces * own_rows, LANES), jnp.float32)] * members,
        in_specs=vmem_specs(7),
        out_specs=vmem_specs(1 + members),
        scratch_shapes=[pltpu.VMEM(grid, jnp.float32)] * 8 + [pltpu.VMEM((window, LANES), jnp.float32)] * 2,
        compiler_params=pltpu.CompilerParams(vmem_limit_bytes=24 * 2**20),
        name="forecast",
    )(
        state,
        water_depth,
        wet_mask,
        obs_cell.reshape(panel),
        celer_gain.reshape(panel),
        near,
        far,
    )
    received = lax.all_to_all(sends, "member", split_axis=0, concat_axis=0, tiled=True)
    rest = trade(rest)
    received = received.reshape(members * packet, LANES)

    patch_index = lax.axis_index("member") * per_dev + jnp.arange(per_dev, dtype=jnp.int32)
    row_index = patch_index * REGION_POINTS // width
    centre = obs_tile + row_index * obs_tile // rows
    dist = (obs_list[0] - centre[:, None]).astype(jnp.float32) / radius
    damp = 1.0 + 4.0 * dist * dist
    live = jnp.arange(slots, dtype=jnp.int32)[None, :] < obs_count[0][:, None]
    spot = side_by_side(obs_list[0] - (obs_tile - radius), pairs)
    mix = pl.pallas_call(
        functools.partial(weight_kernel, (members, halo)),
        out_shape=jax.ShapeDtypeStruct((members, LANES), jnp.float32),
        in_specs=vmem_specs(8),
        out_specs=vmem_specs(1)[0],
        scratch_shapes=[pltpu.VMEM((window, LANES), jnp.float32)] * 2,
        compiler_params=pltpu.CompilerParams(vmem_limit_bytes=24 * 2**20),
        name="weights",
    )(
        received,
        spot,
        side_by_side(damp, pairs),
        side_by_side(live.astype(jnp.float32), pairs),
        obs_value.reshape(panel),
        obs_error.reshape(panel),
        near,
        far,
    )
    analysed = pl.pallas_call(
        functools.partial(mix_kernel, (members, own_rows, pieces)),
        out_shape=jax.ShapeDtypeStruct((members, 4, own_rows, width), jnp.float32),
        in_specs=vmem_specs(2 + members),
        out_specs=vmem_specs(1)[0],
        scratch_shapes=[pltpu.VMEM((LANES, members), jnp.float32)],
        compiler_params=pltpu.CompilerParams(vmem_limit_bytes=24 * 2**20),
        name="mix",
    )(received, mix, *rest)
    result = lax.all_to_all(analysed, "member", split_axis=0, concat_axis=0, tiled=True)
    return jnp.transpose(result, (1, 0, 2, 3)).reshape(1, 4, rows, width)


def solution(mesh):
    return jax.shard_map(
        body,
        mesh=mesh,
        in_specs=(
            P("member", None, "tile", None),
            P("tile", None),
            P("tile", None),
            P("tile"),
            P("tile"),
            P("tile"),
            P("tile"),
            P("tile", "member", None),
            P("tile", "member"),
        ),
        out_specs=P("member", None, "tile", None),
        check_vma=False,
    )
```

```python
import functools

import jax
import jax.numpy as jnp
from jax import lax
from jax.experimental import pallas as pl
from jax.experimental.pallas import tpu as pltpu
from jax.sharding import PartitionSpec as P

REGION_POINTS = 256
STEPS = 4
NS_ITERS = 14
CELLS_PER_OBS = 8
LANES = 128

FRICTION = 0.98
PRESSURE = 0.25
DIVERGE = 0.25
FORCING = 0.05
UPWIND = 0.4
DAMPING = 0.02
HIGH = lax.Precision.HIGHEST

PAD = 8
PACKED = 2


def iota(shape, dim):
    return lax.broadcasted_iota(jnp.int32, shape, dim)


def edge_kernel(halo, *refs):
    grids, obs, outs = refs[:3], refs[3:7], refs[7:9]
    buf_ref, wet_ref, cell_ref, in_sems, out_sems = refs[9:]
    rows = grids[1].shape[0]
    inner = obs[0].shape[0]
    even = lax.axis_index("tile") % 2 == 0
    fetches, stores = [], []

    def fetch(source, target):
        fetches.append(pltpu.make_async_copy(source, target, in_sems.at[len(fetches)]))
        fetches[-1].start()

    def store(side, start, count):
        span = pl.ds(start, count)
        copy = pltpu.make_async_copy(buf_ref.at[side, span, :], outs[side].at[span, :], out_sems.at[len(stores)])
        stores.append(copy)
        copy.start()

    is_last = [even, jnp.logical_not(even)]
    for i in (5, 0, 1, 2, 3, 4):
        for side in range(2):
            start = pl.multiple_of(jnp.where(is_last[side], rows - halo, 0), 8)
            source = (grids[0].at[i] if i < 4 else grids[i - 3]).at[pl.ds(start, halo), :]
            fetch(source, buf_ref.at[side, pl.ds(i * halo, halo), :] if i < 5 else wet_ref.at[side])
    for j in range(4):
        for side in range(2):
            start = pl.multiple_of(jnp.where(is_last[side], inner - 8, 0), 8)
            target = buf_ref.at[side, pl.ds(6 * halo, 8), pl.ds(j * LANES, LANES)] if j else cell_ref.at[side]
            fetch(obs[j].at[pl.ds(start, 8), :], target)
    for at, copy in enumerate(fetches):
        copy.wait()
        side = at % 2
        if at < 2:
            buf_ref[side, 5 * halo : 6 * halo, :] = wet_ref[side].astype(jnp.float32)
            store(side, 5 * halo, halo)
        elif at < 12:
            store(side, (at // 2 - 1) * halo, halo)
        elif at < 14:
            buf_ref[side, 6 * halo : 6 * halo + 8, 0:LANES] = (cell_ref[side] % CELLS_PER_OBS).astype(jnp.float32)
        elif at >= 18:
            store(side, 6 * halo, 8)
    for copy in stores:
        copy.wait()


def side_by_side(x, pairs):
    return jnp.concatenate([x[:pairs], x[pairs:]], axis=1)


def window_parts(win, own, near_ref, far_ref, base, j, even):
    inner = own.shape[0]
    span = (win.shape[0] - inner) // 2
    lanes = slice(j * LANES, (j + 1) * LANES)
    near, far = near_ref[base : base + 8, lanes], far_ref[base : base + 8, lanes]
    win[0:span, :] = jnp.where(even, far, near)[8 - span :, :]
    win[span : span + inner, :] = own
    win[span + inner :, :] = jnp.where(even, near, far)[:span, :]


def forecast_kernel(
    sizes,
    state_ref,
    depth_ref,
    mask_ref,
    cell_ref,
    gain_ref,
    near_ref,
    far_ref,
    *refs,
):
    members, own_rows, halo, obs_halo = sizes
    out_ref, rest_refs, scratch = refs[0], refs[1 : members + 1], refs[members + 1 :]
    s_ref, u_ref, v_ref, e_ref, h_ref, w_ref, flux_ref, part_ref, cell_win, gain_win, pack_ref, equiv_buf, sems = scratch
    even = lax.axis_index("tile") % 2 == 0
    rows, width = depth_ref.shape
    pieces = width // LANES
    total = rows + 2 * halo
    first = PAD + halo
    own = pl.ds(first, rows)
    fields = (s_ref, u_ref, v_ref, e_ref, h_ref, w_ref)
    near_at = pl.multiple_of(jnp.where(even, first + rows, PAD), 8)
    far_at = pl.multiple_of(jnp.where(even, PAD, first + rows), 8)
    edge = jnp.zeros((PAD, LANES), jnp.float32)
    for q in range(pieces):
        lanes = slice(q * LANES, (q + 1) * LANES)
        for i, field in enumerate(fields):
            field[q, pl.ds(near_at, halo), :] = near_ref[i * halo : (i + 1) * halo, lanes]
            field[q, pl.ds(far_at, halo), :] = far_ref[i * halo : (i + 1) * halo, lanes]
            if i < 4:
                field[q, own, :] = state_ref[i, :, lanes]
        h_ref[q, own, :] = depth_ref[:, lanes]
        w_ref[q, own, :] = mask_ref[:, lanes].astype(jnp.float32)
        for field in (s_ref, e_ref, flux_ref):
            field[q, 0:PAD, :] = edge
            field[q, PAD + total : PAD + total + PAD, :] = edge

    lane = iota((8, LANES), 1)
    at_first, at_last = lane == 0, lane == LANES - 1

    def across(x):
        ahead = [pltpu.roll(piece, LANES - 1, 1) for piece in x] + [0.0]
        behind = [0.0] + [pltpu.roll(piece, 1, 1) for piece in x]
        return [
            jnp.where(at_last, ahead[q + 1], ahead[q]) - jnp.where(at_first, behind[q], behind[q + 1])
            for q in range(pieces)
        ]

    for step in range(STEPS):
        for block in range(total // 8):
            r = PAD + 8 * block
            here, below, above = pl.ds(r, 8), pl.ds(r + 1, 8), pl.ds(r - 1, 8)
            s = [s_ref[q, here, :] for q in range(pieces)]
            slope = across(s)
            flux = []
            for q in range(pieces):
                w, h = w_ref[q, here, :], h_ref[q, here, :]
                u = w * (FRICTION * u_ref[q, here, :] - PRESSURE * (s_ref[q, below, :] - s_ref[q, above, :]))
                u_ref[q, here, :] = u
                flux_ref[q, here, :] = h * u
                v = w * (FRICTION * v_ref[q, here, :] - PRESSURE * slope[q])
                v_ref[q, here, :] = v
                flux.append(h * v)
            rise = across(flux)
            for q in range(pieces):
                part_ref[q, here, :] = s[q] - DIVERGE * rise[q] + FORCING * e_ref[q, here, :]
        for block in reversed(range(total // 8)):
            r = PAD + 8 * block
            here, below, above = pl.ds(r, 8), pl.ds(r + 1, 8), pl.ds(r - 1, 8)
            for q in range(pieces):
                w = w_ref[q, here, :]
                rise = flux_ref[q, below, :] - flux_ref[q, above, :]
                s_ref[q, here, :] = w * (part_ref[q, here, :] - DIVERGE * rise)
                e = e_ref[q, here, :]
                e_ref[q, here, :] = w * (e - UPWIND * (e - e_ref[q, above, :]) - DAMPING * e)

    me = lax.axis_index("member")
    copies = []
    for j in range(members):
        source = first + j * own_rows
        for i in range(PACKED):
            for q in range(pieces):
                target = (i * pieces + q) * own_rows
                pack_ref[j, target : target + own_rows, :] = fields[i][q, source : source + own_rows, :]
        target = out_ref.at[j, pl.ds(0, PACKED * pieces * own_rows), :]
        copies.append(pltpu.make_async_copy(pack_ref.at[j], target, sems.at[j]))
        copies[-1].start()
    for j in range(members):
        source = pl.multiple_of(first + (me ^ j) * own_rows, min(own_rows, 8))
        for i in range(PACKED, 4):
            for q in range(pieces):
                target = ((i - PACKED) * pieces + q) * own_rows
                rest_refs[j][target : target + own_rows, :] = fields[i][q, pl.ds(source, own_rows), :]

    window = cell_win.shape[0]
    base = 6 * halo
    offsets = (cell_ref[...] % CELLS_PER_OBS).astype(jnp.float32)
    window_parts(cell_win, offsets, near_ref, far_ref, base, 0, even)
    window_parts(gain_win, gain_ref[...], near_ref, far_ref, base, 1, even)
    half = width // CELLS_PER_OBS
    top = first - obs_halo // half
    column = iota((LANES, 2 * width), 1)
    cell_at = column // (2 * LANES) * LANES + column % LANES
    parity = column // LANES % 2
    spread = jnp.where(
        iota((LANES, 2 * width), 0) == parity * half + cell_at // CELLS_PER_OBS, 1.0, 0.0
    ).astype(jnp.bfloat16)
    offset = jnp.dot(cell_win[...].astype(jnp.bfloat16), spread, preferred_element_type=jnp.float32)
    level = jnp.concatenate(
        [s_ref[q, pl.ds(top + side, window, stride=2), :] for q in range(pieces) for side in range(2)], axis=1
    )
    place = (iota((window, 2 * width), 1) % CELLS_PER_OBS).astype(jnp.float32)
    rest = jnp.where(jnp.abs(offset - place) < 0.5, level, 0.0)
    equiv = jnp.zeros((window, LANES), jnp.float32)
    parts = []
    for i in range(3):
        parts.append(rest.astype(jnp.bfloat16))
        rest = rest - parts[-1].astype(jnp.float32)
    for part in reversed(parts):
        equiv = equiv + lax.dot_general(
            part, spread, (((1,), (1,)), ((), ())), preferred_element_type=jnp.float32
        )
    equiv = equiv * gain_win[...]

    equiv_buf[...] = equiv
    body_rows = PACKED * pieces * own_rows
    for j in range(members):
        target = out_ref.at[j, pl.ds(body_rows, window), :]
        copies.append(pltpu.make_async_copy(equiv_buf, target, sems.at[members + j]))
        copies[-1].start()
    for copy in copies:
        copy.wait()


def group_columns(left, starts, members):
    return [jnp.take_along_axis(left, starts + k, axis=1, mode="promise_in_bounds") for k in range(members)]


def group_matmul(columns, right):
    terms = [column * right[k : k + 1, :] for k, column in enumerate(columns)]
    while len(terms) > 1:
        terms = [a + b for a, b in zip(terms[::2], terms[1::2])]
    return terms[0]


def weight_kernel(
    sizes,
    recv_ref,
    spot_ref,
    damp_ref,
    live_ref,
    value_ref,
    error_ref,
    near_ref,
    far_ref,
    mix_ref,
    value_win,
    error_win,
):
    members, halo = sizes
    window = value_win.shape[0]
    stride = recv_ref.shape[0] // members
    even = lax.axis_index("tile") % 2 == 0
    window_parts(value_win, value_ref[...], near_ref, far_ref, 6 * halo, 2, even)
    window_parts(error_win, error_ref[...], near_ref, far_ref, 6 * halo, 3, even)

    spot = spot_ref[...]
    pairs = spot.shape[0]
    row, lane = spot // LANES, spot % LANES
    rows_of = [jnp.broadcast_to(row[i : i + 1, :], (members, LANES)) for i in range(pairs)]
    lanes_of = [jnp.broadcast_to(lane[i : i + 1, :], (members, LANES)) for i in range(pairs)]
    picked = [jnp.zeros((members, LANES), jnp.float32) for i in range(pairs)]
    value = jnp.zeros((pairs, LANES), jnp.float32)
    error = jnp.zeros((pairs, LANES), jnp.float32)
    for r in range(window):
        source = recv_ref[pl.ds(stride - window + r, members, stride=stride), :]
        for i in range(pairs):
            got = jnp.take_along_axis(source, lanes_of[i], axis=1, mode="promise_in_bounds")
            picked[i] = jnp.where(rows_of[i] == r, got, picked[i])
        hit = row == r
        line = jnp.broadcast_to(value_win[r : r + 1, :], spot.shape)
        value = jnp.where(hit, jnp.take_along_axis(line, lane, axis=1, mode="promise_in_bounds"), value)
        line = jnp.broadcast_to(error_win[r : r + 1, :], spot.shape)
        error = jnp.where(hit, jnp.take_along_axis(line, lane, axis=1, mode="promise_in_bounds"), error)
    precision = jnp.where(live_ref[...] > 0.0, 1.0 / (damp_ref[...] * error), 0.0)

    left_half = iota((members, LANES), 1) < LANES // 2
    weighted, spreads, innovations = [], [], []
    for i in range(pairs):
        mean = jnp.sum(picked[i], axis=0, keepdims=True) * (1.0 / members)
        spread = picked[i] - mean
        scaled = spread * precision[i : i + 1, :]
        innovation = jnp.broadcast_to(value[i : i + 1, :] - mean, (members, LANES))
        weighted.append(scaled)
        spreads.append(spread)
        innovations.append(innovation)
    every = lax.dot_general(
        jnp.concatenate(
            [jnp.where(left_half, x, 0.0) for x in weighted] + [jnp.where(left_half, 0.0, x) for x in weighted],
            axis=0,
        ),
        jnp.concatenate(spreads + spreads + innovations + innovations, axis=0),
        (((1,), (1,)), ((), ())),
        preferred_element_type=jnp.float32,
        precision=HIGH,
    )
    lane_at = iota((members, LANES), 1)
    patch_at = lane_at // members
    gram = jnp.zeros((members, LANES), jnp.float32)
    proj = jnp.zeros((members, LANES), jnp.float32)
    for p in range(2 * pairs):
        mine = patch_at == p
        block = every[p * members : (p + 1) * members, :]
        gram = jnp.where(mine, block[:, :LANES], gram)
        proj = jnp.where(mine, block[:, LANES:], proj)

    starts = lane_at - lane_at % members
    eye = (lane_at % members == iota((members, LANES), 0)).astype(jnp.float32)
    amat = gram + (members - 1.0) * eye
    diagonal = jnp.broadcast_to(jnp.sum(amat * eye, axis=0, keepdims=True), (members, LANES))
    trace = functools.reduce(jnp.add, group_columns(diagonal, starts, members))

    def iterate(sweep, carry):
        product, inverse = carry
        columns = group_columns(product, starts, members)
        square = group_matmul(columns, product)
        cube = group_matmul(columns, square)
        return (
            2.25 * product - 1.5 * square + 0.25 * cube,
            1.5 * inverse - 0.5 * group_matmul(columns, inverse),
        )

    product, inverse = lax.fori_loop(0, NS_ITERS, iterate, (amat / trace, eye), unroll=members <= 8)
    root = inverse / jnp.sqrt(trace)
    columns = group_columns(root, starts, members)
    wbar = group_matmul(columns, group_matmul(columns, proj))
    wtot = ((members - 1.0) ** 0.5) * root + wbar
    mix = wtot - jnp.sum(wtot, axis=0, keepdims=True) * (1.0 / members) + 1.0 / members
    mix_ref[...] = mix


def mix_kernel(sizes, recv_ref, mix_ref, *refs):
    members, own_rows, pieces = sizes
    rest_refs, (out_ref, table_ref) = refs[:members], refs[members:]
    stride = recv_ref.shape[0] // members
    me = lax.axis_index("member")
    order = (iota((members, members), 0) == iota((members, members), 1) ^ me).astype(jnp.float32)
    table_ref[...] = lax.dot_general(
        mix_ref[...], order, (((0,), (0,)), ((), ())), preferred_element_type=jnp.float32, precision=HIGH
    )
    bases = [pl.multiple_of((me ^ d) * stride, 8) for d in range(members)]

    def analyse(m, carry):
        for side in range(2):
            coefs = table_ref[pl.ds(side * members + m, own_rows, stride=2 * members), :]
            columns = [jnp.broadcast_to(coefs[:, d : d + 1], (own_rows, LANES)) for d in range(members)]
            for i in range(4):
                for q in range(side * pieces // 2, (side + 1) * pieces // 2):
                    total = None
                    for d in range(members):
                        if i < PACKED:
                            start = (i * pieces + q) * own_rows
                            block = recv_ref[pl.ds(bases[d] + start, own_rows), :]
                        else:
                            start = ((i - PACKED) * pieces + q) * own_rows
                            block = rest_refs[d][start : start + own_rows, :]
                        term = columns[d] * block
                        total = term if total is None else total + term
                    out_ref[m, i, :, q * LANES : (q + 1) * LANES] = total
        return carry

    if members <= 8:
        for m in range(members):
            analyse(m, 0)
    else:
        lax.fori_loop(0, members, analyse, 0)


def trade(blocks):
    members = len(blocks)
    held = list(blocks)
    for d in reversed(range(1, members)):
        held[d] = lax.ppermute(blocks[d], "member", [(i, i ^ d) for i in range(members)])
    return held


def place_kernel(recv_ref, out_ref, sems):
    members, _, own_rows, _ = recv_ref.shape
    copies = []
    for j in range(members):
        target = out_ref.at[:, pl.ds(j * own_rows, own_rows), :]
        copies.append(pltpu.make_async_copy(recv_ref.at[j], target, sems.at[j]))
        copies[-1].start()
    for copy in copies:
        copy.wait()


def swaps(near, far):
    count = lax.axis_size("tile")

    def pairs(start):
        twos = [(i, i + 1) for i in range(start, count - 1, 2)]
        return twos + [(b, a) for a, b in twos]

    far = lax.ppermute(far, "tile", pairs(1))
    near = lax.ppermute(near, "tile", pairs(0))
    return near, far


def vmem_specs(count):
    return [pl.BlockSpec(memory_space=pltpu.VMEM)] * count


def body(
    realization_array,
    water_depth,
    wet_mask,
    obs_cell,
    obs_value,
    obs_error,
    celer_gain,
    obs_list,
    obs_count,
):
    members = lax.axis_size("member")
    rows, width = water_depth.shape
    obs_tile = obs_cell.shape[0]
    radius = obs_tile // 8
    halo = radius * CELLS_PER_OBS // width + 2 * STEPS
    per_dev, slots = obs_list.shape[1:]
    own_rows = per_dev * REGION_POINTS // width
    pieces = width // LANES
    state = realization_array[0]
    panel = (obs_tile // LANES, LANES)
    pairs = per_dev * slots // LANES
    edges = pl.pallas_call(
        functools.partial(edge_kernel, halo),
        out_shape=[jax.ShapeDtypeStruct((6 * halo + 8, width), jnp.float32)] * 2,
        in_specs=[pl.BlockSpec(memory_space=pl.ANY)] * 7,
        out_specs=[pl.BlockSpec(memory_space=pl.ANY)] * 2,
        scratch_shapes=[
            pltpu.VMEM((2, 6 * halo + 8, width), jnp.float32),
            pltpu.VMEM((2, halo, width), jnp.int32),
            pltpu.VMEM((2, 8, LANES), jnp.int32),
            pltpu.SemaphoreType.DMA((20,)),
            pltpu.SemaphoreType.DMA((14,)),
        ],
        name="edges",
    )(
        state,
        water_depth,
        wet_mask,
        obs_cell.reshape(panel),
        celer_gain.reshape(panel),
        obs_value.reshape(panel),
        obs_error.reshape(panel),
    )
    near, far = swaps(*edges)

    window = (obs_tile + 2 * radius) // LANES
    packet = PACKED * pieces * own_rows + window
    grid = (pieces, rows + 2 * halo + 2 * PAD, LANES)
    sends, *rest = pl.pallas_call(
        functools.partial(forecast_kernel, (members, own_rows, halo, radius)),
        out_shape=[
            jax.ShapeDtypeStruct((members, packet, LANES), jnp.float32),
        ]
        + [jax.ShapeDtypeStruct(((4 - PACKED) * pieces * own_rows, LANES), jnp.float32)] * members,
        in_specs=vmem_specs(7),
        out_specs=[pl.BlockSpec(memory_space=pl.ANY)] + vmem_specs(members),
        scratch_shapes=[pltpu.VMEM(grid, jnp.float32)] * 8
        + [pltpu.VMEM((window, LANES), jnp.float32)] * 2
        + [
            pltpu.VMEM((members, packet - window, LANES), jnp.float32),
            pltpu.VMEM((window, LANES), jnp.float32),
            pltpu.SemaphoreType.DMA((2 * members,)),
        ],
        compiler_params=pltpu.CompilerParams(vmem_limit_bytes=24 * 2**20),
        name="forecast",
    )(
        state,
        water_depth,
        wet_mask,
        obs_cell.reshape(panel),
        celer_gain.reshape(panel),
        near,
        far,
    )
    received = lax.all_to_all(sends, "member", split_axis=0, concat_axis=0, tiled=True)
    rest = trade(rest)
    received = received.reshape(members * packet, LANES)

    patch_index = lax.axis_index("member") * per_dev + jnp.arange(per_dev, dtype=jnp.int32)
    row_index = patch_index * REGION_POINTS // width
    centre = obs_tile + row_index * obs_tile // rows
    dist = (obs_list[0] - centre[:, None]).astype(jnp.float32) / radius
    damp = 1.0 + 4.0 * dist * dist
    live = jnp.arange(slots, dtype=jnp.int32)[None, :] < obs_count[0][:, None]
    spot = side_by_side(obs_list[0] - (obs_tile - radius), pairs)
    mix = pl.pallas_call(
        functools.partial(weight_kernel, (members, halo)),
        out_shape=jax.ShapeDtypeStruct((members, LANES), jnp.float32),
        in_specs=vmem_specs(8),
        out_specs=vmem_specs(1)[0],
        scratch_shapes=[pltpu.VMEM((window, LANES), jnp.float32)] * 2,
        compiler_params=pltpu.CompilerParams(vmem_limit_bytes=24 * 2**20),
        name="weights",
    )(
        received,
        spot,
        side_by_side(damp, pairs),
        side_by_side(live.astype(jnp.float32), pairs),
        obs_value.reshape(panel),
        obs_error.reshape(panel),
        near,
        far,
    )
    analysed = pl.pallas_call(
        functools.partial(mix_kernel, (members, own_rows, pieces)),
        out_shape=jax.ShapeDtypeStruct((members, 4, own_rows, width), jnp.float32),
        in_specs=vmem_specs(2 + members),
        out_specs=vmem_specs(1)[0],
        scratch_shapes=[pltpu.VMEM((LANES, members), jnp.float32)],
        compiler_params=pltpu.CompilerParams(vmem_limit_bytes=24 * 2**20),
        name="mix",
    )(received, mix, *rest)
    result = lax.all_to_all(analysed, "member", split_axis=0, concat_axis=0, tiled=True)
    if own_rows % 8:
        return jnp.transpose(result, (1, 0, 2, 3)).reshape(1, 4, rows, width)
    return pl.pallas_call(
        place_kernel,
        out_shape=jax.ShapeDtypeStruct((4, rows, width), jnp.float32),
        in_specs=vmem_specs(1),
        out_specs=pl.BlockSpec(memory_space=pl.ANY),
        scratch_shapes=[pltpu.SemaphoreType.DMA((members,))],
        name="place",
    )(result)[None]


def solution(mesh):
    return jax.shard_map(
        body,
        mesh=mesh,
        in_specs=(
            P("member", None, "tile", None),
            P("tile", None),
            P("tile", None),
            P("tile"),
            P("tile"),
            P("tile"),
            P("tile"),
            P("tile", "member", None),
            P("tile", "member"),
        ),
        out_specs=P("member", None, "tile", None),
        check_vma=False,
    )
```

```python
import functools

import jax
import jax.numpy as jnp
from jax import lax
from jax.experimental import pallas as pl
from jax.experimental.pallas import tpu as pltpu
from jax.sharding import PartitionSpec as P

REGION_POINTS = 256
STEPS = 4
NS_ITERS = 14
CELLS_PER_OBS = 8
LANES = 128

FRICTION = 0.98
PRESSURE = 0.25
DIVERGE = 0.25
FORCING = 0.05
UPWIND = 0.4
DAMPING = 0.02
HIGH = lax.Precision.HIGHEST

PAD = 8
PACKED = 2


def iota(shape, dim):
    return lax.broadcasted_iota(jnp.int32, shape, dim)


def edge_kernel(halo, *refs):
    grids, obs, outs = refs[:3], refs[3:7], refs[7:9]
    wet_ref, cell_ref, sems = refs[9:]
    rows = grids[1].shape[0]
    inner = obs[0].shape[0]
    even = lax.axis_index("tile") % 2 == 0
    copies = []

    def fetch(source, target):
        copies.append(pltpu.make_async_copy(source, target, sems.at[len(copies)]))
        copies[-1].start()

    for side, out in enumerate(outs):
        is_last = even if side == 0 else jnp.logical_not(even)
        start = pl.multiple_of(jnp.where(is_last, rows - halo, 0), 8)
        for i in range(6):
            source = (grids[0].at[i] if i < 4 else grids[i - 3]).at[pl.ds(start, halo), :]
            fetch(source, out.at[pl.ds(i * halo, halo), :] if i < 5 else wet_ref.at[side])
        start = pl.multiple_of(jnp.where(is_last, inner - 8, 0), 8)
        for j in range(4):
            target = out.at[pl.ds(6 * halo, 8), pl.ds(j * LANES, LANES)] if j else cell_ref.at[side]
            fetch(obs[j].at[pl.ds(start, 8), :], target)
    for copy in copies:
        copy.wait()
    for side, out in enumerate(outs):
        out[5 * halo : 6 * halo, :] = wet_ref[side].astype(jnp.float32)
        out[6 * halo : 6 * halo + 8, 0:LANES] = (cell_ref[side] % CELLS_PER_OBS).astype(jnp.float32)


def side_by_side(x, pairs):
    return jnp.concatenate([x[:pairs], x[pairs:]], axis=1)


def window_parts(win, own, near_ref, far_ref, base, j, even):
    inner = own.shape[0]
    span = (win.shape[0] - inner) // 2
    lanes = slice(j * LANES, (j + 1) * LANES)
    near, far = near_ref[base : base + 8, lanes], far_ref[base : base + 8, lanes]
    win[0:span, :] = jnp.where(even, far, near)[8 - span :, :]
    win[span : span + inner, :] = own
    win[span + inner :, :] = jnp.where(even, near, far)[:span, :]


def forecast_kernel(
    sizes,
    state_ref,
    depth_ref,
    mask_ref,
    cell_ref,
    gain_ref,
    near_ref,
    far_ref,
    *refs,
):
    members, own_rows, halo, obs_halo = sizes
    out_ref, rest_refs, scratch = refs[0], refs[1 : members + 1], refs[members + 1 :]
    s_ref, u_ref, v_ref, e_ref, h_ref, w_ref, flux_ref, part_ref, cell_win, gain_win = scratch
    even = lax.axis_index("tile") % 2 == 0
    rows, width = depth_ref.shape
    pieces = width // LANES
    total = rows + 2 * halo
    first = PAD + halo
    own = pl.ds(first, rows)
    fields = (s_ref, u_ref, v_ref, e_ref, h_ref, w_ref)
    near_at = pl.multiple_of(jnp.where(even, first + rows, PAD), 8)
    far_at = pl.multiple_of(jnp.where(even, PAD, first + rows), 8)
    edge = jnp.zeros((PAD, LANES), jnp.float32)
    for q in range(pieces):
        lanes = slice(q * LANES, (q + 1) * LANES)
        for i, field in enumerate(fields):
            field[q, pl.ds(near_at, halo), :] = near_ref[i * halo : (i + 1) * halo, lanes]
            field[q, pl.ds(far_at, halo), :] = far_ref[i * halo : (i + 1) * halo, lanes]
            if i < 4:
                field[q, own, :] = state_ref[i, :, lanes]
        h_ref[q, own, :] = depth_ref[:, lanes]
        w_ref[q, own, :] = mask_ref[:, lanes].astype(jnp.float32)
        for field in (s_ref, e_ref, flux_ref):
            field[q, 0:PAD, :] = edge
            field[q, PAD + total : PAD + total + PAD, :] = edge

    lane = iota((8, LANES), 1)
    at_first, at_last = lane == 0, lane == LANES - 1

    def across(x):
        ahead = [pltpu.roll(piece, LANES - 1, 1) for piece in x] + [0.0]
        behind = [0.0] + [pltpu.roll(piece, 1, 1) for piece in x]
        return [
            jnp.where(at_last, ahead[q + 1], ahead[q]) - jnp.where(at_first, behind[q], behind[q + 1])
            for q in range(pieces)
        ]

    for step in range(STEPS):
        for block in range(total // 8):
            r = PAD + 8 * block
            here, below, above = pl.ds(r, 8), pl.ds(r + 1, 8), pl.ds(r - 1, 8)
            s = [s_ref[q, here, :] for q in range(pieces)]
            slope = across(s)
            flux = []
            for q in range(pieces):
                w, h = w_ref[q, here, :], h_ref[q, here, :]
                u = w * (FRICTION * u_ref[q, here, :] - PRESSURE * (s_ref[q, below, :] - s_ref[q, above, :]))
                u_ref[q, here, :] = u
                flux_ref[q, here, :] = h * u
                v = w * (FRICTION * v_ref[q, here, :] - PRESSURE * slope[q])
                v_ref[q, here, :] = v
                flux.append(h * v)
            rise = across(flux)
            for q in range(pieces):
                part_ref[q, here, :] = s[q] - DIVERGE * rise[q] + FORCING * e_ref[q, here, :]
        for block in reversed(range(total // 8)):
            r = PAD + 8 * block
            here, below, above = pl.ds(r, 8), pl.ds(r + 1, 8), pl.ds(r - 1, 8)
            for q in range(pieces):
                w = w_ref[q, here, :]
                rise = flux_ref[q, below, :] - flux_ref[q, above, :]
                s_ref[q, here, :] = w * (part_ref[q, here, :] - DIVERGE * rise)
                e = e_ref[q, here, :]
                e_ref[q, here, :] = w * (e - UPWIND * (e - e_ref[q, above, :]) - DAMPING * e)

    window = cell_win.shape[0]
    base = 6 * halo
    offsets = (cell_ref[...] % CELLS_PER_OBS).astype(jnp.float32)
    window_parts(cell_win, offsets, near_ref, far_ref, base, 0, even)
    window_parts(gain_win, gain_ref[...], near_ref, far_ref, base, 1, even)
    half = width // CELLS_PER_OBS
    top = first - obs_halo // half
    column = iota((LANES, 2 * width), 1)
    cell_at = column // (2 * LANES) * LANES + column % LANES
    parity = column // LANES % 2
    spread = jnp.where(
        iota((LANES, 2 * width), 0) == parity * half + cell_at // CELLS_PER_OBS, 1.0, 0.0
    ).astype(jnp.bfloat16)
    offset = jnp.dot(cell_win[...].astype(jnp.bfloat16), spread, preferred_element_type=jnp.float32)
    level = jnp.concatenate(
        [s_ref[q, pl.ds(top + side, window, stride=2), :] for q in range(pieces) for side in range(2)], axis=1
    )
    place = (iota((window, 2 * width), 1) % CELLS_PER_OBS).astype(jnp.float32)
    rest = jnp.where(jnp.abs(offset - place) < 0.5, level, 0.0)
    equiv = jnp.zeros((window, LANES), jnp.float32)
    parts = []
    for i in range(3):
        parts.append(rest.astype(jnp.bfloat16))
        rest = rest - parts[-1].astype(jnp.float32)
    for part in reversed(parts):
        equiv = equiv + lax.dot_general(
            part, spread, (((1,), (1,)), ((), ())), preferred_element_type=jnp.float32
        )
    equiv = equiv * gain_win[...]

    me = lax.axis_index("member")
    for j in range(members):
        source = first + j * own_rows
        for i in range(PACKED):
            for q in range(pieces):
                target = (i * pieces + q) * own_rows
                out_ref[j, target : target + own_rows, :] = fields[i][q, source : source + own_rows, :]
        body_rows = PACKED * pieces * own_rows
        out_ref[j, body_rows : body_rows + window, :] = equiv
        source = pl.multiple_of(first + (me ^ j) * own_rows, min(own_rows, 8))
        for i in range(PACKED, 4):
            for q in range(pieces):
                target = ((i - PACKED) * pieces + q) * own_rows
                rest_refs[j][target : target + own_rows, :] = fields[i][q, pl.ds(source, own_rows), :]


def group_columns(left, starts, members):
    return [jnp.take_along_axis(left, starts + k, axis=1, mode="promise_in_bounds") for k in range(members)]


def group_matmul(columns, right):
    terms = [column * right[k : k + 1, :] for k, column in enumerate(columns)]
    while len(terms) > 1:
        terms = [a + b for a, b in zip(terms[::2], terms[1::2])]
    return terms[0]


def weight_kernel(
    sizes,
    recv_ref,
    spot_ref,
    damp_ref,
    live_ref,
    value_ref,
    error_ref,
    near_ref,
    far_ref,
    mix_ref,
    value_win,
    error_win,
):
    members, halo = sizes
    window = value_win.shape[0]
    stride = recv_ref.shape[0] // members
    even = lax.axis_index("tile") % 2 == 0
    window_parts(value_win, value_ref[...], near_ref, far_ref, 6 * halo, 2, even)
    window_parts(error_win, error_ref[...], near_ref, far_ref, 6 * halo, 3, even)

    spot = spot_ref[...]
    pairs = spot.shape[0]
    row, lane = spot // LANES, spot % LANES
    rows_of = [jnp.broadcast_to(row[i : i + 1, :], (members, LANES)) for i in range(pairs)]
    lanes_of = [jnp.broadcast_to(lane[i : i + 1, :], (members, LANES)) for i in range(pairs)]
    picked = [jnp.zeros((members, LANES), jnp.float32) for i in range(pairs)]
    value = jnp.zeros((pairs, LANES), jnp.float32)
    error = jnp.zeros((pairs, LANES), jnp.float32)
    for r in range(window):
        source = recv_ref[pl.ds(stride - window + r, members, stride=stride), :]
        for i in range(pairs):
            got = jnp.take_along_axis(source, lanes_of[i], axis=1, mode="promise_in_bounds")
            picked[i] = jnp.where(rows_of[i] == r, got, picked[i])
        hit = row == r
        line = jnp.broadcast_to(value_win[r : r + 1, :], spot.shape)
        value = jnp.where(hit, jnp.take_along_axis(line, lane, axis=1, mode="promise_in_bounds"), value)
        line = jnp.broadcast_to(error_win[r : r + 1, :], spot.shape)
        error = jnp.where(hit, jnp.take_along_axis(line, lane, axis=1, mode="promise_in_bounds"), error)
    precision = jnp.where(live_ref[...] > 0.0, 1.0 / (damp_ref[...] * error), 0.0)

    left_half = iota((members, LANES), 1) < LANES // 2
    weighted, spreads, innovations = [], [], []
    for i in range(pairs):
        mean = jnp.sum(picked[i], axis=0, keepdims=True) * (1.0 / members)
        spread = picked[i] - mean
        scaled = spread * precision[i : i + 1, :]
        innovation = jnp.broadcast_to(value[i : i + 1, :] - mean, (members, LANES))
        weighted.append(scaled)
        spreads.append(spread)
        innovations.append(innovation)
    every = lax.dot_general(
        jnp.concatenate(
            [jnp.where(left_half, x, 0.0) for x in weighted] + [jnp.where(left_half, 0.0, x) for x in weighted],
            axis=0,
        ),
        jnp.concatenate(spreads + spreads + innovations + innovations, axis=0),
        (((1,), (1,)), ((), ())),
        preferred_element_type=jnp.float32,
        precision=HIGH,
    )
    lane_at = iota((members, LANES), 1)
    patch_at = lane_at // members
    gram = jnp.zeros((members, LANES), jnp.float32)
    proj = jnp.zeros((members, LANES), jnp.float32)
    for p in range(2 * pairs):
        mine = patch_at == p
        block = every[p * members : (p + 1) * members, :]
        gram = jnp.where(mine, block[:, :LANES], gram)
        proj = jnp.where(mine, block[:, LANES:], proj)

    starts = lane_at - lane_at % members
    eye = (lane_at % members == iota((members, LANES), 0)).astype(jnp.float32)
    amat = gram + (members - 1.0) * eye
    diagonal = jnp.broadcast_to(jnp.sum(amat * eye, axis=0, keepdims=True), (members, LANES))
    trace = functools.reduce(jnp.add, group_columns(diagonal, starts, members))

    def iterate(sweep, carry):
        product, inverse = carry
        columns = group_columns(product, starts, members)
        square = group_matmul(columns, product)
        cube = group_matmul(columns, square)
        return (
            2.25 * product - 1.5 * square + 0.25 * cube,
            1.5 * inverse - 0.5 * group_matmul(columns, inverse),
        )

    product, inverse = lax.fori_loop(0, NS_ITERS, iterate, (amat / trace, eye), unroll=members <= 8)
    root = inverse / jnp.sqrt(trace)
    columns = group_columns(root, starts, members)
    wbar = group_matmul(columns, group_matmul(columns, proj))
    wtot = ((members - 1.0) ** 0.5) * root + wbar
    mix = wtot - jnp.sum(wtot, axis=0, keepdims=True) * (1.0 / members) + 1.0 / members
    mix_ref[...] = mix


def mix_kernel(sizes, recv_ref, mix_ref, *refs):
    members, own_rows, pieces = sizes
    rest_refs, (out_ref, table_ref) = refs[:members], refs[members:]
    stride = recv_ref.shape[0] // members
    me = lax.axis_index("member")
    order = (iota((members, members), 0) == iota((members, members), 1) ^ me).astype(jnp.float32)
    table_ref[...] = lax.dot_general(
        mix_ref[...], order, (((0,), (0,)), ((), ())), preferred_element_type=jnp.float32, precision=HIGH
    )
    bases = [pl.multiple_of((me ^ d) * stride, 8) for d in range(members)]

    def analyse(m, carry):
        for side in range(2):
            coefs = table_ref[pl.ds(side * members + m, own_rows, stride=2 * members), :]
            columns = [jnp.broadcast_to(coefs[:, d : d + 1], (own_rows, LANES)) for d in range(members)]
            for i in range(4):
                for q in range(side * pieces // 2, (side + 1) * pieces // 2):
                    total = None
                    for d in range(members):
                        if i < PACKED:
                            start = (i * pieces + q) * own_rows
                            block = recv_ref[pl.ds(bases[d] + start, own_rows), :]
                        else:
                            start = ((i - PACKED) * pieces + q) * own_rows
                            block = rest_refs[d][start : start + own_rows, :]
                        term = columns[d] * block
                        total = term if total is None else total + term
                    out_ref[m, i, :, q * LANES : (q + 1) * LANES] = total
        return carry

    if members <= 8:
        for m in range(members):
            analyse(m, 0)
    else:
        lax.fori_loop(0, members, analyse, 0)


def trade(blocks):
    members = len(blocks)
    held = list(blocks)
    for d in reversed(range(1, members)):
        held[d] = lax.ppermute(blocks[d], "member", [(i, i ^ d) for i in range(members)])
    return held


def swaps(near, far):
    count = lax.axis_size("tile")

    def pairs(start):
        twos = [(i, i + 1) for i in range(start, count - 1, 2)]
        return twos + [(b, a) for a, b in twos]

    far = lax.ppermute(far, "tile", pairs(1))
    near = lax.ppermute(near, "tile", pairs(0))
    return near, far


def vmem_specs(count):
    return [pl.BlockSpec(memory_space=pltpu.VMEM)] * count


def body(
    realization_array,
    water_depth,
    wet_mask,
    obs_cell,
    obs_value,
    obs_error,
    celer_gain,
    obs_list,
    obs_count,
):
    members = lax.axis_size("member")
    rows, width = water_depth.shape
    obs_tile = obs_cell.shape[0]
    radius = obs_tile // 8
    halo = radius * CELLS_PER_OBS // width + 2 * STEPS
    per_dev, slots = obs_list.shape[1:]
    own_rows = per_dev * REGION_POINTS // width
    pieces = width // LANES
    state = realization_array[0]
    panel = (obs_tile // LANES, LANES)
    pairs = per_dev * slots // LANES
    edges = pl.pallas_call(
        functools.partial(edge_kernel, halo),
        out_shape=[pltpu.VMEM((6 * halo + 8, width), jnp.float32)] * 2,
        in_specs=[pl.BlockSpec(memory_space=pl.ANY)] * 7,
        out_specs=vmem_specs(2),
        scratch_shapes=[
            pltpu.VMEM((2, halo, width), jnp.int32),
            pltpu.VMEM((2, 8, LANES), jnp.int32),
            pltpu.SemaphoreType.DMA((20,)),
        ],
        name="edges",
    )(
        state,
        water_depth,
        wet_mask,
        obs_cell.reshape(panel),
        celer_gain.reshape(panel),
        obs_value.reshape(panel),
        obs_error.reshape(panel),
    )
    near, far = swaps(*edges)

    window = (obs_tile + 2 * radius) // LANES
    packet = PACKED * pieces * own_rows + window
    grid = (pieces, rows + 2 * halo + 2 * PAD, LANES)
    sends, *rest = pl.pallas_call(
        functools.partial(forecast_kernel, (members, own_rows, halo, radius)),
        out_shape=[
            pltpu.VMEM((members, packet, LANES), jnp.float32),
        ]
        + [jax.ShapeDtypeStruct(((4 - PACKED) * pieces * own_rows, LANES), jnp.float32)] * members,
        in_specs=vmem_specs(7),
        out_specs=vmem_specs(1 + members),
        scratch_shapes=[pltpu.VMEM(grid, jnp.float32)] * 8 + [pltpu.VMEM((window, LANES), jnp.float32)] * 2,
        compiler_params=pltpu.CompilerParams(vmem_limit_bytes=24 * 2**20),
        name="forecast",
    )(
        state,
        water_depth,
        wet_mask,
        obs_cell.reshape(panel),
        celer_gain.reshape(panel),
        near,
        far,
    )
    received = lax.all_to_all(sends, "member", split_axis=0, concat_axis=0, tiled=True)
    rest = trade(rest)
    received = received.reshape(members * packet, LANES)

    patch_index = lax.axis_index("member") * per_dev + jnp.arange(per_dev, dtype=jnp.int32)
    row_index = patch_index * REGION_POINTS // width
    centre = obs_tile + row_index * obs_tile // rows
    dist = (obs_list[0] - centre[:, None]).astype(jnp.float32) / radius
    damp = 1.0 + 4.0 * dist * dist
    live = jnp.arange(slots, dtype=jnp.int32)[None, :] < obs_count[0][:, None]
    spot = side_by_side(obs_list[0] - (obs_tile - radius), pairs)
    mix = pl.pallas_call(
        functools.partial(weight_kernel, (members, halo)),
        out_shape=jax.ShapeDtypeStruct((members, LANES), jnp.float32),
        in_specs=vmem_specs(8),
        out_specs=vmem_specs(1)[0],
        scratch_shapes=[pltpu.VMEM((window, LANES), jnp.float32)] * 2,
        compiler_params=pltpu.CompilerParams(vmem_limit_bytes=24 * 2**20),
        name="weights",
    )(
        received,
        spot,
        side_by_side(damp, pairs),
        side_by_side(live.astype(jnp.float32), pairs),
        obs_value.reshape(panel),
        obs_error.reshape(panel),
        near,
        far,
    )
    analysed = pl.pallas_call(
        functools.partial(mix_kernel, (members, own_rows, pieces)),
        out_shape=jax.ShapeDtypeStruct((members, 4, own_rows, width), jnp.float32),
        in_specs=vmem_specs(2 + members),
        out_specs=vmem_specs(1)[0],
        scratch_shapes=[pltpu.VMEM((LANES, members), jnp.float32)],
        compiler_params=pltpu.CompilerParams(vmem_limit_bytes=24 * 2**20),
        name="mix",
    )(received, mix, *rest)
    result = lax.all_to_all(analysed, "member", split_axis=0, concat_axis=0, tiled=True)
    return jnp.transpose(result, (1, 0, 2, 3)).reshape(1, 4, rows, width)


def solution(mesh):
    return jax.shard_map(
        body,
        mesh=mesh,
        in_specs=(
            P("member", None, "tile", None),
            P("tile", None),
            P("tile", None),
            P("tile"),
            P("tile"),
            P("tile"),
            P("tile"),
            P("tile", "member", None),
            P("tile", "member"),
        ),
        out_specs=P("member", None, "tile", None),
        check_vma=False,
    )
```

```python
import functools

import jax
import jax.numpy as jnp
from jax import lax
from jax.experimental import pallas as pl
from jax.experimental.pallas import tpu as pltpu
from jax.sharding import PartitionSpec as P

REGION_POINTS = 256
STEPS = 4
NS_ITERS = 14
CELLS_PER_OBS = 8
LANES = 128

FRICTION = 0.98
PRESSURE = 0.25
DIVERGE = 0.25
FORCING = 0.05
UPWIND = 0.4
DAMPING = 0.02
HIGH = lax.Precision.HIGHEST

PAD = 8
PACKED = 2


def iota(shape, dim):
    return lax.broadcasted_iota(jnp.int32, shape, dim)


def edge_kernel(halo, *refs):
    grids, obs, outs = refs[:3], refs[3:7], refs[7:9]
    wet_ref, cell_ref, sems = refs[9:]
    rows = grids[1].shape[0]
    inner = obs[0].shape[0]
    even = lax.axis_index("tile") % 2 == 0
    copies = []

    def fetch(source, target):
        copies.append(pltpu.make_async_copy(source, target, sems.at[len(copies)]))
        copies[-1].start()

    for side, out in enumerate(outs):
        is_last = even if side == 0 else jnp.logical_not(even)
        start = pl.multiple_of(jnp.where(is_last, rows - halo, 0), 8)
        for i in range(6):
            source = (grids[0].at[i] if i < 4 else grids[i - 3]).at[pl.ds(start, halo), :]
            fetch(source, out.at[pl.ds(i * halo, halo), :] if i < 5 else wet_ref.at[side])
        start = pl.multiple_of(jnp.where(is_last, inner - 8, 0), 8)
        for j in range(4):
            target = out.at[pl.ds(6 * halo, 8), pl.ds(j * LANES, LANES)] if j else cell_ref.at[side]
            fetch(obs[j].at[pl.ds(start, 8), :], target)
    for copy in copies:
        copy.wait()
    for side, out in enumerate(outs):
        out[5 * halo : 6 * halo, :] = wet_ref[side].astype(jnp.float32)
        out[6 * halo : 6 * halo + 8, 0:LANES] = (cell_ref[side] % CELLS_PER_OBS).astype(jnp.float32)


def side_by_side(x, pairs):
    return jnp.concatenate([x[:pairs], x[pairs:]], axis=1)


def window_parts(win, own, near_ref, far_ref, base, j, even):
    inner = own.shape[0]
    span = (win.shape[0] - inner) // 2
    lanes = slice(j * LANES, (j + 1) * LANES)
    near, far = near_ref[base : base + 8, lanes], far_ref[base : base + 8, lanes]
    win[0:span, :] = jnp.where(even, far, near)[8 - span :, :]
    win[span : span + inner, :] = own
    win[span + inner :, :] = jnp.where(even, near, far)[:span, :]


def forecast_kernel(
    sizes,
    state_ref,
    depth_ref,
    mask_ref,
    cell_ref,
    gain_ref,
    near_ref,
    far_ref,
    *refs,
):
    members, own_rows, halo, obs_halo = sizes
    half = members // 2
    out_ref, equiv_ref, across_ref = refs[:3]
    along_refs, scratch = refs[3 : half + 3], refs[half + 3 :]
    s_ref, u_ref, v_ref, e_ref, h_ref, w_ref, flux_ref, part_ref, cell_win, gain_win = scratch
    even = lax.axis_index("tile") % 2 == 0
    rows, width = depth_ref.shape
    pieces = width // LANES
    total = rows + 2 * halo
    first = PAD + halo
    own = pl.ds(first, rows)
    fields = (s_ref, u_ref, v_ref, e_ref, h_ref, w_ref)
    near_at = pl.multiple_of(jnp.where(even, first + rows, PAD), 8)
    far_at = pl.multiple_of(jnp.where(even, PAD, first + rows), 8)
    edge = jnp.zeros((PAD, LANES), jnp.float32)
    for q in range(pieces):
        lanes = slice(q * LANES, (q + 1) * LANES)
        for i, field in enumerate(fields):
            field[q, pl.ds(near_at, halo), :] = near_ref[i * halo : (i + 1) * halo, lanes]
            field[q, pl.ds(far_at, halo), :] = far_ref[i * halo : (i + 1) * halo, lanes]
            if i < 4:
                field[q, own, :] = state_ref[i, :, lanes]
        h_ref[q, own, :] = depth_ref[:, lanes]
        w_ref[q, own, :] = mask_ref[:, lanes].astype(jnp.float32)
        for field in (s_ref, e_ref, flux_ref):
            field[q, 0:PAD, :] = edge
            field[q, PAD + total : PAD + total + PAD, :] = edge

    lane = iota((8, LANES), 1)
    at_first, at_last = lane == 0, lane == LANES - 1

    def across(x):
        ahead = [pltpu.roll(piece, LANES - 1, 1) for piece in x] + [0.0]
        behind = [0.0] + [pltpu.roll(piece, 1, 1) for piece in x]
        return [
            jnp.where(at_last, ahead[q + 1], ahead[q]) - jnp.where(at_first, behind[q], behind[q + 1])
            for q in range(pieces)
        ]

    for step in range(STEPS):
        for block in range(total // 8):
            r = PAD + 8 * block
            here, below, above = pl.ds(r, 8), pl.ds(r + 1, 8), pl.ds(r - 1, 8)
            s = [s_ref[q, here, :] for q in range(pieces)]
            slope = across(s)
            flux = []
            for q in range(pieces):
                w, h = w_ref[q, here, :], h_ref[q, here, :]
                u = w * (FRICTION * u_ref[q, here, :] - PRESSURE * (s_ref[q, below, :] - s_ref[q, above, :]))
                u_ref[q, here, :] = u
                flux_ref[q, here, :] = h * u
                v = w * (FRICTION * v_ref[q, here, :] - PRESSURE * slope[q])
                v_ref[q, here, :] = v
                flux.append(h * v)
            rise = across(flux)
            for q in range(pieces):
                part_ref[q, here, :] = s[q] - DIVERGE * rise[q] + FORCING * e_ref[q, here, :]
        for block in reversed(range(total // 8)):
            r = PAD + 8 * block
            here, below, above = pl.ds(r, 8), pl.ds(r + 1, 8), pl.ds(r - 1, 8)
            for q in range(pieces):
                w = w_ref[q, here, :]
                rise = flux_ref[q, below, :] - flux_ref[q, above, :]
                s_ref[q, here, :] = w * (part_ref[q, here, :] - DIVERGE * rise)
                e = e_ref[q, here, :]
                e_ref[q, here, :] = w * (e - UPWIND * (e - e_ref[q, above, :]) - DAMPING * e)

    window = cell_win.shape[0]
    base = 6 * halo
    offsets = (cell_ref[...] % CELLS_PER_OBS).astype(jnp.float32)
    window_parts(cell_win, offsets, near_ref, far_ref, base, 0, even)
    window_parts(gain_win, gain_ref[...], near_ref, far_ref, base, 1, even)
    half = width // CELLS_PER_OBS
    top = first - obs_halo // half
    column = iota((LANES, 2 * width), 1)
    cell_at = column // (2 * LANES) * LANES + column % LANES
    parity = column // LANES % 2
    spread = jnp.where(
        iota((LANES, 2 * width), 0) == parity * half + cell_at // CELLS_PER_OBS, 1.0, 0.0
    ).astype(jnp.bfloat16)
    offset = jnp.dot(cell_win[...].astype(jnp.bfloat16), spread, preferred_element_type=jnp.float32)
    level = jnp.concatenate(
        [s_ref[q, pl.ds(top + side, window, stride=2), :] for q in range(pieces) for side in range(2)], axis=1
    )
    place = (iota((window, 2 * width), 1) % CELLS_PER_OBS).astype(jnp.float32)
    rest = jnp.where(jnp.abs(offset - place) < 0.5, level, 0.0)
    equiv = jnp.zeros((window, LANES), jnp.float32)
    parts = []
    for i in range(3):
        parts.append(rest.astype(jnp.bfloat16))
        rest = rest - parts[-1].astype(jnp.float32)
    for part in reversed(parts):
        equiv = equiv + lax.dot_general(
            part, spread, (((1,), (1,)), ((), ())), preferred_element_type=jnp.float32
        )
    equiv = equiv * gain_win[...]
    equiv_ref[...] = equiv
    across_ref[across_ref.shape[0] - window :, :] = equiv

    me = lax.axis_index("member")
    for j in range(members):
        source = first + j * own_rows
        for i in range(PACKED):
            for q in range(pieces):
                target = (i * pieces + q) * own_rows
                out_ref[j, target : target + own_rows, :] = fields[i][q, source : source + own_rows, :]
        source = pl.multiple_of(first + (me ^ j) * own_rows, min(own_rows, 8))
        for i in range(PACKED, 4):
            for q in range(pieces):
                target = ((i - PACKED) * pieces + q) * own_rows
                block = fields[i][q, pl.ds(source, own_rows), :]
                if j % 2:
                    target += j // 2 * (4 - PACKED) * pieces * own_rows
                    across_ref[target : target + own_rows, :] = block
                else:
                    along_refs[j // 2][target : target + own_rows, :] = block


def group_columns(left, starts, members):
    return [jnp.take_along_axis(left, starts + k, axis=1, mode="promise_in_bounds") for k in range(members)]


def group_matmul(columns, right):
    terms = [column * right[k : k + 1, :] for k, column in enumerate(columns)]
    while len(terms) > 1:
        terms = [a + b for a, b in zip(terms[::2], terms[1::2])]
    return terms[0]


def weight_kernel(sizes, four_ref, *refs):
    members, halo = sizes
    half = members // 2
    near_refs, refs = refs[: half // 2 - 1], refs[half // 2 - 1 :]
    spot_ref, damp_ref, live_ref, value_ref, error_ref, near_ref, far_ref = refs[:7]
    mix_ref, value_win, error_win, equiv_win = refs[7:]
    window = value_win.shape[0]
    for i, ref in enumerate((four_ref, *near_refs)):
        start = ref.shape[0] - 4 * window
        for place in (2 * i, 2 * i + half, 2 * i + 1, 2 * i + half + 1):
            equiv_win[place * window : (place + 1) * window, :] = ref[start : start + window, :]
            start += window
    even = lax.axis_index("tile") % 2 == 0
    window_parts(value_win, value_ref[...], near_ref, far_ref, 6 * halo, 2, even)
    window_parts(error_win, error_ref[...], near_ref, far_ref, 6 * halo, 3, even)

    spot = spot_ref[...]
    pairs = spot.shape[0]
    row, lane = spot // LANES, spot % LANES
    rows_of = [jnp.broadcast_to(row[i : i + 1, :], (members, LANES)) for i in range(pairs)]
    lanes_of = [jnp.broadcast_to(lane[i : i + 1, :], (members, LANES)) for i in range(pairs)]
    picked = [jnp.zeros((members, LANES), jnp.float32) for i in range(pairs)]
    value = jnp.zeros((pairs, LANES), jnp.float32)
    error = jnp.zeros((pairs, LANES), jnp.float32)
    for r in range(window):
        source = equiv_win[pl.ds(r, members, stride=window), :]
        for i in range(pairs):
            got = jnp.take_along_axis(source, lanes_of[i], axis=1, mode="promise_in_bounds")
            picked[i] = jnp.where(rows_of[i] == r, got, picked[i])
        hit = row == r
        line = jnp.broadcast_to(value_win[r : r + 1, :], spot.shape)
        value = jnp.where(hit, jnp.take_along_axis(line, lane, axis=1, mode="promise_in_bounds"), value)
        line = jnp.broadcast_to(error_win[r : r + 1, :], spot.shape)
        error = jnp.where(hit, jnp.take_along_axis(line, lane, axis=1, mode="promise_in_bounds"), error)
    precision = jnp.where(live_ref[...] > 0.0, 1.0 / (damp_ref[...] * error), 0.0)

    left_half = iota((members, LANES), 1) < LANES // 2
    weighted, spreads, innovations = [], [], []
    for i in range(pairs):
        mean = jnp.sum(picked[i], axis=0, keepdims=True) * (1.0 / members)
        spread = picked[i] - mean
        scaled = spread * precision[i : i + 1, :]
        innovation = jnp.broadcast_to(value[i : i + 1, :] - mean, (members, LANES))
        weighted.append(scaled)
        spreads.append(spread)
        innovations.append(innovation)
    every = lax.dot_general(
        jnp.concatenate(
            [jnp.where(left_half, x, 0.0) for x in weighted] + [jnp.where(left_half, 0.0, x) for x in weighted],
            axis=0,
        ),
        jnp.concatenate(spreads + spreads + innovations + innovations, axis=0),
        (((1,), (1,)), ((), ())),
        preferred_element_type=jnp.float32,
        precision=HIGH,
    )
    lane_at = iota((members, LANES), 1)
    patch_at = lane_at // members
    gram = jnp.zeros((members, LANES), jnp.float32)
    proj = jnp.zeros((members, LANES), jnp.float32)
    for p in range(2 * pairs):
        mine = patch_at == p
        block = every[p * members : (p + 1) * members, :]
        gram = jnp.where(mine, block[:, :LANES], gram)
        proj = jnp.where(mine, block[:, LANES:], proj)

    starts = lane_at - lane_at % members
    eye = (lane_at % members == iota((members, LANES), 0)).astype(jnp.float32)
    amat = gram + (members - 1.0) * eye
    diagonal = jnp.broadcast_to(jnp.sum(amat * eye, axis=0, keepdims=True), (members, LANES))
    trace = functools.reduce(jnp.add, group_columns(diagonal, starts, members))

    def iterate(sweep, carry):
        product, inverse = carry
        columns = group_columns(product, starts, members)
        square = group_matmul(columns, product)
        cube = group_matmul(columns, square)
        return (
            2.25 * product - 1.5 * square + 0.25 * cube,
            1.5 * inverse - 0.5 * group_matmul(columns, inverse),
        )

    product, inverse = lax.fori_loop(0, NS_ITERS, iterate, (amat / trace, eye), unroll=members <= 8)
    root = inverse / jnp.sqrt(trace)
    columns = group_columns(root, starts, members)
    wbar = group_matmul(columns, group_matmul(columns, proj))
    wtot = ((members - 1.0) ** 0.5) * root + wbar
    mix = wtot - jnp.sum(wtot, axis=0, keepdims=True) * (1.0 / members) + 1.0 / members
    mix_ref[...] = mix


def mix_kernel(sizes, recv_ref, mix_ref, *refs):
    members, own_rows, pieces = sizes
    half = members // 2
    rest_refs, (out_ref, table_ref) = refs[: half + 1], refs[half + 1 :]
    rest_rows = (4 - PACKED) * pieces * own_rows
    stride = recv_ref.shape[0] // members
    me = lax.axis_index("member")
    table_ref[...] = mix_ref[...].T
    bases = [pl.multiple_of((me ^ d) * stride, 8) for d in range(members)]

    def analyse(m, carry):
        for side in range(2):
            coefs = table_ref[pl.ds(side * members + m, own_rows, stride=2 * members), :]
            columns = [jnp.broadcast_to(coefs[:, d : d + 1], (own_rows, LANES)) for d in range(members)]
            for i in range(4):
                for q in range(side * pieces // 2, (side + 1) * pieces // 2):
                    total = None
                    for d in range(members):
                        if i < PACKED:
                            start = (i * pieces + q) * own_rows
                            block = recv_ref[pl.ds(bases[d] + start, own_rows), :]
                        else:
                            start = ((i - PACKED) * pieces + q) * own_rows
                            if d >= 2:
                                start += d % 2 * rest_rows
                            block = rest_refs[d if d < 2 else d // 2 + 1][start : start + own_rows, :]
                        term = columns[d] * block
                        total = term if total is None else total + term
                    out_ref[me ^ m, i, :, q * LANES : (q + 1) * LANES] = total
        return carry

    if members <= 8:
        for m in range(members):
            analyse(m, 0)
    else:
        lax.fori_loop(0, members, analyse, 0)


def trade(block, distance):
    members = lax.axis_size("member")
    return lax.ppermute(block, "member", [(i, i ^ distance) for i in range(members)])


def trade_blocks(equiv, across, along):
    half = len(along)
    size = along[0].shape[0]
    passed = trade(across, 1)
    far = [trade(equiv, half + i) for i in range(2)]
    four = jnp.concatenate([equiv, far[0], passed[half * size :], far[1]], axis=0)
    pairs = []
    for i in range(1, half):
        parts = [along[i], passed[i * size : (i + 1) * size]] + ([four] if 2 * i < half else [])
        pairs.append(trade(jnp.concatenate(parts, axis=0), 2 * i))
    return four, pairs[: half // 2 - 1], [along[0], passed, *pairs]


def swaps(near, far):
    count = lax.axis_size("tile")

    def pairs(start):
        twos = [(i, i + 1) for i in range(start, count - 1, 2)]
        return twos + [(b, a) for a, b in twos]

    far = lax.ppermute(far, "tile", pairs(1))
    near = lax.ppermute(near, "tile", pairs(0))
    return near, far


def vmem_specs(count):
    return [pl.BlockSpec(memory_space=pltpu.VMEM)] * count


def body(
    realization_array,
    water_depth,
    wet_mask,
    obs_cell,
    obs_value,
    obs_error,
    celer_gain,
    obs_list,
    obs_count,
):
    members = lax.axis_size("member")
    rows, width = water_depth.shape
    obs_tile = obs_cell.shape[0]
    radius = obs_tile // 8
    halo = radius * CELLS_PER_OBS // width + 2 * STEPS
    per_dev, slots = obs_list.shape[1:]
    own_rows = per_dev * REGION_POINTS // width
    pieces = width // LANES
    state = realization_array[0]
    panel = (obs_tile // LANES, LANES)
    pairs = per_dev * slots // LANES
    edges = pl.pallas_call(
        functools.partial(edge_kernel, halo),
        out_shape=[pltpu.VMEM((6 * halo + 8, width), jnp.float32)] * 2,
        in_specs=[pl.BlockSpec(memory_space=pl.ANY)] * 7,
        out_specs=vmem_specs(2),
        scratch_shapes=[
            pltpu.VMEM((2, halo, width), jnp.int32),
            pltpu.VMEM((2, 8, LANES), jnp.int32),
            pltpu.SemaphoreType.DMA((20,)),
        ],
        name="edges",
    )(
        state,
        water_depth,
        wet_mask,
        obs_cell.reshape(panel),
        celer_gain.reshape(panel),
        obs_value.reshape(panel),
        obs_error.reshape(panel),
    )
    near, far = swaps(*edges)

    window = (obs_tile + 2 * radius) // LANES
    packet = PACKED * pieces * own_rows
    grid = (pieces, rows + 2 * halo + 2 * PAD, LANES)
    half = members // 2
    rest_rows = (4 - PACKED) * pieces * own_rows
    sends, equiv, across, *along = pl.pallas_call(
        functools.partial(forecast_kernel, (members, own_rows, halo, radius)),
        out_shape=[
            pltpu.VMEM((members, packet, LANES), jnp.float32),
            jax.ShapeDtypeStruct((window, LANES), jnp.float32),
            jax.ShapeDtypeStruct((half * rest_rows + window, LANES), jnp.float32),
        ]
        + [jax.ShapeDtypeStruct((rest_rows, LANES), jnp.float32)] * half,
        in_specs=vmem_specs(7),
        out_specs=vmem_specs(3 + half),
        scratch_shapes=[pltpu.VMEM(grid, jnp.float32)] * 8 + [pltpu.VMEM((window, LANES), jnp.float32)] * 2,
        compiler_params=pltpu.CompilerParams(vmem_limit_bytes=24 * 2**20),
        name="forecast",
    )(
        state,
        water_depth,
        wet_mask,
        obs_cell.reshape(panel),
        celer_gain.reshape(panel),
        near,
        far,
    )
    received = lax.all_to_all(sends, "member", split_axis=0, concat_axis=0, tiled=True)
    four, near_pairs, rest = trade_blocks(equiv, across, along)
    received = received.reshape(members * packet, LANES)

    patch_index = lax.axis_index("member") * per_dev + jnp.arange(per_dev, dtype=jnp.int32)
    row_index = patch_index * REGION_POINTS // width
    centre = obs_tile + row_index * obs_tile // rows
    dist = (obs_list[0] - centre[:, None]).astype(jnp.float32) / radius
    damp = 1.0 + 4.0 * dist * dist
    live = jnp.arange(slots, dtype=jnp.int32)[None, :] < obs_count[0][:, None]
    spot = side_by_side(obs_list[0] - (obs_tile - radius), pairs)
    mix = pl.pallas_call(
        functools.partial(weight_kernel, (members, halo)),
        out_shape=jax.ShapeDtypeStruct((members, LANES), jnp.float32),
        in_specs=vmem_specs(8 + len(near_pairs)),
        out_specs=vmem_specs(1)[0],
        scratch_shapes=[pltpu.VMEM((window, LANES), jnp.float32)] * 2
        + [pltpu.VMEM((members * window, LANES), jnp.float32)],
        compiler_params=pltpu.CompilerParams(vmem_limit_bytes=24 * 2**20),
        name="weights",
    )(
        four,
        *near_pairs,
        spot,
        side_by_side(damp, pairs),
        side_by_side(live.astype(jnp.float32), pairs),
        obs_value.reshape(panel),
        obs_error.reshape(panel),
        near,
        far,
    )
    analysed = pl.pallas_call(
        functools.partial(mix_kernel, (members, own_rows, pieces)),
        out_shape=jax.ShapeDtypeStruct((members, 4, own_rows, width), jnp.float32),
        in_specs=vmem_specs(3 + half),
        out_specs=vmem_specs(1)[0],
        scratch_shapes=[pltpu.VMEM((LANES, members), jnp.float32)],
        compiler_params=pltpu.CompilerParams(vmem_limit_bytes=24 * 2**20),
        name="mix",
    )(received, mix, *rest)
    result = lax.all_to_all(analysed, "member", split_axis=0, concat_axis=0, tiled=True)
    return jnp.transpose(result, (1, 0, 2, 3)).reshape(1, 4, rows, width)


def solution(mesh):
    return jax.shard_map(
        body,
        mesh=mesh,
        in_specs=(
            P("member", None, "tile", None),
            P("tile", None),
            P("tile", None),
            P("tile"),
            P("tile"),
            P("tile"),
            P("tile"),
            P("tile", "member", None),
            P("tile", "member"),
        ),
        out_specs=P("member", None, "tile", None),
        check_vma=False,
    )
```

```python
import functools

import jax
import jax.numpy as jnp
from jax import lax
from jax.experimental import pallas as pl
from jax.experimental.pallas import tpu as pltpu
from jax.sharding import PartitionSpec as P

REGION_POINTS = 256
STEPS = 4
NS_ITERS = 14
CELLS_PER_OBS = 8
LANES = 128

FRICTION = 0.98
PRESSURE = 0.25
DIVERGE = 0.25
FORCING = 0.05
UPWIND = 0.4
DAMPING = 0.02
HIGH = lax.Precision.HIGHEST

PAD = 8
PACKED = 3


def iota(shape, dim):
    return lax.broadcasted_iota(jnp.int32, shape, dim)


def edge_kernel(halo, *refs):
    grids, obs, outs = refs[:3], refs[3:7], refs[7:9]
    wet_ref, cell_ref, sems = refs[9:]
    rows = grids[1].shape[0]
    inner = obs[0].shape[0]
    even = lax.axis_index("tile") % 2 == 0
    copies = []

    def fetch(source, target):
        copies.append(pltpu.make_async_copy(source, target, sems.at[len(copies)]))
        copies[-1].start()

    for side, out in enumerate(outs):
        is_last = even if side == 0 else jnp.logical_not(even)
        start = pl.multiple_of(jnp.where(is_last, rows - halo, 0), 8)
        for i in range(6):
            source = (grids[0].at[i] if i < 4 else grids[i - 3]).at[pl.ds(start, halo), :]
            fetch(source, out.at[pl.ds(i * halo, halo), :] if i < 5 else wet_ref.at[side])
        start = pl.multiple_of(jnp.where(is_last, inner - 8, 0), 8)
        for j in range(4):
            target = out.at[pl.ds(6 * halo, 8), pl.ds(j * LANES, LANES)] if j else cell_ref.at[side]
            fetch(obs[j].at[pl.ds(start, 8), :], target)
    for copy in copies:
        copy.wait()
    for side, out in enumerate(outs):
        out[5 * halo : 6 * halo, :] = wet_ref[side].astype(jnp.float32)
        out[6 * halo : 6 * halo + 8, 0:LANES] = (cell_ref[side] % CELLS_PER_OBS).astype(jnp.float32)


def side_by_side(x, pairs):
    return jnp.concatenate([x[:pairs], x[pairs:]], axis=1)


def window_parts(win, own, near_ref, far_ref, base, j, even):
    inner = own.shape[0]
    span = (win.shape[0] - inner) // 2
    lanes = slice(j * LANES, (j + 1) * LANES)
    near, far = near_ref[base : base + 8, lanes], far_ref[base : base + 8, lanes]
    win[0:span, :] = jnp.where(even, far, near)[8 - span :, :]
    win[span : span + inner, :] = own
    win[span + inner :, :] = jnp.where(even, near, far)[:span, :]


def forecast_kernel(
    sizes,
    state_ref,
    depth_ref,
    mask_ref,
    cell_ref,
    gain_ref,
    near_ref,
    far_ref,
    *refs,
):
    members, own_rows, halo, obs_halo = sizes
    half = members // 2
    out_ref, equiv_ref, across_ref = refs[:3]
    along_refs, scratch = refs[3 : half + 3], refs[half + 3 :]
    s_ref, u_ref, v_ref, e_ref, h_ref, w_ref, flux_ref, part_ref, cell_win, gain_win = scratch
    even = lax.axis_index("tile") % 2 == 0
    rows, width = depth_ref.shape
    pieces = width // LANES
    total = rows + 2 * halo
    first = PAD + halo
    own = pl.ds(first, rows)
    fields = (s_ref, u_ref, v_ref, e_ref, h_ref, w_ref)
    near_at = pl.multiple_of(jnp.where(even, first + rows, PAD), 8)
    far_at = pl.multiple_of(jnp.where(even, PAD, first + rows), 8)
    edge = jnp.zeros((PAD, LANES), jnp.float32)
    for q in range(pieces):
        lanes = slice(q * LANES, (q + 1) * LANES)
        for i, field in enumerate(fields):
            field[q, pl.ds(near_at, halo), :] = near_ref[i * halo : (i + 1) * halo, lanes]
            field[q, pl.ds(far_at, halo), :] = far_ref[i * halo : (i + 1) * halo, lanes]
            if i < 4:
                field[q, own, :] = state_ref[i, :, lanes]
        h_ref[q, own, :] = depth_ref[:, lanes]
        w_ref[q, own, :] = mask_ref[:, lanes].astype(jnp.float32)
        for field in (s_ref, e_ref, flux_ref):
            field[q, 0:PAD, :] = edge
            field[q, PAD + total : PAD + total + PAD, :] = edge

    lane = iota((8, LANES), 1)
    at_first, at_last = lane == 0, lane == LANES - 1

    def across(x):
        ahead = [pltpu.roll(piece, LANES - 1, 1) for piece in x] + [0.0]
        behind = [0.0] + [pltpu.roll(piece, 1, 1) for piece in x]
        return [
            jnp.where(at_last, ahead[q + 1], ahead[q]) - jnp.where(at_first, behind[q], behind[q + 1])
            for q in range(pieces)
        ]

    for step in range(STEPS):
        for block in range(total // 8):
            r = PAD + 8 * block
            here, below, above = pl.ds(r, 8), pl.ds(r + 1, 8), pl.ds(r - 1, 8)
            s = [s_ref[q, here, :] for q in range(pieces)]
            slope = across(s)
            flux = []
            for q in range(pieces):
                w, h = w_ref[q, here, :], h_ref[q, here, :]
                u = w * (FRICTION * u_ref[q, here, :] - PRESSURE * (s_ref[q, below, :] - s_ref[q, above, :]))
                u_ref[q, here, :] = u
                flux_ref[q, here, :] = h * u
                v = w * (FRICTION * v_ref[q, here, :] - PRESSURE * slope[q])
                v_ref[q, here, :] = v
                flux.append(h * v)
            rise = across(flux)
            for q in range(pieces):
                part_ref[q, here, :] = s[q] - DIVERGE * rise[q] + FORCING * e_ref[q, here, :]
        for block in reversed(range(total // 8)):
            r = PAD + 8 * block
            here, below, above = pl.ds(r, 8), pl.ds(r + 1, 8), pl.ds(r - 1, 8)
            for q in range(pieces):
                w = w_ref[q, here, :]
                rise = flux_ref[q, below, :] - flux_ref[q, above, :]
                s_ref[q, here, :] = w * (part_ref[q, here, :] - DIVERGE * rise)
                e = e_ref[q, here, :]
                e_ref[q, here, :] = w * (e - UPWIND * (e - e_ref[q, above, :]) - DAMPING * e)

    window = cell_win.shape[0]
    base = 6 * halo
    offsets = (cell_ref[...] % CELLS_PER_OBS).astype(jnp.float32)
    window_parts(cell_win, offsets, near_ref, far_ref, base, 0, even)
    window_parts(gain_win, gain_ref[...], near_ref, far_ref, base, 1, even)
    half = width // CELLS_PER_OBS
    top = first - obs_halo // half
    column = iota((LANES, 2 * width), 1)
    cell_at = column // (2 * LANES) * LANES + column % LANES
    parity = column // LANES % 2
    spread = jnp.where(
        iota((LANES, 2 * width), 0) == parity * half + cell_at // CELLS_PER_OBS, 1.0, 0.0
    ).astype(jnp.bfloat16)
    offset = jnp.dot(cell_win[...].astype(jnp.bfloat16), spread, preferred_element_type=jnp.float32)
    level = jnp.concatenate(
        [s_ref[q, pl.ds(top + side, window, stride=2), :] for q in range(pieces) for side in range(2)], axis=1
    )
    place = (iota((window, 2 * width), 1) % CELLS_PER_OBS).astype(jnp.float32)
    rest = jnp.where(jnp.abs(offset - place) < 0.5, level, 0.0)
    equiv = jnp.zeros((window, LANES), jnp.float32)
    parts = []
    for i in range(3):
        parts.append(rest.astype(jnp.bfloat16))
        rest = rest - parts[-1].astype(jnp.float32)
    for part in reversed(parts):
        equiv = equiv + lax.dot_general(
            part, spread, (((1,), (1,)), ((), ())), preferred_element_type=jnp.float32
        )
    equiv_ref[...] = equiv * gain_win[...]

    me = lax.axis_index("member")
    for j in range(members):
        source = first + j * own_rows
        for i in range(PACKED):
            for q in range(pieces):
                target = (i * pieces + q) * own_rows
                out_ref[j, target : target + own_rows, :] = fields[i][q, source : source + own_rows, :]
        source = pl.multiple_of(first + (me ^ j) * own_rows, min(own_rows, 8))
        for i in range(PACKED, 4):
            for q in range(pieces):
                target = ((i - PACKED) * pieces + q) * own_rows
                block = fields[i][q, pl.ds(source, own_rows), :]
                if j % 2:
                    target += j // 2 * (4 - PACKED) * pieces * own_rows
                    across_ref[target : target + own_rows, :] = block
                else:
                    along_refs[j // 2][target : target + own_rows, :] = block


def group_columns(left, starts, members):
    return [jnp.take_along_axis(left, starts + k, axis=1, mode="promise_in_bounds") for k in range(members)]


def group_matmul(columns, right):
    terms = [column * right[k : k + 1, :] for k, column in enumerate(columns)]
    while len(terms) > 1:
        terms = [a + b for a, b in zip(terms[::2], terms[1::2])]
    return terms[0]


def weight_kernel(sizes, four_ref, *refs):
    members, halo = sizes
    half = members // 2
    near_refs, refs = refs[: half // 2 - 1], refs[half // 2 - 1 :]
    spot_ref, damp_ref, live_ref, value_ref, error_ref, near_ref, far_ref = refs[:7]
    mix_ref, value_win, error_win, equiv_win = refs[7:]
    window = value_win.shape[0]
    for i, ref in enumerate((four_ref, *near_refs)):
        start = ref.shape[0] - 4 * window
        for place in (2 * i, 2 * i + half, 2 * i + 1, 2 * i + half + 1):
            equiv_win[place * window : (place + 1) * window, :] = ref[start : start + window, :]
            start += window
    even = lax.axis_index("tile") % 2 == 0
    window_parts(value_win, value_ref[...], near_ref, far_ref, 6 * halo, 2, even)
    window_parts(error_win, error_ref[...], near_ref, far_ref, 6 * halo, 3, even)

    spot = spot_ref[...]
    pairs = spot.shape[0]
    row, lane = spot // LANES, spot % LANES
    rows_of = [jnp.broadcast_to(row[i : i + 1, :], (members, LANES)) for i in range(pairs)]
    lanes_of = [jnp.broadcast_to(lane[i : i + 1, :], (members, LANES)) for i in range(pairs)]
    picked = [jnp.zeros((members, LANES), jnp.float32) for i in range(pairs)]
    value = jnp.zeros((pairs, LANES), jnp.float32)
    error = jnp.zeros((pairs, LANES), jnp.float32)
    for r in range(window):
        source = equiv_win[pl.ds(r, members, stride=window), :]
        for i in range(pairs):
            got = jnp.take_along_axis(source, lanes_of[i], axis=1, mode="promise_in_bounds")
            picked[i] = jnp.where(rows_of[i] == r, got, picked[i])
        hit = row == r
        line = jnp.broadcast_to(value_win[r : r + 1, :], spot.shape)
        value = jnp.where(hit, jnp.take_along_axis(line, lane, axis=1, mode="promise_in_bounds"), value)
        line = jnp.broadcast_to(error_win[r : r + 1, :], spot.shape)
        error = jnp.where(hit, jnp.take_along_axis(line, lane, axis=1, mode="promise_in_bounds"), error)
    precision = jnp.where(live_ref[...] > 0.0, 1.0 / (damp_ref[...] * error), 0.0)

    left_half = iota((members, LANES), 1) < LANES // 2
    weighted, spreads, innovations = [], [], []
    for i in range(pairs):
        mean = jnp.sum(picked[i], axis=0, keepdims=True) * (1.0 / members)
        spread = picked[i] - mean
        scaled = spread * precision[i : i + 1, :]
        innovation = jnp.broadcast_to(value[i : i + 1, :] - mean, (members, LANES))
        weighted.append(scaled)
        spreads.append(spread)
        innovations.append(innovation)
    every = lax.dot_general(
        jnp.concatenate(
            [jnp.where(left_half, x, 0.0) for x in weighted] + [jnp.where(left_half, 0.0, x) for x in weighted],
            axis=0,
        ),
        jnp.concatenate(spreads + spreads + innovations + innovations, axis=0),
        (((1,), (1,)), ((), ())),
        preferred_element_type=jnp.float32,
        precision=HIGH,
    )
    lane_at = iota((members, LANES), 1)
    patch_at = lane_at // members
    gram = jnp.zeros((members, LANES), jnp.float32)
    proj = jnp.zeros((members, LANES), jnp.float32)
    for p in range(2 * pairs):
        mine = patch_at == p
        block = every[p * members : (p + 1) * members, :]
        gram = jnp.where(mine, block[:, :LANES], gram)
        proj = jnp.where(mine, block[:, LANES:], proj)

    starts = lane_at - lane_at % members
    eye = (lane_at % members == iota((members, LANES), 0)).astype(jnp.float32)
    amat = gram + (members - 1.0) * eye
    diagonal = jnp.broadcast_to(jnp.sum(amat * eye, axis=0, keepdims=True), (members, LANES))
    trace = functools.reduce(jnp.add, group_columns(diagonal, starts, members))

    def iterate(sweep, carry):
        product, inverse = carry
        columns = group_columns(product, starts, members)
        square = group_matmul(columns, product)
        cube = group_matmul(columns, square)
        return (
            2.25 * product - 1.5 * square + 0.25 * cube,
            1.5 * inverse - 0.5 * group_matmul(columns, inverse),
        )

    product, inverse = lax.fori_loop(0, NS_ITERS, iterate, (amat / trace, eye), unroll=members <= 8)
    root = inverse / jnp.sqrt(trace)
    columns = group_columns(root, starts, members)
    wbar = group_matmul(columns, group_matmul(columns, proj))
    wtot = ((members - 1.0) ** 0.5) * root + wbar
    mix = wtot - jnp.sum(wtot, axis=0, keepdims=True) * (1.0 / members) + 1.0 / members
    mix_ref[...] = mix


def mix_kernel(sizes, recv_ref, mix_ref, *refs):
    members, own_rows, pieces = sizes
    half = members // 2
    rest_refs, (out_ref, table_ref) = refs[: half + 1], refs[half + 1 :]
    rest_rows = (4 - PACKED) * pieces * own_rows
    stride = recv_ref.shape[0] // members
    me = lax.axis_index("member")
    table_ref[...] = mix_ref[...].T
    bases = [pl.multiple_of((me ^ d) * stride, 8) for d in range(members)]

    def analyse(m, carry):
        for side in range(2):
            coefs = table_ref[pl.ds(side * members + m, own_rows, stride=2 * members), :]
            columns = [jnp.broadcast_to(coefs[:, d : d + 1], (own_rows, LANES)) for d in range(members)]
            for i in range(4):
                for q in range(side * pieces // 2, (side + 1) * pieces // 2):
                    total = None
                    for d in range(members):
                        if i < PACKED:
                            start = (i * pieces + q) * own_rows
                            block = recv_ref[pl.ds(bases[d] + start, own_rows), :]
                        else:
                            start = ((i - PACKED) * pieces + q) * own_rows
                            if d >= 2:
                                start += d % 2 * rest_rows
                            block = rest_refs[d if d < 2 else d // 2 + 1][start : start + own_rows, :]
                        term = columns[d] * block
                        total = term if total is None else total + term
                    out_ref[me ^ m, i, :, q * LANES : (q + 1) * LANES] = total
        return carry

    if members <= 8:
        for m in range(members):
            analyse(m, 0)
    else:
        lax.fori_loop(0, members, analyse, 0)


def trade(block, distance):
    members = lax.axis_size("member")
    return lax.ppermute(block, "member", [(i, i ^ distance) for i in range(members)])


def trade_blocks(equiv, across, along):
    half = len(along)
    size = along[0].shape[0]
    far_equiv = trade(equiv, half)
    passed = trade(across, 1)
    two = jnp.concatenate([equiv, far_equiv], axis=0)
    four = jnp.concatenate([two, trade(two, 1)], axis=0)
    pairs = []
    for i in range(1, half):
        parts = [along[i], passed[i * size : (i + 1) * size]] + ([four] if 2 * i < half else [])
        pairs.append(trade(jnp.concatenate(parts, axis=0), 2 * i))
    return four, pairs[: half // 2 - 1], [along[0], passed, *pairs]


def swaps(near, far):
    count = lax.axis_size("tile")

    def pairs(start):
        twos = [(i, i + 1) for i in range(start, count - 1, 2)]
        return twos + [(b, a) for a, b in twos]

    far = lax.ppermute(far, "tile", pairs(1))
    near = lax.ppermute(near, "tile", pairs(0))
    return near, far


def vmem_specs(count):
    return [pl.BlockSpec(memory_space=pltpu.VMEM)] * count


def body(
    realization_array,
    water_depth,
    wet_mask,
    obs_cell,
    obs_value,
    obs_error,
    celer_gain,
    obs_list,
    obs_count,
):
    members = lax.axis_size("member")
    rows, width = water_depth.shape
    obs_tile = obs_cell.shape[0]
    radius = obs_tile // 8
    halo = radius * CELLS_PER_OBS // width + 2 * STEPS
    per_dev, slots = obs_list.shape[1:]
    own_rows = per_dev * REGION_POINTS // width
    pieces = width // LANES
    state = realization_array[0]
    panel = (obs_tile // LANES, LANES)
    pairs = per_dev * slots // LANES
    edges = pl.pallas_call(
        functools.partial(edge_kernel, halo),
        out_shape=[pltpu.VMEM((6 * halo + 8, width), jnp.float32)] * 2,
        in_specs=[pl.BlockSpec(memory_space=pl.ANY)] * 7,
        out_specs=vmem_specs(2),
        scratch_shapes=[
            pltpu.VMEM((2, halo, width), jnp.int32),
            pltpu.VMEM((2, 8, LANES), jnp.int32),
            pltpu.SemaphoreType.DMA((20,)),
        ],
        name="edges",
    )(
        state,
        water_depth,
        wet_mask,
        obs_cell.reshape(panel),
        celer_gain.reshape(panel),
        obs_value.reshape(panel),
        obs_error.reshape(panel),
    )
    near, far = swaps(*edges)

    window = (obs_tile + 2 * radius) // LANES
    packet = PACKED * pieces * own_rows
    grid = (pieces, rows + 2 * halo + 2 * PAD, LANES)
    half = members // 2
    rest_rows = (4 - PACKED) * pieces * own_rows
    sends, equiv, across, *along = pl.pallas_call(
        functools.partial(forecast_kernel, (members, own_rows, halo, radius)),
        out_shape=[
            pltpu.VMEM((members, packet, LANES), jnp.float32),
            jax.ShapeDtypeStruct((window, LANES), jnp.float32),
            jax.ShapeDtypeStruct((half * rest_rows, LANES), jnp.float32),
        ]
        + [jax.ShapeDtypeStruct((rest_rows, LANES), jnp.float32)] * half,
        in_specs=vmem_specs(7),
        out_specs=vmem_specs(3 + half),
        scratch_shapes=[pltpu.VMEM(grid, jnp.float32)] * 8 + [pltpu.VMEM((window, LANES), jnp.float32)] * 2,
        compiler_params=pltpu.CompilerParams(vmem_limit_bytes=24 * 2**20),
        name="forecast",
    )(
        state,
        water_depth,
        wet_mask,
        obs_cell.reshape(panel),
        celer_gain.reshape(panel),
        near,
        far,
    )
    received = lax.all_to_all(sends, "member", split_axis=0, concat_axis=0, tiled=True)
    four, near_pairs, rest = trade_blocks(equiv, across, along)
    received = received.reshape(members * packet, LANES)

    patch_index = lax.axis_index("member") * per_dev + jnp.arange(per_dev, dtype=jnp.int32)
    row_index = patch_index * REGION_POINTS // width
    centre = obs_tile + row_index * obs_tile // rows
    dist = (obs_list[0] - centre[:, None]).astype(jnp.float32) / radius
    damp = 1.0 + 4.0 * dist * dist
    live = jnp.arange(slots, dtype=jnp.int32)[None, :] < obs_count[0][:, None]
    spot = side_by_side(obs_list[0] - (obs_tile - radius), pairs)
    mix = pl.pallas_call(
        functools.partial(weight_kernel, (members, halo)),
        out_shape=jax.ShapeDtypeStruct((members, LANES), jnp.float32),
        in_specs=vmem_specs(8 + len(near_pairs)),
        out_specs=vmem_specs(1)[0],
        scratch_shapes=[pltpu.VMEM((window, LANES), jnp.float32)] * 2
        + [pltpu.VMEM((members * window, LANES), jnp.float32)],
        compiler_params=pltpu.CompilerParams(vmem_limit_bytes=24 * 2**20),
        name="weights",
    )(
        four,
        *near_pairs,
        spot,
        side_by_side(damp, pairs),
        side_by_side(live.astype(jnp.float32), pairs),
        obs_value.reshape(panel),
        obs_error.reshape(panel),
        near,
        far,
    )
    analysed = pl.pallas_call(
        functools.partial(mix_kernel, (members, own_rows, pieces)),
        out_shape=jax.ShapeDtypeStruct((members, 4, own_rows, width), jnp.float32),
        in_specs=vmem_specs(3 + half),
        out_specs=vmem_specs(1)[0],
        scratch_shapes=[pltpu.VMEM((LANES, members), jnp.float32)],
        compiler_params=pltpu.CompilerParams(vmem_limit_bytes=24 * 2**20),
        name="mix",
    )(received, mix, *rest)
    result = lax.all_to_all(analysed, "member", split_axis=0, concat_axis=0, tiled=True)
    return jnp.transpose(result, (1, 0, 2, 3)).reshape(1, 4, rows, width)


def solution(mesh):
    return jax.shard_map(
        body,
        mesh=mesh,
        in_specs=(
            P("member", None, "tile", None),
            P("tile", None),
            P("tile", None),
            P("tile"),
            P("tile"),
            P("tile"),
            P("tile"),
            P("tile", "member", None),
            P("tile", "member"),
        ),
        out_specs=P("member", None, "tile", None),
        check_vma=False,
    )
```

```python
import functools

import jax
import jax.numpy as jnp
from jax import lax
from jax.experimental import pallas as pl
from jax.experimental.pallas import tpu as pltpu
from jax.sharding import PartitionSpec as P

REGION_POINTS = 256
STEPS = 4
NS_ITERS = 14
CELLS_PER_OBS = 8
LANES = 128

FRICTION = 0.98
PRESSURE = 0.25
DIVERGE = 0.25
FORCING = 0.05
UPWIND = 0.4
DAMPING = 0.02
HIGH = lax.Precision.HIGHEST

PAD = 8
PACKED = 2


def iota(shape, dim):
    return lax.broadcasted_iota(jnp.int32, shape, dim)


def edge_kernel(halo, *refs):
    grids, obs, outs = refs[:3], refs[3:7], refs[7:9]
    wet_ref, cell_ref, sems = refs[9:]
    rows = grids[1].shape[0]
    inner = obs[0].shape[0]
    even = lax.axis_index("tile") % 2 == 0
    copies = []

    def fetch(source, target):
        copies.append(pltpu.make_async_copy(source, target, sems.at[len(copies)]))
        copies[-1].start()

    for side, out in enumerate(outs):
        is_last = even if side == 0 else jnp.logical_not(even)
        start = pl.multiple_of(jnp.where(is_last, rows - halo, 0), 8)
        for i in range(6):
            source = (grids[0].at[i] if i < 4 else grids[i - 3]).at[pl.ds(start, halo), :]
            fetch(source, out.at[pl.ds(i * halo, halo), :] if i < 5 else wet_ref.at[side])
        start = pl.multiple_of(jnp.where(is_last, inner - 8, 0), 8)
        for j in range(4):
            target = out.at[pl.ds(6 * halo, 8), pl.ds(j * LANES, LANES)] if j else cell_ref.at[side]
            fetch(obs[j].at[pl.ds(start, 8), :], target)
    for copy in copies:
        copy.wait()
    for side, out in enumerate(outs):
        out[5 * halo : 6 * halo, :] = wet_ref[side].astype(jnp.float32)
        out[6 * halo : 6 * halo + 8, 0:LANES] = (cell_ref[side] % CELLS_PER_OBS).astype(jnp.float32)


def side_by_side(x, pairs):
    return jnp.concatenate([x[:pairs], x[pairs:]], axis=1)


def window_parts(win, own, near_ref, far_ref, base, j, even):
    inner = own.shape[0]
    span = (win.shape[0] - inner) // 2
    lanes = slice(j * LANES, (j + 1) * LANES)
    near, far = near_ref[base : base + 8, lanes], far_ref[base : base + 8, lanes]
    win[0:span, :] = jnp.where(even, far, near)[8 - span :, :]
    win[span : span + inner, :] = own
    win[span + inner :, :] = jnp.where(even, near, far)[:span, :]


def forecast_kernel(
    sizes,
    state_ref,
    depth_ref,
    mask_ref,
    cell_ref,
    gain_ref,
    near_ref,
    far_ref,
    *refs,
):
    members, own_rows, halo, obs_halo = sizes
    half = members // 2
    out_ref, equiv_ref, across_ref = refs[:3]
    along_refs, scratch = refs[3 : half + 3], refs[half + 3 :]
    s_ref, u_ref, v_ref, e_ref, h_ref, w_ref, flux_ref, part_ref, cell_win, gain_win = scratch
    even = lax.axis_index("tile") % 2 == 0
    rows, width = depth_ref.shape
    pieces = width // LANES
    total = rows + 2 * halo
    first = PAD + halo
    own = pl.ds(first, rows)
    fields = (s_ref, u_ref, v_ref, e_ref, h_ref, w_ref)
    near_at = pl.multiple_of(jnp.where(even, first + rows, PAD), 8)
    far_at = pl.multiple_of(jnp.where(even, PAD, first + rows), 8)
    edge = jnp.zeros((PAD, LANES), jnp.float32)
    for q in range(pieces):
        lanes = slice(q * LANES, (q + 1) * LANES)
        for i, field in enumerate(fields):
            field[q, pl.ds(near_at, halo), :] = near_ref[i * halo : (i + 1) * halo, lanes]
            field[q, pl.ds(far_at, halo), :] = far_ref[i * halo : (i + 1) * halo, lanes]
            if i < 4:
                field[q, own, :] = state_ref[i, :, lanes]
        h_ref[q, own, :] = depth_ref[:, lanes]
        s_ref[q, PAD : PAD + total, :] *= PRESSURE
        h_ref[q, PAD : PAD + total, :] *= PRESSURE * DIVERGE
        w_ref[q, own, :] = mask_ref[:, lanes].astype(jnp.float32)
        for field in (s_ref, e_ref, flux_ref):
            field[q, 0:PAD, :] = edge
            field[q, PAD + total : PAD + total + PAD, :] = edge

    lane = iota((8, LANES), 1)
    at_first, at_last = lane == 0, lane == LANES - 1

    def across(x):
        ahead = [pltpu.roll(piece, LANES - 1, 1) for piece in x] + [0.0]
        behind = [0.0] + [pltpu.roll(piece, 1, 1) for piece in x]
        return [
            jnp.where(at_last, ahead[q + 1], ahead[q]) - jnp.where(at_first, behind[q], behind[q + 1])
            for q in range(pieces)
        ]

    outer = (halo - obs_halo * CELLS_PER_OBS // width) // 8
    for step in range(STEPS):
        skip, skip_energy = (outer, halo // 8) if step == STEPS - 1 else (0, 0)
        for block in range(total // 8):
            r = PAD + 8 * block
            here, below, above = pl.ds(r, 8), pl.ds(r + 1, 8), pl.ds(r - 1, 8)
            inside = skip <= block < total // 8 - skip
            s = [s_ref[q, here, :] for q in range(pieces)]
            slope = across(s) if inside else None
            flux = []
            for q in range(pieces):
                w, h = w_ref[q, here, :], h_ref[q, here, :]
                u = w * (FRICTION * u_ref[q, here, :] - (s_ref[q, below, :] - s_ref[q, above, :]))
                u_ref[q, here, :] = u
                flux_ref[q, here, :] = h * u
                if inside:
                    v = w * (FRICTION * v_ref[q, here, :] - slope[q])
                    v_ref[q, here, :] = v
                    flux.append(h * v)
            if inside:
                rise = across(flux)
                for q in range(pieces):
                    part_ref[q, here, :] = s[q] - rise[q] + (PRESSURE * FORCING) * e_ref[q, here, :]
        for block in reversed(range(skip, total // 8 - skip)):
            r = PAD + 8 * block
            here, below, above = pl.ds(r, 8), pl.ds(r + 1, 8), pl.ds(r - 1, 8)
            for q in range(pieces):
                w = w_ref[q, here, :]
                rise = flux_ref[q, below, :] - flux_ref[q, above, :]
                s_ref[q, here, :] = w * (part_ref[q, here, :] - rise)
                if skip_energy <= block < total // 8 - skip_energy:
                    e = e_ref[q, here, :]
                    e_ref[q, here, :] = w * ((1.0 - UPWIND - DAMPING) * e + UPWIND * e_ref[q, above, :])

    window = cell_win.shape[0]
    base = 6 * halo
    offsets = (cell_ref[...] % CELLS_PER_OBS).astype(jnp.float32)
    window_parts(cell_win, offsets, near_ref, far_ref, base, 0, even)
    window_parts(gain_win, gain_ref[...], near_ref, far_ref, base, 1, even)
    half = width // CELLS_PER_OBS
    top = first - obs_halo // half
    column = iota((LANES, 2 * width), 1)
    cell_at = column // (2 * LANES) * LANES + column % LANES
    parity = column // LANES % 2
    spread = jnp.where(
        iota((LANES, 2 * width), 0) == parity * half + cell_at // CELLS_PER_OBS, 1.0, 0.0
    ).astype(jnp.bfloat16)
    offset = jnp.dot(cell_win[...].astype(jnp.bfloat16), spread, preferred_element_type=jnp.float32)
    level = jnp.concatenate(
        [s_ref[q, pl.ds(top + side, window, stride=2), :] for q in range(pieces) for side in range(2)], axis=1
    )
    place = (iota((window, 2 * width), 1) % CELLS_PER_OBS).astype(jnp.float32)
    rest = jnp.where(jnp.abs(offset - place) < 0.5, level, 0.0)
    equiv = jnp.zeros((window, LANES), jnp.float32)
    parts = []
    for i in range(3):
        parts.append(rest.astype(jnp.bfloat16))
        rest = rest - parts[-1].astype(jnp.float32)
    for part in reversed(parts):
        equiv = equiv + lax.dot_general(
            part, spread, (((1,), (1,)), ((), ())), preferred_element_type=jnp.float32
        )
    equiv = equiv * ((1.0 / PRESSURE) * gain_win[...])
    equiv_ref[...] = equiv
    across_ref[across_ref.shape[0] - window :, :] = equiv

    me = lax.axis_index("member")
    for j in range(members):
        source = first + j * own_rows
        for i in range(PACKED):
            for q in range(pieces):
                target = (i * pieces + q) * own_rows
                block = fields[i][q, source : source + own_rows, :]
                out_ref[j, target : target + own_rows, :] = block if i else block * (1.0 / PRESSURE)
        source = pl.multiple_of(first + (me ^ j) * own_rows, min(own_rows, 8))
        for i in range(PACKED, 4):
            for q in range(pieces):
                target = ((i - PACKED) * pieces + q) * own_rows
                block = fields[i][q, pl.ds(source, own_rows), :]
                if j % 2:
                    target += j // 2 * (4 - PACKED) * pieces * own_rows
                    across_ref[target : target + own_rows, :] = block
                else:
                    along_refs[j // 2][target : target + own_rows, :] = block


def group_columns(left, starts, members):
    return [jnp.take_along_axis(left, starts + k, axis=1, mode="promise_in_bounds") for k in range(members)]


def group_matmul(columns, right):
    terms = [column * right[k : k + 1, :] for k, column in enumerate(columns)]
    while len(terms) > 1:
        terms = [a + b for a, b in zip(terms[::2], terms[1::2])]
    return terms[0]


def weight_kernel(sizes, three_ref, last_ref, *refs):
    members, halo = sizes
    half = members // 2
    near_refs, refs = refs[: half // 2 - 1], refs[half // 2 - 1 :]
    spot_ref, damp_ref, live_ref, value_ref, error_ref, near_ref, far_ref = refs[:7]
    mix_ref, value_win, error_win, equiv_win = refs[7:]
    window = value_win.shape[0]
    for i, ref in enumerate((three_ref, *near_refs)):
        start = ref.shape[0] - 3 * window
        for place in (2 * i, 2 * i + 1, 2 * i + half):
            equiv_win[place * window : (place + 1) * window, :] = ref[start : start + window, :]
            start += window
        place = 2 * i + half + 1
        equiv_win[place * window : (place + 1) * window, :] = last_ref[i * window : (i + 1) * window, :]
    even = lax.axis_index("tile") % 2 == 0
    window_parts(value_win, value_ref[...], near_ref, far_ref, 6 * halo, 2, even)
    window_parts(error_win, error_ref[...], near_ref, far_ref, 6 * halo, 3, even)

    spot = spot_ref[...]
    pairs = spot.shape[0]
    row, lane = spot // LANES, spot % LANES
    rows_of = [jnp.broadcast_to(row[i : i + 1, :], (members, LANES)) for i in range(pairs)]
    lanes_of = [jnp.broadcast_to(lane[i : i + 1, :], (members, LANES)) for i in range(pairs)]
    picked = [jnp.zeros((members, LANES), jnp.float32) for i in range(pairs)]
    value = jnp.zeros((pairs, LANES), jnp.float32)
    error = jnp.zeros((pairs, LANES), jnp.float32)
    for r in range(window):
        source = equiv_win[pl.ds(r, members, stride=window), :]
        for i in range(pairs):
            got = jnp.take_along_axis(source, lanes_of[i], axis=1, mode="promise_in_bounds")
            picked[i] = jnp.where(rows_of[i] == r, got, picked[i])
        hit = row == r
        line = jnp.broadcast_to(value_win[r : r + 1, :], spot.shape)
        value = jnp.where(hit, jnp.take_along_axis(line, lane, axis=1, mode="promise_in_bounds"), value)
        line = jnp.broadcast_to(error_win[r : r + 1, :], spot.shape)
        error = jnp.where(hit, jnp.take_along_axis(line, lane, axis=1, mode="promise_in_bounds"), error)
    precision = jnp.where(live_ref[...] > 0.0, 1.0 / (damp_ref[...] * error), 0.0)

    left_half = iota((members, LANES), 1) < LANES // 2
    weighted, spreads, innovations = [], [], []
    for i in range(pairs):
        mean = jnp.sum(picked[i], axis=0, keepdims=True) * (1.0 / members)
        spread = picked[i] - mean
        scaled = spread * precision[i : i + 1, :]
        innovation = jnp.broadcast_to(value[i : i + 1, :] - mean, (members, LANES))
        weighted.append(scaled)
        spreads.append(spread)
        innovations.append(innovation)
    every = lax.dot_general(
        jnp.concatenate(
            [jnp.where(left_half, x, 0.0) for x in weighted] + [jnp.where(left_half, 0.0, x) for x in weighted],
            axis=0,
        ),
        jnp.concatenate(spreads + spreads + innovations + innovations, axis=0),
        (((1,), (1,)), ((), ())),
        preferred_element_type=jnp.float32,
        precision=HIGH,
    )
    lane_at = iota((members, LANES), 1)
    patch_at = lane_at // members
    gram = jnp.zeros((members, LANES), jnp.float32)
    proj = jnp.zeros((members, LANES), jnp.float32)
    for p in range(2 * pairs):
        mine = patch_at == p
        block = every[p * members : (p + 1) * members, :]
        gram = jnp.where(mine, block[:, :LANES], gram)
        proj = jnp.where(mine, block[:, LANES:], proj)

    starts = lane_at - lane_at % members
    eye = (lane_at % members == iota((members, LANES), 0)).astype(jnp.float32)
    amat = gram + (members - 1.0) * eye
    diagonal = jnp.broadcast_to(jnp.sum(amat * eye, axis=0, keepdims=True), (members, LANES))
    trace = functools.reduce(jnp.add, group_columns(diagonal, starts, members))

    def iterate(sweep, carry):
        product, inverse = carry
        columns = group_columns(product, starts, members)
        square = group_matmul(columns, product)
        cube = group_matmul(columns, square)
        return (
            2.25 * product - 1.5 * square + 0.25 * cube,
            1.5 * inverse - 0.5 * group_matmul(columns, inverse),
        )

    product, inverse = lax.fori_loop(0, NS_ITERS, iterate, (amat / trace, eye), unroll=members <= 8)
    root = inverse / jnp.sqrt(trace)
    columns = group_columns(root, starts, members)
    wbar = group_matmul(columns, group_matmul(columns, proj))
    wtot = ((members - 1.0) ** 0.5) * root + wbar
    mix = wtot - jnp.sum(wtot, axis=0, keepdims=True) * (1.0 / members) + 1.0 / members
    mix_ref[...] = mix


def mix_kernel(sizes, recv_ref, mix_ref, *refs):
    members, own_rows, pieces = sizes
    half = members // 2
    rest_refs, (out_ref, table_ref) = refs[: half + 1], refs[half + 1 :]
    rest_rows = (4 - PACKED) * pieces * own_rows
    stride = recv_ref.shape[0] // members
    me = lax.axis_index("member")
    table_ref[...] = mix_ref[...].T
    bases = [pl.multiple_of((me ^ d) * stride, 8) for d in range(members)]

    def analyse(m, carry):
        for side in range(2):
            coefs = table_ref[pl.ds(side * members + m, own_rows, stride=2 * members), :]
            columns = [jnp.broadcast_to(coefs[:, d : d + 1], (own_rows, LANES)) for d in range(members)]
            for i in range(4):
                for q in range(side * pieces // 2, (side + 1) * pieces // 2):
                    total = None
                    for d in range(members):
                        if i < PACKED:
                            start = (i * pieces + q) * own_rows
                            block = recv_ref[pl.ds(bases[d] + start, own_rows), :]
                        else:
                            start = ((i - PACKED) * pieces + q) * own_rows
                            if d >= 2:
                                start += d % 2 * rest_rows
                            block = rest_refs[d if d < 2 else d // 2 + 1][start : start + own_rows, :]
                        term = columns[d] * block
                        total = term if total is None else total + term
                    out_ref[me ^ m, i, :, q * LANES : (q + 1) * LANES] = total
        return carry

    if members <= 8:
        for m in range(members):
            analyse(m, 0)
    else:
        lax.fori_loop(0, members, analyse, 0)


def trade(block, distance):
    members = lax.axis_size("member")
    return lax.ppermute(block, "member", [(i, i ^ distance) for i in range(members)])


def trade_blocks(equiv, across, along):
    half = len(along)
    size = along[0].shape[0]
    window = equiv.shape[0]
    passed = trade(across, 1)
    far = trade(equiv, half)
    three = jnp.concatenate([equiv, passed[half * size :], far], axis=0)
    pairs = []
    for i in range(1, half):
        parts = [along[i], passed[i * size : (i + 1) * size]] + ([three] if 2 * i < half else [])
        pairs.append(trade(jnp.concatenate(parts, axis=0), 2 * i))
    near = pairs[: half // 2 - 1]
    last = trade(jnp.concatenate([far] + [x[x.shape[0] - window :] for x in near], axis=0), 1)
    return three, last, near, [along[0], passed, *pairs]


def swaps(near, far):
    count = lax.axis_size("tile")

    def pairs(start):
        twos = [(i, i + 1) for i in range(start, count - 1, 2)]
        return twos + [(b, a) for a, b in twos]

    far = lax.ppermute(far, "tile", pairs(1))
    near = lax.ppermute(near, "tile", pairs(0))
    return near, far


def vmem_specs(count):
    return [pl.BlockSpec(memory_space=pltpu.VMEM)] * count


def body(
    realization_array,
    water_depth,
    wet_mask,
    obs_cell,
    obs_value,
    obs_error,
    celer_gain,
    obs_list,
    obs_count,
):
    members = lax.axis_size("member")
    rows, width = water_depth.shape
    obs_tile = obs_cell.shape[0]
    radius = obs_tile // 8
    halo = radius * CELLS_PER_OBS // width + 2 * STEPS
    per_dev, slots = obs_list.shape[1:]
    own_rows = per_dev * REGION_POINTS // width
    pieces = width // LANES
    state = realization_array[0]
    panel = (obs_tile // LANES, LANES)
    pairs = per_dev * slots // LANES
    edges = pl.pallas_call(
        functools.partial(edge_kernel, halo),
        out_shape=[pltpu.VMEM((6 * halo + 8, width), jnp.float32)] * 2,
        in_specs=[pl.BlockSpec(memory_space=pl.ANY)] * 7,
        out_specs=vmem_specs(2),
        scratch_shapes=[
            pltpu.VMEM((2, halo, width), jnp.int32),
            pltpu.VMEM((2, 8, LANES), jnp.int32),
            pltpu.SemaphoreType.DMA((20,)),
        ],
        name="edges",
    )(
        state,
        water_depth,
        wet_mask,
        obs_cell.reshape(panel),
        celer_gain.reshape(panel),
        obs_value.reshape(panel),
        obs_error.reshape(panel),
    )
    near, far = swaps(*edges)

    window = (obs_tile + 2 * radius) // LANES
    packet = PACKED * pieces * own_rows
    grid = (pieces, rows + 2 * halo + 2 * PAD, LANES)
    half = members // 2
    rest_rows = (4 - PACKED) * pieces * own_rows
    sends, equiv, across, *along = pl.pallas_call(
        functools.partial(forecast_kernel, (members, own_rows, halo, radius)),
        out_shape=[
            pltpu.VMEM((members, packet, LANES), jnp.float32),
            jax.ShapeDtypeStruct((window, LANES), jnp.float32),
            jax.ShapeDtypeStruct((half * rest_rows + window, LANES), jnp.float32),
        ]
        + [jax.ShapeDtypeStruct((rest_rows, LANES), jnp.float32)] * half,
        in_specs=vmem_specs(7),
        out_specs=vmem_specs(3 + half),
        scratch_shapes=[pltpu.VMEM(grid, jnp.float32)] * 8 + [pltpu.VMEM((window, LANES), jnp.float32)] * 2,
        compiler_params=pltpu.CompilerParams(vmem_limit_bytes=24 * 2**20),
        name="forecast",
    )(
        state,
        water_depth,
        wet_mask,
        obs_cell.reshape(panel),
        celer_gain.reshape(panel),
        near,
        far,
    )
    received = lax.all_to_all(sends, "member", split_axis=0, concat_axis=0, tiled=True)
    three, last, near_pairs, rest = trade_blocks(equiv, across, along)
    received = received.reshape(members * packet, LANES)

    patch_index = lax.axis_index("member") * per_dev + jnp.arange(per_dev, dtype=jnp.int32)
    row_index = patch_index * REGION_POINTS // width
    centre = obs_tile + row_index * obs_tile // rows
    dist = (obs_list[0] - centre[:, None]).astype(jnp.float32) / radius
    damp = 1.0 + 4.0 * dist * dist
    live = jnp.arange(slots, dtype=jnp.int32)[None, :] < obs_count[0][:, None]
    spot = side_by_side(obs_list[0] - (obs_tile - radius), pairs)
    mix = pl.pallas_call(
        functools.partial(weight_kernel, (members, halo)),
        out_shape=jax.ShapeDtypeStruct((members, LANES), jnp.float32),
        in_specs=vmem_specs(9 + len(near_pairs)),
        out_specs=vmem_specs(1)[0],
        scratch_shapes=[pltpu.VMEM((window, LANES), jnp.float32)] * 2
        + [pltpu.VMEM((members * window, LANES), jnp.float32)],
        compiler_params=pltpu.CompilerParams(vmem_limit_bytes=24 * 2**20),
        name="weights",
    )(
        three,
        last,
        *near_pairs,
        spot,
        side_by_side(damp, pairs),
        side_by_side(live.astype(jnp.float32), pairs),
        obs_value.reshape(panel),
        obs_error.reshape(panel),
        near,
        far,
    )
    analysed = pl.pallas_call(
        functools.partial(mix_kernel, (members, own_rows, pieces)),
        out_shape=jax.ShapeDtypeStruct((members, 4, own_rows, width), jnp.float32),
        in_specs=vmem_specs(3 + half),
        out_specs=vmem_specs(1)[0],
        scratch_shapes=[pltpu.VMEM((LANES, members), jnp.float32)],
        compiler_params=pltpu.CompilerParams(vmem_limit_bytes=24 * 2**20),
        name="mix",
    )(received, mix, *rest)
    result = lax.all_to_all(analysed, "member", split_axis=0, concat_axis=0, tiled=True)
    return jnp.transpose(result, (1, 0, 2, 3)).reshape(1, 4, rows, width)


def solution(mesh):
    return jax.shard_map(
        body,
        mesh=mesh,
        in_specs=(
            P("member", None, "tile", None),
            P("tile", None),
            P("tile", None),
            P("tile"),
            P("tile"),
            P("tile"),
            P("tile"),
            P("tile", "member", None),
            P("tile", "member"),
        ),
        out_specs=P("member", None, "tile", None),
        check_vma=False,
    )
```

```python
import functools

import jax
import jax.numpy as jnp
from jax import lax
from jax.experimental import pallas as pl
from jax.experimental.pallas import tpu as pltpu
from jax.sharding import PartitionSpec as P

REGION_POINTS = 256
STEPS = 4
NS_ITERS = 14
CELLS_PER_OBS = 8
LANES = 128

FRICTION = 0.98
PRESSURE = 0.25
DIVERGE = 0.25
FORCING = 0.05
UPWIND = 0.4
DAMPING = 0.02
HIGH = lax.Precision.HIGHEST

PAD = 8
PACKED = 2


def iota(shape, dim):
    return lax.broadcasted_iota(jnp.int32, shape, dim)


def edge_kernel(halo, *refs):
    grids, obs, outs = refs[:3], refs[3:7], refs[7:9]
    wet_ref, cell_ref, sems = refs[9:]
    rows = grids[1].shape[0]
    inner = obs[0].shape[0]
    even = lax.axis_index("tile") % 2 == 0
    copies = []

    def fetch(source, target):
        copies.append(pltpu.make_async_copy(source, target, sems.at[len(copies)]))
        copies[-1].start()

    for side, out in enumerate(outs):
        is_last = even if side == 0 else jnp.logical_not(even)
        start = pl.multiple_of(jnp.where(is_last, rows - halo, 0), 8)
        for i in range(6):
            source = (grids[0].at[i] if i < 4 else grids[i - 3]).at[pl.ds(start, halo), :]
            fetch(source, out.at[pl.ds(i * halo, halo), :] if i < 5 else wet_ref.at[side])
        start = pl.multiple_of(jnp.where(is_last, inner - 8, 0), 8)
        for j in range(4):
            target = out.at[pl.ds(6 * halo, 8), pl.ds(j * LANES, LANES)] if j else cell_ref.at[side]
            fetch(obs[j].at[pl.ds(start, 8), :], target)
    for copy in copies:
        copy.wait()
    for side, out in enumerate(outs):
        out[5 * halo : 6 * halo, :] = wet_ref[side].astype(jnp.float32)
        out[6 * halo : 6 * halo + 8, 0:LANES] = (cell_ref[side] % CELLS_PER_OBS).astype(jnp.float32)


def side_by_side(x, pairs):
    return jnp.concatenate([x[:pairs], x[pairs:]], axis=1)


def window_parts(win, own, near_ref, far_ref, base, j, even):
    inner = own.shape[0]
    span = (win.shape[0] - inner) // 2
    lanes = slice(j * LANES, (j + 1) * LANES)
    near, far = near_ref[base : base + 8, lanes], far_ref[base : base + 8, lanes]
    win[0:span, :] = jnp.where(even, far, near)[8 - span :, :]
    win[span : span + inner, :] = own
    win[span + inner :, :] = jnp.where(even, near, far)[:span, :]


def forecast_kernel(
    sizes,
    state_ref,
    depth_ref,
    mask_ref,
    cell_ref,
    gain_ref,
    near_ref,
    far_ref,
    *refs,
):
    members, own_rows, halo, obs_halo = sizes
    half = members // 2
    out_ref, equiv_ref, across_ref = refs[:3]
    along_refs, scratch = refs[3 : half + 3], refs[half + 3 :]
    s_ref, u_ref, v_ref, e_ref, h_ref, w_ref, flux_ref, part_ref, cell_win, gain_win = scratch
    even = lax.axis_index("tile") % 2 == 0
    rows, width = depth_ref.shape
    pieces = width // LANES
    total = rows + 2 * halo
    first = PAD + halo
    own = pl.ds(first, rows)
    fields = (s_ref, u_ref, v_ref, e_ref, h_ref, w_ref)
    near_at = pl.multiple_of(jnp.where(even, first + rows, PAD), 8)
    far_at = pl.multiple_of(jnp.where(even, PAD, first + rows), 8)
    edge = jnp.zeros((PAD, LANES), jnp.float32)
    for q in range(pieces):
        lanes = slice(q * LANES, (q + 1) * LANES)
        for i, field in enumerate(fields):
            field[q, pl.ds(near_at, halo), :] = near_ref[i * halo : (i + 1) * halo, lanes]
            field[q, pl.ds(far_at, halo), :] = far_ref[i * halo : (i + 1) * halo, lanes]
            if i < 4:
                field[q, own, :] = state_ref[i, :, lanes]
        h_ref[q, own, :] = depth_ref[:, lanes]
        s_ref[q, PAD : PAD + total, :] *= PRESSURE
        h_ref[q, PAD : PAD + total, :] *= PRESSURE * DIVERGE
        w_ref[q, own, :] = mask_ref[:, lanes].astype(jnp.float32)
        for field in (s_ref, e_ref, flux_ref):
            field[q, 0:PAD, :] = edge
            field[q, PAD + total : PAD + total + PAD, :] = edge

    lane = iota((8, LANES), 1)
    at_first, at_last = lane == 0, lane == LANES - 1

    def across(x):
        ahead = [pltpu.roll(piece, LANES - 1, 1) for piece in x] + [0.0]
        behind = [0.0] + [pltpu.roll(piece, 1, 1) for piece in x]
        return [
            jnp.where(at_last, ahead[q + 1], ahead[q]) - jnp.where(at_first, behind[q], behind[q + 1])
            for q in range(pieces)
        ]

    outer = (halo - obs_halo * CELLS_PER_OBS // width) // 8
    for step in range(STEPS):
        skip, skip_energy = (outer, halo // 8) if step == STEPS - 1 else (0, 0)
        for block in range(total // 8):
            r = PAD + 8 * block
            here, below, above = pl.ds(r, 8), pl.ds(r + 1, 8), pl.ds(r - 1, 8)
            inside = skip <= block < total // 8 - skip
            s = [s_ref[q, here, :] for q in range(pieces)]
            slope = across(s) if inside else None
            flux = []
            for q in range(pieces):
                w, h = w_ref[q, here, :], h_ref[q, here, :]
                u = w * (FRICTION * u_ref[q, here, :] - (s_ref[q, below, :] - s_ref[q, above, :]))
                u_ref[q, here, :] = u
                flux_ref[q, here, :] = h * u
                if inside:
                    v = w * (FRICTION * v_ref[q, here, :] - slope[q])
                    v_ref[q, here, :] = v
                    flux.append(h * v)
            if inside:
                rise = across(flux)
                for q in range(pieces):
                    part_ref[q, here, :] = s[q] - rise[q] + (PRESSURE * FORCING) * e_ref[q, here, :]
        for block in reversed(range(skip, total // 8 - skip)):
            r = PAD + 8 * block
            here, below, above = pl.ds(r, 8), pl.ds(r + 1, 8), pl.ds(r - 1, 8)
            for q in range(pieces):
                w = w_ref[q, here, :]
                rise = flux_ref[q, below, :] - flux_ref[q, above, :]
                s_ref[q, here, :] = w * (part_ref[q, here, :] - rise)
                if skip_energy <= block < total // 8 - skip_energy:
                    e = e_ref[q, here, :]
                    e_ref[q, here, :] = w * ((1.0 - UPWIND - DAMPING) * e + UPWIND * e_ref[q, above, :])

    window = cell_win.shape[0]
    base = 6 * halo
    offsets = (cell_ref[...] % CELLS_PER_OBS).astype(jnp.float32)
    window_parts(cell_win, offsets, near_ref, far_ref, base, 0, even)
    window_parts(gain_win, gain_ref[...], near_ref, far_ref, base, 1, even)
    half = width // CELLS_PER_OBS
    top = first - obs_halo // half
    column = iota((LANES, 2 * width), 1)
    cell_at = column // (2 * LANES) * LANES + column % LANES
    parity = column // LANES % 2
    spread = jnp.where(
        iota((LANES, 2 * width), 0) == parity * half + cell_at // CELLS_PER_OBS, 1.0, 0.0
    ).astype(jnp.bfloat16)
    offset = jnp.dot(cell_win[...].astype(jnp.bfloat16), spread, preferred_element_type=jnp.float32)
    level = jnp.concatenate(
        [s_ref[q, pl.ds(top + side, window, stride=2), :] for q in range(pieces) for side in range(2)], axis=1
    )
    place = (iota((window, 2 * width), 1) % CELLS_PER_OBS).astype(jnp.float32)
    rest = jnp.where(jnp.abs(offset - place) < 0.5, level, 0.0)
    equiv = jnp.zeros((window, LANES), jnp.float32)
    parts = []
    for i in range(3):
        parts.append(rest.astype(jnp.bfloat16))
        rest = rest - parts[-1].astype(jnp.float32)
    for part in reversed(parts):
        equiv = equiv + lax.dot_general(
            part, spread, (((1,), (1,)), ((), ())), preferred_element_type=jnp.float32
        )
    equiv = equiv * ((1.0 / PRESSURE) * gain_win[...])
    equiv_ref[...] = equiv
    across_ref[across_ref.shape[0] - window :, :] = equiv

    me = lax.axis_index("member")
    for j in range(members):
        source = first + j * own_rows
        for i in range(PACKED):
            for q in range(pieces):
                target = (i * pieces + q) * own_rows
                block = fields[i][q, source : source + own_rows, :]
                out_ref[j, target : target + own_rows, :] = block if i else block * (1.0 / PRESSURE)
        source = pl.multiple_of(first + (me ^ j) * own_rows, min(own_rows, 8))
        for i in range(PACKED, 4):
            for q in range(pieces):
                target = ((i - PACKED) * pieces + q) * own_rows
                block = fields[i][q, pl.ds(source, own_rows), :]
                if j % 2:
                    target += j // 2 * (4 - PACKED) * pieces * own_rows
                    across_ref[target : target + own_rows, :] = block
                else:
                    along_refs[j // 2][target : target + own_rows, :] = block


def group_columns(left, starts, members):
    return [jnp.take_along_axis(left, starts + k, axis=1, mode="promise_in_bounds") for k in range(members)]


def group_matmul(columns, right):
    terms = [column * right[k : k + 1, :] for k, column in enumerate(columns)]
    while len(terms) > 1:
        terms = [a + b for a, b in zip(terms[::2], terms[1::2])]
    return terms[0]


def precision_kernel(
    halo, spot_ref, damp_ref, live_ref, value_ref, error_ref, near_ref, far_ref, out_ref, value_win, error_win
):
    window = value_win.shape[0]
    even = lax.axis_index("tile") % 2 == 0
    window_parts(value_win, value_ref[...], near_ref, far_ref, 6 * halo, 2, even)
    window_parts(error_win, error_ref[...], near_ref, far_ref, 6 * halo, 3, even)
    spot = spot_ref[...]
    row, lane = spot // LANES, spot % LANES
    value = jnp.zeros(spot.shape, jnp.float32)
    error = jnp.zeros(spot.shape, jnp.float32)
    for r in range(window):
        hit = row == r
        line = jnp.broadcast_to(value_win[r : r + 1, :], spot.shape)
        value = jnp.where(hit, jnp.take_along_axis(line, lane, axis=1, mode="promise_in_bounds"), value)
        line = jnp.broadcast_to(error_win[r : r + 1, :], spot.shape)
        error = jnp.where(hit, jnp.take_along_axis(line, lane, axis=1, mode="promise_in_bounds"), error)
    out_ref[0] = value
    out_ref[1] = jnp.where(live_ref[...] > 0.0, 1.0 / (damp_ref[...] * error), 0.0)


def weight_kernel(members, three_ref, last_ref, *refs):
    half = members // 2
    near_refs, (spot_ref, known_ref, mix_ref, equiv_win) = refs[: half // 2 - 1], refs[half // 2 - 1 :]
    window = equiv_win.shape[0] // members
    for i, ref in enumerate((three_ref, *near_refs)):
        for j, place in enumerate((2 * i, 2 * i + 1, 2 * i + half)):
            equiv_win[place * window : (place + 1) * window, :] = ref[j * window : (j + 1) * window, :]
        place = 2 * i + half + 1
        equiv_win[place * window : (place + 1) * window, :] = last_ref[i * window : (i + 1) * window, :]
    value, precision = known_ref[0], known_ref[1]

    spot = spot_ref[...]
    pairs = spot.shape[0]
    row, lane = spot // LANES, spot % LANES
    rows_of = [jnp.broadcast_to(row[i : i + 1, :], (members, LANES)) for i in range(pairs)]
    lanes_of = [jnp.broadcast_to(lane[i : i + 1, :], (members, LANES)) for i in range(pairs)]
    picked = [jnp.zeros((members, LANES), jnp.float32) for i in range(pairs)]
    for r in range(window):
        source = equiv_win[pl.ds(r, members, stride=window), :]
        for i in range(pairs):
            got = jnp.take_along_axis(source, lanes_of[i], axis=1, mode="promise_in_bounds")
            picked[i] = jnp.where(rows_of[i] == r, got, picked[i])

    left_half = iota((members, LANES), 1) < LANES // 2
    weighted, spreads, innovations = [], [], []
    for i in range(pairs):
        mean = jnp.sum(picked[i], axis=0, keepdims=True) * (1.0 / members)
        spread = picked[i] - mean
        scaled = spread * precision[i : i + 1, :]
        innovation = jnp.broadcast_to(value[i : i + 1, :] - mean, (members, LANES))
        weighted.append(scaled)
        spreads.append(spread)
        innovations.append(innovation)
    every = lax.dot_general(
        jnp.concatenate(
            [jnp.where(left_half, x, 0.0) for x in weighted] + [jnp.where(left_half, 0.0, x) for x in weighted],
            axis=0,
        ),
        jnp.concatenate(spreads + spreads + innovations + innovations, axis=0),
        (((1,), (1,)), ((), ())),
        preferred_element_type=jnp.float32,
        precision=HIGH,
    )
    lane_at = iota((members, LANES), 1)
    patch_at = lane_at // members
    gram = jnp.zeros((members, LANES), jnp.float32)
    proj = jnp.zeros((members, LANES), jnp.float32)
    for p in range(2 * pairs):
        mine = patch_at == p
        block = every[p * members : (p + 1) * members, :]
        gram = jnp.where(mine, block[:, :LANES], gram)
        proj = jnp.where(mine, block[:, LANES:], proj)

    starts = lane_at - lane_at % members
    eye = (lane_at % members == iota((members, LANES), 0)).astype(jnp.float32)
    amat = gram + (members - 1.0) * eye
    diagonal = jnp.broadcast_to(jnp.sum(amat * eye, axis=0, keepdims=True), (members, LANES))
    trace = functools.reduce(jnp.add, group_columns(diagonal, starts, members))

    def iterate(sweep, carry):
        product, inverse = carry
        columns = group_columns(product, starts, members)
        square = group_matmul(columns, product)
        cube = group_matmul(columns, square)
        return (
            2.25 * product - 1.5 * square + 0.25 * cube,
            1.5 * inverse - 0.5 * group_matmul(columns, inverse),
        )

    product, inverse = lax.fori_loop(0, NS_ITERS, iterate, (amat / trace, eye), unroll=members <= 8)
    root = inverse / jnp.sqrt(trace)
    columns = group_columns(root, starts, members)
    wbar = group_matmul(columns, group_matmul(columns, proj))
    wtot = ((members - 1.0) ** 0.5) * root + wbar
    mix = wtot - jnp.sum(wtot, axis=0, keepdims=True) * (1.0 / members) + 1.0 / members
    mix_ref[...] = mix


def mix_kernel(sizes, recv_ref, mix_ref, *refs):
    members, own_rows, pieces = sizes
    half = members // 2
    rest_refs, (out_ref, table_ref) = refs[: half + 1], refs[half + 1 :]
    rest_rows = (4 - PACKED) * pieces * own_rows
    stride = recv_ref.shape[0] // members
    me = lax.axis_index("member")
    table_ref[...] = mix_ref[...].T
    bases = [pl.multiple_of((me ^ d) * stride, 8) for d in range(members)]

    def analyse(m, carry):
        for side in range(2):
            coefs = table_ref[pl.ds(side * members + m, own_rows, stride=2 * members), :]
            columns = [jnp.broadcast_to(coefs[:, d : d + 1], (own_rows, LANES)) for d in range(members)]
            for i in range(4):
                for q in range(side * pieces // 2, (side + 1) * pieces // 2):
                    total = None
                    for d in range(members):
                        if i < PACKED:
                            start = (i * pieces + q) * own_rows
                            block = recv_ref[pl.ds(bases[d] + start, own_rows), :]
                        else:
                            start = ((i - PACKED) * pieces + q) * own_rows
                            if d >= 2:
                                start += d % 2 * rest_rows
                            block = rest_refs[d if d < 2 else d // 2 + 1][start : start + own_rows, :]
                        term = columns[d] * block
                        total = term if total is None else total + term
                    out_ref[me ^ m, i, :, q * LANES : (q + 1) * LANES] = total
        return carry

    if members <= 8:
        for m in range(members):
            analyse(m, 0)
    else:
        lax.fori_loop(0, members, analyse, 0)


def trade(block, distance):
    members = lax.axis_size("member")
    return lax.ppermute(block, "member", [(i, i ^ distance) for i in range(members)])


def trade_blocks(equiv, across, along):
    half = len(along)
    size = along[0].shape[0]
    window = equiv.shape[0]
    passed = trade(across, 1)
    far = trade(equiv, half)
    three = jnp.concatenate([equiv, passed[half * size :], far], axis=0)
    near = [trade(three, 2 * i) for i in range(1, half // 2)]
    last = trade(jnp.concatenate([far] + [x[2 * window :] for x in near], axis=0), 1)
    pairs = [
        trade(jnp.concatenate([along[i], passed[i * size : (i + 1) * size]], axis=0), 2 * i)
        for i in range(1, half)
    ]
    return three, last, near, [along[0], passed, *pairs]


def swaps(near, far):
    count = lax.axis_size("tile")

    def pairs(start):
        twos = [(i, i + 1) for i in range(start, count - 1, 2)]
        return twos + [(b, a) for a, b in twos]

    far = lax.ppermute(far, "tile", pairs(1))
    near = lax.ppermute(near, "tile", pairs(0))
    return near, far


def vmem_specs(count):
    return [pl.BlockSpec(memory_space=pltpu.VMEM)] * count


def body(
    realization_array,
    water_depth,
    wet_mask,
    obs_cell,
    obs_value,
    obs_error,
    celer_gain,
    obs_list,
    obs_count,
):
    members = lax.axis_size("member")
    rows, width = water_depth.shape
    obs_tile = obs_cell.shape[0]
    radius = obs_tile // 8
    halo = radius * CELLS_PER_OBS // width + 2 * STEPS
    per_dev, slots = obs_list.shape[1:]
    own_rows = per_dev * REGION_POINTS // width
    pieces = width // LANES
    state = realization_array[0]
    panel = (obs_tile // LANES, LANES)
    pairs = per_dev * slots // LANES
    edges = pl.pallas_call(
        functools.partial(edge_kernel, halo),
        out_shape=[pltpu.VMEM((6 * halo + 8, width), jnp.float32)] * 2,
        in_specs=[pl.BlockSpec(memory_space=pl.ANY)] * 7,
        out_specs=vmem_specs(2),
        scratch_shapes=[
            pltpu.VMEM((2, halo, width), jnp.int32),
            pltpu.VMEM((2, 8, LANES), jnp.int32),
            pltpu.SemaphoreType.DMA((20,)),
        ],
        name="edges",
    )(
        state,
        water_depth,
        wet_mask,
        obs_cell.reshape(panel),
        celer_gain.reshape(panel),
        obs_value.reshape(panel),
        obs_error.reshape(panel),
    )
    near, far = swaps(*edges)

    window = (obs_tile + 2 * radius) // LANES
    packet = PACKED * pieces * own_rows
    grid = (pieces, rows + 2 * halo + 2 * PAD, LANES)
    half = members // 2
    rest_rows = (4 - PACKED) * pieces * own_rows
    sends, equiv, across, *along = pl.pallas_call(
        functools.partial(forecast_kernel, (members, own_rows, halo, radius)),
        out_shape=[
            pltpu.VMEM((members, packet, LANES), jnp.float32),
            jax.ShapeDtypeStruct((window, LANES), jnp.float32),
            jax.ShapeDtypeStruct((half * rest_rows + window, LANES), jnp.float32),
        ]
        + [jax.ShapeDtypeStruct((rest_rows, LANES), jnp.float32)] * half,
        in_specs=vmem_specs(7),
        out_specs=vmem_specs(3 + half),
        scratch_shapes=[pltpu.VMEM(grid, jnp.float32)] * 8 + [pltpu.VMEM((window, LANES), jnp.float32)] * 2,
        compiler_params=pltpu.CompilerParams(vmem_limit_bytes=24 * 2**20),
        name="forecast",
    )(
        state,
        water_depth,
        wet_mask,
        obs_cell.reshape(panel),
        celer_gain.reshape(panel),
        near,
        far,
    )
    received = lax.all_to_all(sends, "member", split_axis=0, concat_axis=0, tiled=True)
    three, last, near_equivs, rest = trade_blocks(equiv, across, along)
    received = received.reshape(members * packet, LANES)

    patch_index = lax.axis_index("member") * per_dev + jnp.arange(per_dev, dtype=jnp.int32)
    row_index = patch_index * REGION_POINTS // width
    centre = obs_tile + row_index * obs_tile // rows
    dist = (obs_list[0] - centre[:, None]).astype(jnp.float32) / radius
    damp = 1.0 + 4.0 * dist * dist
    live = jnp.arange(slots, dtype=jnp.int32)[None, :] < obs_count[0][:, None]
    spot = side_by_side(obs_list[0] - (obs_tile - radius), pairs)
    known = pl.pallas_call(
        functools.partial(precision_kernel, halo),
        out_shape=pltpu.VMEM((2, pairs, LANES), jnp.float32),
        in_specs=vmem_specs(7),
        out_specs=vmem_specs(1)[0],
        scratch_shapes=[pltpu.VMEM((window, LANES), jnp.float32)] * 2,
        name="precision",
    )(
        spot,
        side_by_side(damp, pairs),
        side_by_side(live.astype(jnp.float32), pairs),
        obs_value.reshape(panel),
        obs_error.reshape(panel),
        near,
        far,
    )
    mix = pl.pallas_call(
        functools.partial(weight_kernel, members),
        out_shape=jax.ShapeDtypeStruct((members, LANES), jnp.float32),
        in_specs=vmem_specs(4 + len(near_equivs)),
        out_specs=vmem_specs(1)[0],
        scratch_shapes=[pltpu.VMEM((members * window, LANES), jnp.float32)],
        compiler_params=pltpu.CompilerParams(vmem_limit_bytes=24 * 2**20),
        name="weights",
    )(three, last, *near_equivs, spot, known)
    analysed = pl.pallas_call(
        functools.partial(mix_kernel, (members, own_rows, pieces)),
        out_shape=jax.ShapeDtypeStruct((members, 4, own_rows, width), jnp.float32),
        in_specs=vmem_specs(3 + half),
        out_specs=vmem_specs(1)[0],
        scratch_shapes=[pltpu.VMEM((LANES, members), jnp.float32)],
        compiler_params=pltpu.CompilerParams(vmem_limit_bytes=24 * 2**20),
        name="mix",
    )(received, mix, *rest)
    result = lax.all_to_all(analysed, "member", split_axis=0, concat_axis=0, tiled=True)
    return jnp.transpose(result, (1, 0, 2, 3)).reshape(1, 4, rows, width)


def solution(mesh):
    return jax.shard_map(
        body,
        mesh=mesh,
        in_specs=(
            P("member", None, "tile", None),
            P("tile", None),
            P("tile", None),
            P("tile"),
            P("tile"),
            P("tile"),
            P("tile"),
            P("tile", "member", None),
            P("tile", "member"),
        ),
        out_specs=P("member", None, "tile", None),
        check_vma=False,
    )
```

```python
import functools

import jax
import jax.numpy as jnp
from jax import lax
from jax.experimental import pallas as pl
from jax.experimental.pallas import tpu as pltpu
from jax.sharding import PartitionSpec as P

REGION_POINTS = 256
STEPS = 4
NS_ITERS = 14
CELLS_PER_OBS = 8
LANES = 128

FRICTION = 0.98
PRESSURE = 0.25
DIVERGE = 0.25
FORCING = 0.05
UPWIND = 0.4
DAMPING = 0.02
HIGH = lax.Precision.HIGHEST

PAD = 8
PACKED = 2


def iota(shape, dim):
    return lax.broadcasted_iota(jnp.int32, shape, dim)


def edge_kernel(halo, *refs):
    grids, obs, outs = refs[:3], refs[3:7], refs[7:9]
    wet_ref, cell_ref, sems = refs[9:]
    rows = grids[1].shape[0]
    inner = obs[0].shape[0]
    even = lax.axis_index("tile") % 2 == 0
    copies = []

    def fetch(source, target):
        copies.append(pltpu.make_async_copy(source, target, sems.at[len(copies)]))
        copies[-1].start()

    for side, out in enumerate(outs):
        is_last = even if side == 0 else jnp.logical_not(even)
        start = pl.multiple_of(jnp.where(is_last, rows - halo, 0), 8)
        for i in range(6):
            source = (grids[0].at[i] if i < 4 else grids[i - 3]).at[pl.ds(start, halo), :]
            fetch(source, out.at[pl.ds(i * halo, halo), :] if i < 5 else wet_ref.at[side])
        start = pl.multiple_of(jnp.where(is_last, inner - 8, 0), 8)
        for j in range(4):
            target = out.at[pl.ds(6 * halo, 8), pl.ds(j * LANES, LANES)] if j else cell_ref.at[side]
            fetch(obs[j].at[pl.ds(start, 8), :], target)
    for copy in copies:
        copy.wait()
    for side, out in enumerate(outs):
        out[5 * halo : 6 * halo, :] = wet_ref[side].astype(jnp.float32)
        out[6 * halo : 6 * halo + 8, 0:LANES] = (cell_ref[side] % CELLS_PER_OBS).astype(jnp.float32)


def side_by_side(x, pairs):
    return jnp.concatenate([x[:pairs], x[pairs:]], axis=1)


def window_parts(win, own, near_ref, far_ref, base, j, even):
    inner = own.shape[0]
    span = (win.shape[0] - inner) // 2
    lanes = slice(j * LANES, (j + 1) * LANES)
    near, far = near_ref[base : base + 8, lanes], far_ref[base : base + 8, lanes]
    win[0:span, :] = jnp.where(even, far, near)[8 - span :, :]
    win[span : span + inner, :] = own
    win[span + inner :, :] = jnp.where(even, near, far)[:span, :]


def forecast_kernel(
    sizes,
    state_ref,
    depth_ref,
    mask_ref,
    cell_ref,
    gain_ref,
    near_ref,
    far_ref,
    *refs,
):
    members, own_rows, halo, obs_halo = sizes
    half = members // 2
    out_ref, equiv_ref, across_ref = refs[:3]
    along_refs, scratch = refs[3 : half + 3], refs[half + 3 :]
    s_ref, u_ref, v_ref, e_ref, h_ref, w_ref, flux_ref, part_ref, cell_win, gain_win = scratch
    even = lax.axis_index("tile") % 2 == 0
    rows, width = depth_ref.shape
    pieces = width // LANES
    total = rows + 2 * halo
    first = PAD + halo
    own = pl.ds(first, rows)
    fields = (s_ref, u_ref, v_ref, e_ref, h_ref, w_ref)
    near_at = pl.multiple_of(jnp.where(even, first + rows, PAD), 8)
    far_at = pl.multiple_of(jnp.where(even, PAD, first + rows), 8)
    edge = jnp.zeros((PAD, LANES), jnp.float32)
    for q in range(pieces):
        lanes = slice(q * LANES, (q + 1) * LANES)
        for i, field in enumerate(fields):
            field[q, pl.ds(near_at, halo), :] = near_ref[i * halo : (i + 1) * halo, lanes]
            field[q, pl.ds(far_at, halo), :] = far_ref[i * halo : (i + 1) * halo, lanes]
            if i < 4:
                field[q, own, :] = state_ref[i, :, lanes]
        h_ref[q, own, :] = depth_ref[:, lanes]
        s_ref[q, PAD : PAD + total, :] *= PRESSURE
        h_ref[q, PAD : PAD + total, :] *= PRESSURE * DIVERGE
        w_ref[q, own, :] = mask_ref[:, lanes].astype(jnp.float32)
        for field in (s_ref, e_ref, flux_ref):
            field[q, 0:PAD, :] = edge
            field[q, PAD + total : PAD + total + PAD, :] = edge

    lane = iota((8, LANES), 1)
    at_first, at_last = lane == 0, lane == LANES - 1

    def across(x):
        ahead = [pltpu.roll(piece, LANES - 1, 1) for piece in x] + [0.0]
        behind = [0.0] + [pltpu.roll(piece, 1, 1) for piece in x]
        return [
            jnp.where(at_last, ahead[q + 1], ahead[q]) - jnp.where(at_first, behind[q], behind[q + 1])
            for q in range(pieces)
        ]

    outer = (halo - obs_halo * CELLS_PER_OBS // width) // 8
    for step in range(STEPS):
        skip, skip_energy = (outer, halo // 8) if step == STEPS - 1 else (0, 0)
        for block in range(total // 8):
            r = PAD + 8 * block
            here, below, above = pl.ds(r, 8), pl.ds(r + 1, 8), pl.ds(r - 1, 8)
            inside = skip <= block < total // 8 - skip
            s = [s_ref[q, here, :] for q in range(pieces)]
            slope = across(s) if inside else None
            flux = []
            for q in range(pieces):
                w, h = w_ref[q, here, :], h_ref[q, here, :]
                u = w * (FRICTION * u_ref[q, here, :] - (s_ref[q, below, :] - s_ref[q, above, :]))
                u_ref[q, here, :] = u
                flux_ref[q, here, :] = h * u
                if inside:
                    v = w * (FRICTION * v_ref[q, here, :] - slope[q])
                    v_ref[q, here, :] = v
                    flux.append(h * v)
            if inside:
                rise = across(flux)
                for q in range(pieces):
                    part_ref[q, here, :] = s[q] - rise[q] + (PRESSURE * FORCING) * e_ref[q, here, :]
        for block in reversed(range(skip, total // 8 - skip)):
            r = PAD + 8 * block
            here, below, above = pl.ds(r, 8), pl.ds(r + 1, 8), pl.ds(r - 1, 8)
            for q in range(pieces):
                w = w_ref[q, here, :]
                rise = flux_ref[q, below, :] - flux_ref[q, above, :]
                s_ref[q, here, :] = w * (part_ref[q, here, :] - rise)
                if skip_energy <= block < total // 8 - skip_energy:
                    e = e_ref[q, here, :]
                    e_ref[q, here, :] = w * ((1.0 - UPWIND - DAMPING) * e + UPWIND * e_ref[q, above, :])

    window = cell_win.shape[0]
    base = 6 * halo
    offsets = (cell_ref[...] % CELLS_PER_OBS).astype(jnp.float32)
    window_parts(cell_win, offsets, near_ref, far_ref, base, 0, even)
    window_parts(gain_win, gain_ref[...], near_ref, far_ref, base, 1, even)
    half = width // CELLS_PER_OBS
    top = first - obs_halo // half
    column = iota((LANES, 2 * width), 1)
    cell_at = column // (2 * LANES) * LANES + column % LANES
    parity = column // LANES % 2
    spread = jnp.where(
        iota((LANES, 2 * width), 0) == parity * half + cell_at // CELLS_PER_OBS, 1.0, 0.0
    ).astype(jnp.bfloat16)
    offset = jnp.dot(cell_win[...].astype(jnp.bfloat16), spread, preferred_element_type=jnp.float32)
    level = jnp.concatenate(
        [s_ref[q, pl.ds(top + side, window, stride=2), :] for q in range(pieces) for side in range(2)], axis=1
    )
    place = (iota((window, 2 * width), 1) % CELLS_PER_OBS).astype(jnp.float32)
    rest = jnp.where(jnp.abs(offset - place) < 0.5, level, 0.0)
    equiv = jnp.zeros((window, LANES), jnp.float32)
    parts = []
    for i in range(3):
        parts.append(rest.astype(jnp.bfloat16))
        rest = rest - parts[-1].astype(jnp.float32)
    for part in reversed(parts):
        equiv = equiv + lax.dot_general(
            part, spread, (((1,), (1,)), ((), ())), preferred_element_type=jnp.float32
        )
    equiv = equiv * ((1.0 / PRESSURE) * gain_win[...])
    equiv_ref[...] = equiv
    across_ref[across_ref.shape[0] - window :, :] = equiv

    me = lax.axis_index("member")
    for j in range(members):
        source = first + j * own_rows
        for i in range(PACKED):
            for q in range(pieces):
                target = (i * pieces + q) * own_rows
                block = fields[i][q, source : source + own_rows, :]
                out_ref[j, target : target + own_rows, :] = block if i else block * (1.0 / PRESSURE)
        source = pl.multiple_of(first + (me ^ j) * own_rows, min(own_rows, 8))
        for i in range(PACKED, 4):
            for q in range(pieces):
                target = ((i - PACKED) * pieces + q) * own_rows
                block = fields[i][q, pl.ds(source, own_rows), :]
                if j % 2:
                    target += j // 2 * (4 - PACKED) * pieces * own_rows
                    across_ref[target : target + own_rows, :] = block
                else:
                    along_refs[j // 2][target : target + own_rows, :] = block


def group_columns(left, starts, members):
    return [jnp.take_along_axis(left, starts + k, axis=1, mode="promise_in_bounds") for k in range(members)]


def group_matmul(columns, right):
    terms = [column * right[k : k + 1, :] for k, column in enumerate(columns)]
    while len(terms) > 1:
        terms = [a + b for a, b in zip(terms[::2], terms[1::2])]
    return terms[0]


def precision_kernel(
    sizes, list_ref, count_ref, value_ref, error_ref, near_ref, far_ref, out_ref, spot_ref, value_win, error_win
):
    halo, rows, width, radius = sizes
    window = value_win.shape[0]
    per_dev, slots = list_ref.shape
    obs_tile = value_ref.shape[0] * LANES
    even = lax.axis_index("tile") % 2 == 0
    window_parts(value_win, value_ref[...], near_ref, far_ref, 6 * halo, 2, even)
    window_parts(error_win, error_ref[...], near_ref, far_ref, 6 * halo, 3, even)
    named = list_ref[...]
    patch = iota((per_dev, slots), 0)
    row_index = (lax.axis_index("member") * per_dev + patch) * REGION_POINTS // width
    dist = (named - (obs_tile + row_index * obs_tile // rows)).astype(jnp.float32) / radius
    counts = jnp.zeros((per_dev, slots), jnp.int32)
    for p in range(per_dev):
        counts = jnp.where(patch == p, count_ref[0, p], counts)
    live = jnp.where(iota((per_dev, slots), 1) < counts, 1.0, 0.0)
    live = side_by_side(live, per_dev // 2)
    damp = side_by_side(1.0 + 4.0 * dist * dist, per_dev // 2)
    spot = side_by_side(named - (obs_tile - radius), per_dev // 2)
    spot_ref[...] = spot
    row, lane = spot // LANES, spot % LANES
    value = jnp.zeros(spot.shape, jnp.float32)
    error = jnp.zeros(spot.shape, jnp.float32)
    for r in range(window):
        hit = row == r
        line = jnp.broadcast_to(value_win[r : r + 1, :], spot.shape)
        value = jnp.where(hit, jnp.take_along_axis(line, lane, axis=1, mode="promise_in_bounds"), value)
        line = jnp.broadcast_to(error_win[r : r + 1, :], spot.shape)
        error = jnp.where(hit, jnp.take_along_axis(line, lane, axis=1, mode="promise_in_bounds"), error)
    out_ref[0] = value
    out_ref[1] = jnp.where(live > 0.0, 1.0 / (damp * error), 0.0)


def weight_kernel(members, three_ref, last_ref, *refs):
    half = members // 2
    near_refs, (spot_ref, known_ref, mix_ref, equiv_win) = refs[: half // 2 - 1], refs[half // 2 - 1 :]
    window = equiv_win.shape[0] // members
    for i, ref in enumerate((three_ref, *near_refs)):
        for j, place in enumerate((2 * i, 2 * i + 1, 2 * i + half)):
            equiv_win[place * window : (place + 1) * window, :] = ref[j * window : (j + 1) * window, :]
        place = 2 * i + half + 1
        equiv_win[place * window : (place + 1) * window, :] = last_ref[i * window : (i + 1) * window, :]
    value, precision = known_ref[0], known_ref[1]

    spot = spot_ref[...]
    pairs = spot.shape[0]
    row, lane = spot // LANES, spot % LANES
    rows_of = [jnp.broadcast_to(row[i : i + 1, :], (members, LANES)) for i in range(pairs)]
    lanes_of = [jnp.broadcast_to(lane[i : i + 1, :], (members, LANES)) for i in range(pairs)]
    picked = [jnp.zeros((members, LANES), jnp.float32) for i in range(pairs)]
    for r in range(window):
        source = equiv_win[pl.ds(r, members, stride=window), :]
        for i in range(pairs):
            got = jnp.take_along_axis(source, lanes_of[i], axis=1, mode="promise_in_bounds")
            picked[i] = jnp.where(rows_of[i] == r, got, picked[i])

    left_half = iota((members, LANES), 1) < LANES // 2
    weighted, spreads, innovations = [], [], []
    for i in range(pairs):
        mean = jnp.sum(picked[i], axis=0, keepdims=True) * (1.0 / members)
        spread = picked[i] - mean
        scaled = spread * precision[i : i + 1, :]
        innovation = jnp.broadcast_to(value[i : i + 1, :] - mean, (members, LANES))
        weighted.append(scaled)
        spreads.append(spread)
        innovations.append(innovation)
    every = lax.dot_general(
        jnp.concatenate(
            [jnp.where(left_half, x, 0.0) for x in weighted] + [jnp.where(left_half, 0.0, x) for x in weighted],
            axis=0,
        ),
        jnp.concatenate(spreads + spreads + innovations + innovations, axis=0),
        (((1,), (1,)), ((), ())),
        preferred_element_type=jnp.float32,
        precision=HIGH,
    )
    lane_at = iota((members, LANES), 1)
    patch_at = lane_at // members
    gram = jnp.zeros((members, LANES), jnp.float32)
    proj = jnp.zeros((members, LANES), jnp.float32)
    for p in range(2 * pairs):
        mine = patch_at == p
        block = every[p * members : (p + 1) * members, :]
        gram = jnp.where(mine, block[:, :LANES], gram)
        proj = jnp.where(mine, block[:, LANES:], proj)

    starts = lane_at - lane_at % members
    eye = (lane_at % members == iota((members, LANES), 0)).astype(jnp.float32)
    amat = gram + (members - 1.0) * eye
    diagonal = jnp.broadcast_to(jnp.sum(amat * eye, axis=0, keepdims=True), (members, LANES))
    trace = functools.reduce(jnp.add, group_columns(diagonal, starts, members))

    def iterate(sweep, carry):
        product, inverse = carry
        columns = group_columns(product, starts, members)
        square = group_matmul(columns, product)
        cube = group_matmul(columns, square)
        return (
            2.25 * product - 1.5 * square + 0.25 * cube,
            1.5 * inverse - 0.5 * group_matmul(columns, inverse),
        )

    product, inverse = lax.fori_loop(0, NS_ITERS, iterate, (amat / trace, eye), unroll=members <= 8)
    root = inverse / jnp.sqrt(trace)
    columns = group_columns(root, starts, members)
    wbar = group_matmul(columns, group_matmul(columns, proj))
    wtot = ((members - 1.0) ** 0.5) * root + wbar
    mix = wtot - jnp.sum(wtot, axis=0, keepdims=True) * (1.0 / members) + 1.0 / members
    mix_ref[...] = mix


def mix_kernel(sizes, recv_ref, mix_ref, *refs):
    members, own_rows, pieces = sizes
    half = members // 2
    rest_refs, (out_ref, table_ref) = refs[: half + 1], refs[half + 1 :]
    rest_rows = (4 - PACKED) * pieces * own_rows
    stride = recv_ref.shape[0] // members
    me = lax.axis_index("member")
    table_ref[...] = mix_ref[...].T
    bases = [pl.multiple_of((me ^ d) * stride, 8) for d in range(members)]

    def analyse(m, carry):
        for side in range(2):
            coefs = table_ref[pl.ds(side * members + m, own_rows, stride=2 * members), :]
            columns = [jnp.broadcast_to(coefs[:, d : d + 1], (own_rows, LANES)) for d in range(members)]
            for i in range(4):
                for q in range(side * pieces // 2, (side + 1) * pieces // 2):
                    total = None
                    for d in range(members):
                        if i < PACKED:
                            start = (i * pieces + q) * own_rows
                            block = recv_ref[pl.ds(bases[d] + start, own_rows), :]
                        else:
                            start = ((i - PACKED) * pieces + q) * own_rows
                            if d >= 2:
                                start += d % 2 * rest_rows
                            block = rest_refs[d if d < 2 else d // 2 + 1][start : start + own_rows, :]
                        term = columns[d] * block
                        total = term if total is None else total + term
                    out_ref[me ^ m, i, :, q * LANES : (q + 1) * LANES] = total
        return carry

    if members <= 8:
        for m in range(members):
            analyse(m, 0)
    else:
        lax.fori_loop(0, members, analyse, 0)


def trade(block, distance):
    members = lax.axis_size("member")
    return lax.ppermute(block, "member", [(i, i ^ distance) for i in range(members)])


def trade_blocks(equiv, across, along):
    half = len(along)
    size = along[0].shape[0]
    window = equiv.shape[0]
    passed = trade(across, 1)
    far = trade(equiv, half)
    three = jnp.concatenate([equiv, passed[half * size :], far], axis=0)
    near = [trade(three, 2 * i) for i in range(1, half // 2)]
    last = trade(jnp.concatenate([far] + [x[2 * window :] for x in near], axis=0), 1)
    pairs = [
        trade(jnp.concatenate([along[i], passed[i * size : (i + 1) * size]], axis=0), 2 * i)
        for i in range(1, half)
    ]
    return three, last, near, [along[0], passed, *pairs]


def swaps(near, far):
    count = lax.axis_size("tile")

    def pairs(start):
        twos = [(i, i + 1) for i in range(start, count - 1, 2)]
        return twos + [(b, a) for a, b in twos]

    far = lax.ppermute(far, "tile", pairs(1))
    near = lax.ppermute(near, "tile", pairs(0))
    return near, far


def vmem_specs(count):
    return [pl.BlockSpec(memory_space=pltpu.VMEM)] * count


def body(
    realization_array,
    water_depth,
    wet_mask,
    obs_cell,
    obs_value,
    obs_error,
    celer_gain,
    obs_list,
    obs_count,
):
    members = lax.axis_size("member")
    rows, width = water_depth.shape
    obs_tile = obs_cell.shape[0]
    radius = obs_tile // 8
    halo = radius * CELLS_PER_OBS // width + 2 * STEPS
    per_dev, slots = obs_list.shape[1:]
    own_rows = per_dev * REGION_POINTS // width
    pieces = width // LANES
    state = realization_array[0]
    panel = (obs_tile // LANES, LANES)
    pairs = per_dev * slots // LANES
    edges = pl.pallas_call(
        functools.partial(edge_kernel, halo),
        out_shape=[pltpu.VMEM((6 * halo + 8, width), jnp.float32)] * 2,
        in_specs=[pl.BlockSpec(memory_space=pl.ANY)] * 7,
        out_specs=vmem_specs(2),
        scratch_shapes=[
            pltpu.VMEM((2, halo, width), jnp.int32),
            pltpu.VMEM((2, 8, LANES), jnp.int32),
            pltpu.SemaphoreType.DMA((20,)),
        ],
        name="edges",
    )(
        state,
        water_depth,
        wet_mask,
        obs_cell.reshape(panel),
        celer_gain.reshape(panel),
        obs_value.reshape(panel),
        obs_error.reshape(panel),
    )
    near, far = swaps(*edges)

    window = (obs_tile + 2 * radius) // LANES
    packet = PACKED * pieces * own_rows
    grid = (pieces, rows + 2 * halo + 2 * PAD, LANES)
    half = members // 2
    rest_rows = (4 - PACKED) * pieces * own_rows
    sends, equiv, across, *along = pl.pallas_call(
        functools.partial(forecast_kernel, (members, own_rows, halo, radius)),
        out_shape=[
            pltpu.VMEM((members, packet, LANES), jnp.float32),
            jax.ShapeDtypeStruct((window, LANES), jnp.float32),
            jax.ShapeDtypeStruct((half * rest_rows + window, LANES), jnp.float32),
        ]
        + [jax.ShapeDtypeStruct((rest_rows, LANES), jnp.float32)] * half,
        in_specs=vmem_specs(7),
        out_specs=vmem_specs(3 + half),
        scratch_shapes=[pltpu.VMEM(grid, jnp.float32)] * 8 + [pltpu.VMEM((window, LANES), jnp.float32)] * 2,
        compiler_params=pltpu.CompilerParams(vmem_limit_bytes=24 * 2**20),
        name="forecast",
    )(
        state,
        water_depth,
        wet_mask,
        obs_cell.reshape(panel),
        celer_gain.reshape(panel),
        near,
        far,
    )
    received = lax.all_to_all(sends, "member", split_axis=0, concat_axis=0, tiled=True)
    three, last, near_equivs, rest = trade_blocks(equiv, across, along)
    received = received.reshape(members * packet, LANES)

    known, spot = pl.pallas_call(
        functools.partial(precision_kernel, (halo, rows, width, radius)),
        out_shape=[pltpu.VMEM((2, pairs, LANES), jnp.float32), pltpu.VMEM((pairs, LANES), jnp.int32)],
        in_specs=vmem_specs(1) + [pl.BlockSpec(memory_space=pltpu.SMEM)] + vmem_specs(4),
        out_specs=vmem_specs(2),
        scratch_shapes=[pltpu.VMEM((window, LANES), jnp.float32)] * 2,
        name="precision",
    )(
        obs_list[0],
        obs_count,
        obs_value.reshape(panel),
        obs_error.reshape(panel),
        near,
        far,
    )
    mix = pl.pallas_call(
        functools.partial(weight_kernel, members),
        out_shape=jax.ShapeDtypeStruct((members, LANES), jnp.float32),
        in_specs=vmem_specs(4 + len(near_equivs)),
        out_specs=vmem_specs(1)[0],
        scratch_shapes=[pltpu.VMEM((members * window, LANES), jnp.float32)],
        compiler_params=pltpu.CompilerParams(vmem_limit_bytes=24 * 2**20),
        name="weights",
    )(three, last, *near_equivs, spot, known)
    analysed = pl.pallas_call(
        functools.partial(mix_kernel, (members, own_rows, pieces)),
        out_shape=jax.ShapeDtypeStruct((members, 4, own_rows, width), jnp.float32),
        in_specs=vmem_specs(3 + half),
        out_specs=vmem_specs(1)[0],
        scratch_shapes=[pltpu.VMEM((LANES, members), jnp.float32)],
        compiler_params=pltpu.CompilerParams(vmem_limit_bytes=24 * 2**20),
        name="mix",
    )(received, mix, *rest)
    result = lax.all_to_all(analysed, "member", split_axis=0, concat_axis=0, tiled=True)
    return jnp.transpose(result, (1, 0, 2, 3)).reshape(1, 4, rows, width)


def solution(mesh):
    return jax.shard_map(
        body,
        mesh=mesh,
        in_specs=(
            P("member", None, "tile", None),
            P("tile", None),
            P("tile", None),
            P("tile"),
            P("tile"),
            P("tile"),
            P("tile"),
            P("tile", "member", None),
            P("tile", "member"),
        ),
        out_specs=P("member", None, "tile", None),
        check_vma=False,
    )
```

```python
import functools

import jax
import jax.numpy as jnp
from jax import lax
from jax.experimental import pallas as pl
from jax.experimental.pallas import tpu as pltpu
from jax.sharding import PartitionSpec as P

REGION_POINTS = 256
STEPS = 4
NS_ITERS = 14
CELLS_PER_OBS = 8
LANES = 128

FRICTION = 0.98
PRESSURE = 0.25
DIVERGE = 0.25
FORCING = 0.05
UPWIND = 0.4
DAMPING = 0.02
HIGH = lax.Precision.HIGHEST

PAD = 8


def iota(shape, dim):
    return lax.broadcasted_iota(jnp.int32, shape, dim)


def edge_kernel(halo, *refs):
    grids, obs, outs = refs[:3], refs[3:7], refs[7:9]
    wet_ref, cell_ref, sems = refs[9:]
    rows = grids[1].shape[0]
    inner = obs[0].shape[0]
    even = lax.axis_index("tile") % 2 == 0
    copies = []

    def fetch(source, target):
        copies.append(pltpu.make_async_copy(source, target, sems.at[len(copies)]))
        copies[-1].start()

    for side, out in enumerate(outs):
        is_last = even if side == 0 else jnp.logical_not(even)
        start = pl.multiple_of(jnp.where(is_last, rows - halo, 0), 8)
        for i in range(6):
            source = (grids[0].at[i] if i < 4 else grids[i - 3]).at[pl.ds(start, halo), :]
            fetch(source, out.at[pl.ds(i * halo, halo), :] if i < 5 else wet_ref.at[side])
        start = pl.multiple_of(jnp.where(is_last, inner - 8, 0), 8)
        for j in range(4):
            target = out.at[pl.ds(6 * halo, 8), pl.ds(j * LANES, LANES)] if j else cell_ref.at[side]
            fetch(obs[j].at[pl.ds(start, 8), :], target)
    for copy in copies:
        copy.wait()
    for side, out in enumerate(outs):
        out[5 * halo : 6 * halo, :] = wet_ref[side].astype(jnp.float32)
        out[6 * halo : 6 * halo + 8, 0:LANES] = (cell_ref[side] % CELLS_PER_OBS).astype(jnp.float32)


def side_by_side(x, pairs):
    return jnp.concatenate([x[:pairs], x[pairs:]], axis=1)


def window_parts(win, own, near_ref, far_ref, base, j, even):
    inner = own.shape[0]
    span = (win.shape[0] - inner) // 2
    lanes = slice(j * LANES, (j + 1) * LANES)
    near, far = near_ref[base : base + 8, lanes], far_ref[base : base + 8, lanes]
    win[0:span, :] = jnp.where(even, far, near)[8 - span :, :]
    win[span : span + inner, :] = own
    win[span + inner :, :] = jnp.where(even, near, far)[:span, :]


def forecast_kernel(
    sizes,
    state_ref,
    depth_ref,
    mask_ref,
    cell_ref,
    gain_ref,
    near_ref,
    far_ref,
    *refs,
):
    members, own_rows, halo, obs_halo = sizes
    half = members // 2
    equiv_ref, across_ref = refs[:2]
    along_refs, scratch = refs[2 : half + 2], refs[half + 2 :]
    s_ref, u_ref, v_ref, e_ref, h_ref, w_ref, flux_ref, part_ref, cell_win, gain_win = scratch
    even = lax.axis_index("tile") % 2 == 0
    rows, width = depth_ref.shape
    pieces = width // LANES
    total = rows + 2 * halo
    first = PAD + halo
    own = pl.ds(first, rows)
    fields = (s_ref, u_ref, v_ref, e_ref, h_ref, w_ref)
    near_at = pl.multiple_of(jnp.where(even, first + rows, PAD), 8)
    far_at = pl.multiple_of(jnp.where(even, PAD, first + rows), 8)
    edge = jnp.zeros((PAD, LANES), jnp.float32)
    for q in range(pieces):
        lanes = slice(q * LANES, (q + 1) * LANES)
        for i, field in enumerate(fields):
            field[q, pl.ds(near_at, halo), :] = near_ref[i * halo : (i + 1) * halo, lanes]
            field[q, pl.ds(far_at, halo), :] = far_ref[i * halo : (i + 1) * halo, lanes]
            if i < 4:
                field[q, own, :] = state_ref[i, :, lanes]
        h_ref[q, own, :] = depth_ref[:, lanes]
        s_ref[q, PAD : PAD + total, :] *= PRESSURE
        h_ref[q, PAD : PAD + total, :] *= PRESSURE * DIVERGE
        w_ref[q, own, :] = mask_ref[:, lanes].astype(jnp.float32)
        for field in (s_ref, e_ref, flux_ref):
            field[q, 0:PAD, :] = edge
            field[q, PAD + total : PAD + total + PAD, :] = edge

    lane = iota((8, LANES), 1)
    at_first, at_last = lane == 0, lane == LANES - 1

    def across(x):
        ahead = [pltpu.roll(piece, LANES - 1, 1) for piece in x] + [0.0]
        behind = [0.0] + [pltpu.roll(piece, 1, 1) for piece in x]
        return [
            jnp.where(at_last, ahead[q + 1], ahead[q]) - jnp.where(at_first, behind[q], behind[q + 1])
            for q in range(pieces)
        ]

    outer = (halo - obs_halo * CELLS_PER_OBS // width) // 8
    for step in range(STEPS):
        skip, skip_energy = (outer, halo // 8) if step == STEPS - 1 else (0, 0)
        for block in range(total // 8):
            r = PAD + 8 * block
            here, below, above = pl.ds(r, 8), pl.ds(r + 1, 8), pl.ds(r - 1, 8)
            inside = skip <= block < total // 8 - skip
            s = [s_ref[q, here, :] for q in range(pieces)]
            slope = across(s) if inside else None
            flux = []
            for q in range(pieces):
                w, h = w_ref[q, here, :], h_ref[q, here, :]
                u = w * (FRICTION * u_ref[q, here, :] - (s_ref[q, below, :] - s_ref[q, above, :]))
                u_ref[q, here, :] = u
                flux_ref[q, here, :] = h * u
                if inside:
                    v = w * (FRICTION * v_ref[q, here, :] - slope[q])
                    v_ref[q, here, :] = v
                    flux.append(h * v)
            if inside:
                rise = across(flux)
                for q in range(pieces):
                    part_ref[q, here, :] = s[q] - rise[q] + (PRESSURE * FORCING) * e_ref[q, here, :]
        for block in reversed(range(skip, total // 8 - skip)):
            r = PAD + 8 * block
            here, below, above = pl.ds(r, 8), pl.ds(r + 1, 8), pl.ds(r - 1, 8)
            for q in range(pieces):
                w = w_ref[q, here, :]
                rise = flux_ref[q, below, :] - flux_ref[q, above, :]
                s_ref[q, here, :] = w * (part_ref[q, here, :] - rise)
                if skip_energy <= block < total // 8 - skip_energy:
                    e = e_ref[q, here, :]
                    e_ref[q, here, :] = w * ((1.0 - UPWIND - DAMPING) * e + UPWIND * e_ref[q, above, :])

    window = cell_win.shape[0]
    base = 6 * halo
    offsets = (cell_ref[...] % CELLS_PER_OBS).astype(jnp.float32)
    window_parts(cell_win, offsets, near_ref, far_ref, base, 0, even)
    window_parts(gain_win, gain_ref[...], near_ref, far_ref, base, 1, even)
    half = width // CELLS_PER_OBS
    top = first - obs_halo // half
    column = iota((LANES, 2 * width), 1)
    cell_at = column // (2 * LANES) * LANES + column % LANES
    parity = column // LANES % 2
    spread = jnp.where(
        iota((LANES, 2 * width), 0) == parity * half + cell_at // CELLS_PER_OBS, 1.0, 0.0
    ).astype(jnp.bfloat16)
    offset = jnp.dot(cell_win[...].astype(jnp.bfloat16), spread, preferred_element_type=jnp.float32)
    level = jnp.concatenate(
        [s_ref[q, pl.ds(top + side, window, stride=2), :] for q in range(pieces) for side in range(2)], axis=1
    )
    place = (iota((window, 2 * width), 1) % CELLS_PER_OBS).astype(jnp.float32)
    rest = jnp.where(jnp.abs(offset - place) < 0.5, level, 0.0)
    equiv = jnp.zeros((window, LANES), jnp.float32)
    parts = []
    for i in range(3):
        parts.append(rest.astype(jnp.bfloat16))
        rest = rest - parts[-1].astype(jnp.float32)
    for part in reversed(parts):
        equiv = equiv + lax.dot_general(
            part, spread, (((1,), (1,)), ((), ())), preferred_element_type=jnp.float32
        )
    equiv = equiv * ((1.0 / PRESSURE) * gain_win[...])
    equiv_ref[...] = equiv
    across_ref[across_ref.shape[0] - window :, :] = equiv

    me = lax.axis_index("member")
    for j in range(members):
        source = pl.multiple_of(first + (me ^ j) * own_rows, min(own_rows, 8))
        for i in range(4):
            for q in range(pieces):
                target = (i * pieces + q) * own_rows
                block = fields[i][q, pl.ds(source, own_rows), :]
                block = block if i else block * (1.0 / PRESSURE)
                if j % 2:
                    target += j // 2 * 4 * pieces * own_rows
                    across_ref[target : target + own_rows, :] = block
                else:
                    along_refs[j // 2][target : target + own_rows, :] = block


def group_columns(left, starts, members):
    return [jnp.take_along_axis(left, starts + k, axis=1, mode="promise_in_bounds") for k in range(members)]


def group_matmul(columns, right):
    terms = [column * right[k : k + 1, :] for k, column in enumerate(columns)]
    while len(terms) > 1:
        terms = [a + b for a, b in zip(terms[::2], terms[1::2])]
    return terms[0]


def precision_kernel(
    sizes, list_ref, count_ref, value_ref, error_ref, near_ref, far_ref, out_ref, spot_ref, value_win, error_win
):
    halo, rows, width, radius = sizes
    window = value_win.shape[0]
    per_dev, slots = list_ref.shape
    obs_tile = value_ref.shape[0] * LANES
    even = lax.axis_index("tile") % 2 == 0
    window_parts(value_win, value_ref[...], near_ref, far_ref, 6 * halo, 2, even)
    window_parts(error_win, error_ref[...], near_ref, far_ref, 6 * halo, 3, even)
    named = list_ref[...]
    patch = iota((per_dev, slots), 0)
    row_index = (lax.axis_index("member") * per_dev + patch) * REGION_POINTS // width
    dist = (named - (obs_tile + row_index * obs_tile // rows)).astype(jnp.float32) / radius
    counts = jnp.zeros((per_dev, slots), jnp.int32)
    for p in range(per_dev):
        counts = jnp.where(patch == p, count_ref[0, p], counts)
    live = jnp.where(iota((per_dev, slots), 1) < counts, 1.0, 0.0)
    live = side_by_side(live, per_dev // 2)
    damp = side_by_side(1.0 + 4.0 * dist * dist, per_dev // 2)
    spot = side_by_side(named - (obs_tile - radius), per_dev // 2)
    spot_ref[...] = spot
    row, lane = spot // LANES, spot % LANES
    value = jnp.zeros(spot.shape, jnp.float32)
    error = jnp.zeros(spot.shape, jnp.float32)
    for r in range(window):
        hit = row == r
        line = jnp.broadcast_to(value_win[r : r + 1, :], spot.shape)
        value = jnp.where(hit, jnp.take_along_axis(line, lane, axis=1, mode="promise_in_bounds"), value)
        line = jnp.broadcast_to(error_win[r : r + 1, :], spot.shape)
        error = jnp.where(hit, jnp.take_along_axis(line, lane, axis=1, mode="promise_in_bounds"), error)
    out_ref[0] = value
    out_ref[1] = jnp.where(live > 0.0, 1.0 / (damp * error), 0.0)


def weight_kernel(members, three_ref, last_ref, *refs):
    half = members // 2
    near_refs, (spot_ref, known_ref, mix_ref, equiv_win) = refs[: half // 2 - 1], refs[half // 2 - 1 :]
    window = equiv_win.shape[0] // members
    for i, ref in enumerate((three_ref, *near_refs)):
        for j, place in enumerate((2 * i, 2 * i + 1, 2 * i + half)):
            equiv_win[place * window : (place + 1) * window, :] = ref[j * window : (j + 1) * window, :]
        place = 2 * i + half + 1
        equiv_win[place * window : (place + 1) * window, :] = last_ref[i * window : (i + 1) * window, :]
    value, precision = known_ref[0], known_ref[1]

    spot = spot_ref[...]
    pairs = spot.shape[0]
    row, lane = spot // LANES, spot % LANES
    rows_of = [jnp.broadcast_to(row[i : i + 1, :], (members, LANES)) for i in range(pairs)]
    lanes_of = [jnp.broadcast_to(lane[i : i + 1, :], (members, LANES)) for i in range(pairs)]
    picked = [jnp.zeros((members, LANES), jnp.float32) for i in range(pairs)]
    for r in range(window):
        source = equiv_win[pl.ds(r, members, stride=window), :]
        for i in range(pairs):
            got = jnp.take_along_axis(source, lanes_of[i], axis=1, mode="promise_in_bounds")
            picked[i] = jnp.where(rows_of[i] == r, got, picked[i])

    left_half = iota((members, LANES), 1) < LANES // 2
    weighted, spreads, innovations = [], [], []
    for i in range(pairs):
        mean = jnp.sum(picked[i], axis=0, keepdims=True) * (1.0 / members)
        spread = picked[i] - mean
        scaled = spread * precision[i : i + 1, :]
        innovation = jnp.broadcast_to(value[i : i + 1, :] - mean, (members, LANES))
        weighted.append(scaled)
        spreads.append(spread)
        innovations.append(innovation)
    every = lax.dot_general(
        jnp.concatenate(
            [jnp.where(left_half, x, 0.0) for x in weighted] + [jnp.where(left_half, 0.0, x) for x in weighted],
            axis=0,
        ),
        jnp.concatenate(spreads + spreads + innovations + innovations, axis=0),
        (((1,), (1,)), ((), ())),
        preferred_element_type=jnp.float32,
        precision=HIGH,
    )
    lane_at = iota((members, LANES), 1)
    patch_at = lane_at // members
    gram = jnp.zeros((members, LANES), jnp.float32)
    proj = jnp.zeros((members, LANES), jnp.float32)
    for p in range(2 * pairs):
        mine = patch_at == p
        block = every[p * members : (p + 1) * members, :]
        gram = jnp.where(mine, block[:, :LANES], gram)
        proj = jnp.where(mine, block[:, LANES:], proj)

    starts = lane_at - lane_at % members
    eye = (lane_at % members == iota((members, LANES), 0)).astype(jnp.float32)
    amat = gram + (members - 1.0) * eye
    diagonal = jnp.broadcast_to(jnp.sum(amat * eye, axis=0, keepdims=True), (members, LANES))
    trace = functools.reduce(jnp.add, group_columns(diagonal, starts, members))

    def iterate(sweep, carry):
        product, inverse = carry
        columns = group_columns(product, starts, members)
        square = group_matmul(columns, product)
        cube = group_matmul(columns, square)
        return (
            2.25 * product - 1.5 * square + 0.25 * cube,
            1.5 * inverse - 0.5 * group_matmul(columns, inverse),
        )

    product, inverse = lax.fori_loop(0, NS_ITERS, iterate, (amat / trace, eye), unroll=members <= 8)
    root = inverse / jnp.sqrt(trace)
    columns = group_columns(root, starts, members)
    wbar = group_matmul(columns, group_matmul(columns, proj))
    wtot = ((members - 1.0) ** 0.5) * root + wbar
    mix = wtot - jnp.sum(wtot, axis=0, keepdims=True) * (1.0 / members) + 1.0 / members
    mix_ref[...] = mix


def mix_kernel(sizes, mix_ref, *refs):
    members, own_rows, pieces = sizes
    half = members // 2
    block_refs, (out_ref, table_ref) = refs[: half + 1], refs[half + 1 :]
    block_rows = 4 * pieces * own_rows
    me = lax.axis_index("member")
    table_ref[...] = mix_ref[...].T

    def analyse(m, carry):
        for side in range(2):
            coefs = table_ref[pl.ds(side * members + m, own_rows, stride=2 * members), :]
            columns = [jnp.broadcast_to(coefs[:, d : d + 1], (own_rows, LANES)) for d in range(members)]
            for i in range(4):
                for q in range(side * pieces // 2, (side + 1) * pieces // 2):
                    total = None
                    for d in range(members):
                        start = (i * pieces + q) * own_rows + (d % 2 * block_rows if d >= 2 else 0)
                        block = block_refs[d if d < 2 else d // 2 + 1][start : start + own_rows, :]
                        term = columns[d] * block
                        total = term if total is None else total + term
                    out_ref[me ^ m, i, :, q * LANES : (q + 1) * LANES] = total
        return carry

    if members <= 8:
        for m in range(members):
            analyse(m, 0)
    else:
        lax.fori_loop(0, members, analyse, 0)


def trade(block, distance):
    members = lax.axis_size("member")
    return lax.ppermute(block, "member", [(i, i ^ distance) for i in range(members)])


def trade_blocks(equiv, across, along):
    half = len(along)
    size = along[0].shape[0]
    window = equiv.shape[0]
    passed = trade(across, 1)
    far = trade(equiv, half)
    three = jnp.concatenate([equiv, passed[half * size :], far], axis=0)
    near = [trade(three, 2 * i) for i in range(1, half // 2)]
    last = trade(jnp.concatenate([far] + [x[2 * window :] for x in near], axis=0), 1)
    pairs = [
        trade(jnp.concatenate([along[i], passed[i * size : (i + 1) * size]], axis=0), 2 * i)
        for i in range(1, half)
    ]
    return three, last, near, [along[0], passed, *pairs]


def swaps(near, far):
    count = lax.axis_size("tile")

    def pairs(start):
        twos = [(i, i + 1) for i in range(start, count - 1, 2)]
        return twos + [(b, a) for a, b in twos]

    far = lax.ppermute(far, "tile", pairs(1))
    near = lax.ppermute(near, "tile", pairs(0))
    return near, far


def vmem_specs(count):
    return [pl.BlockSpec(memory_space=pltpu.VMEM)] * count


def body(
    realization_array,
    water_depth,
    wet_mask,
    obs_cell,
    obs_value,
    obs_error,
    celer_gain,
    obs_list,
    obs_count,
):
    members = lax.axis_size("member")
    rows, width = water_depth.shape
    obs_tile = obs_cell.shape[0]
    radius = obs_tile // 8
    halo = radius * CELLS_PER_OBS // width + 2 * STEPS
    per_dev, slots = obs_list.shape[1:]
    own_rows = per_dev * REGION_POINTS // width
    pieces = width // LANES
    state = realization_array[0]
    panel = (obs_tile // LANES, LANES)
    pairs = per_dev * slots // LANES
    edges = pl.pallas_call(
        functools.partial(edge_kernel, halo),
        out_shape=[pltpu.VMEM((6 * halo + 8, width), jnp.float32)] * 2,
        in_specs=[pl.BlockSpec(memory_space=pl.ANY)] * 7,
        out_specs=vmem_specs(2),
        scratch_shapes=[
            pltpu.VMEM((2, halo, width), jnp.int32),
            pltpu.VMEM((2, 8, LANES), jnp.int32),
            pltpu.SemaphoreType.DMA((20,)),
        ],
        name="edges",
    )(
        state,
        water_depth,
        wet_mask,
        obs_cell.reshape(panel),
        celer_gain.reshape(panel),
        obs_value.reshape(panel),
        obs_error.reshape(panel),
    )
    near, far = swaps(*edges)

    window = (obs_tile + 2 * radius) // LANES
    grid = (pieces, rows + 2 * halo + 2 * PAD, LANES)
    half = members // 2
    block_rows = 4 * pieces * own_rows
    equiv, across, *along = pl.pallas_call(
        functools.partial(forecast_kernel, (members, own_rows, halo, radius)),
        out_shape=[
            jax.ShapeDtypeStruct((window, LANES), jnp.float32),
            jax.ShapeDtypeStruct((half * block_rows + window, LANES), jnp.float32),
        ]
        + [jax.ShapeDtypeStruct((block_rows, LANES), jnp.float32)] * half,
        in_specs=vmem_specs(7),
        out_specs=vmem_specs(2 + half),
        scratch_shapes=[pltpu.VMEM(grid, jnp.float32)] * 8 + [pltpu.VMEM((window, LANES), jnp.float32)] * 2,
        compiler_params=pltpu.CompilerParams(vmem_limit_bytes=24 * 2**20),
        name="forecast",
    )(
        state,
        water_depth,
        wet_mask,
        obs_cell.reshape(panel),
        celer_gain.reshape(panel),
        near,
        far,
    )
    three, last, near_equivs, blocks = trade_blocks(equiv, across, along)

    known, spot = pl.pallas_call(
        functools.partial(precision_kernel, (halo, rows, width, radius)),
        out_shape=[pltpu.VMEM((2, pairs, LANES), jnp.float32), pltpu.VMEM((pairs, LANES), jnp.int32)],
        in_specs=vmem_specs(1) + [pl.BlockSpec(memory_space=pltpu.SMEM)] + vmem_specs(4),
        out_specs=vmem_specs(2),
        scratch_shapes=[pltpu.VMEM((window, LANES), jnp.float32)] * 2,
        name="precision",
    )(
        obs_list[0],
        obs_count,
        obs_value.reshape(panel),
        obs_error.reshape(panel),
        near,
        far,
    )
    mix = pl.pallas_call(
        functools.partial(weight_kernel, members),
        out_shape=jax.ShapeDtypeStruct((members, LANES), jnp.float32),
        in_specs=vmem_specs(4 + len(near_equivs)),
        out_specs=vmem_specs(1)[0],
        scratch_shapes=[pltpu.VMEM((members * window, LANES), jnp.float32)],
        compiler_params=pltpu.CompilerParams(vmem_limit_bytes=24 * 2**20),
        name="weights",
    )(three, last, *near_equivs, spot, known)
    analysed = pl.pallas_call(
        functools.partial(mix_kernel, (members, own_rows, pieces)),
        out_shape=jax.ShapeDtypeStruct((members, 4, own_rows, width), jnp.float32),
        in_specs=vmem_specs(2 + half),
        out_specs=vmem_specs(1)[0],
        scratch_shapes=[pltpu.VMEM((LANES, members), jnp.float32)],
        compiler_params=pltpu.CompilerParams(vmem_limit_bytes=24 * 2**20),
        name="mix",
    )(mix, *blocks)
    result = lax.all_to_all(analysed, "member", split_axis=0, concat_axis=0, tiled=True)
    return jnp.transpose(result, (1, 0, 2, 3)).reshape(1, 4, rows, width)


def solution(mesh):
    return jax.shard_map(
        body,
        mesh=mesh,
        in_specs=(
            P("member", None, "tile", None),
            P("tile", None),
            P("tile", None),
            P("tile"),
            P("tile"),
            P("tile"),
            P("tile"),
            P("tile", "member", None),
            P("tile", "member"),
        ),
        out_specs=P("member", None, "tile", None),
        check_vma=False,
    )
```

```python
import functools

import jax
import jax.numpy as jnp
from jax import lax
from jax.experimental import pallas as pl
from jax.experimental.pallas import tpu as pltpu
from jax.sharding import PartitionSpec as P

REGION_POINTS = 256
STEPS = 4
NS_ITERS = 14
CELLS_PER_OBS = 8
LANES = 128

FRICTION = 0.98
PRESSURE = 0.25
DIVERGE = 0.25
FORCING = 0.05
UPWIND = 0.4
DAMPING = 0.02
HIGH = lax.Precision.HIGHEST

PAD = 8
PACKED = 2


def iota(shape, dim):
    return lax.broadcasted_iota(jnp.int32, shape, dim)


def edge_kernel(halo, *refs):
    grids, obs, outs = refs[:3], refs[3:7], refs[7:9]
    wet_ref, cell_ref, sems = refs[9:]
    rows = grids[1].shape[0]
    inner = obs[0].shape[0]
    even = lax.axis_index("tile") % 2 == 0
    copies = []

    def fetch(source, target):
        copies.append(pltpu.make_async_copy(source, target, sems.at[len(copies)]))
        copies[-1].start()

    for side, out in enumerate(outs):
        is_last = even if side == 0 else jnp.logical_not(even)
        start = pl.multiple_of(jnp.where(is_last, rows - halo, 0), 8)
        for i in range(6):
            source = (grids[0].at[i] if i < 4 else grids[i - 3]).at[pl.ds(start, halo), :]
            fetch(source, out.at[pl.ds(i * halo, halo), :] if i < 5 else wet_ref.at[side])
        start = pl.multiple_of(jnp.where(is_last, inner - 8, 0), 8)
        for j in range(4):
            target = out.at[pl.ds(6 * halo, 8), pl.ds(j * LANES, LANES)] if j else cell_ref.at[side]
            fetch(obs[j].at[pl.ds(start, 8), :], target)
    for copy in copies:
        copy.wait()
    for side, out in enumerate(outs):
        out[5 * halo : 6 * halo, :] = wet_ref[side].astype(jnp.float32)
        out[6 * halo : 6 * halo + 8, 0:LANES] = (cell_ref[side] % CELLS_PER_OBS).astype(jnp.float32)


def side_by_side(x, pairs):
    return jnp.concatenate([x[:pairs], x[pairs:]], axis=1)


def window_parts(win, own, near_ref, far_ref, base, j, even):
    inner = own.shape[0]
    span = (win.shape[0] - inner) // 2
    lanes = slice(j * LANES, (j + 1) * LANES)
    near, far = near_ref[base : base + 8, lanes], far_ref[base : base + 8, lanes]
    win[0:span, :] = jnp.where(even, far, near)[8 - span :, :]
    win[span : span + inner, :] = own
    win[span + inner :, :] = jnp.where(even, near, far)[:span, :]


def forecast_kernel(
    sizes,
    state_ref,
    depth_ref,
    mask_ref,
    cell_ref,
    gain_ref,
    near_ref,
    far_ref,
    *refs,
):
    members, own_rows, halo, obs_halo = sizes
    half = members // 2
    out_ref, equiv_ref, across_ref = refs[:3]
    along_refs, scratch = refs[3 : half + 3], refs[half + 3 :]
    s_ref, u_ref, v_ref, e_ref, h_ref, w_ref, flux_ref, part_ref, cell_win, gain_win, pack_ref, sem = scratch
    even = lax.axis_index("tile") % 2 == 0
    rows, width = depth_ref.shape
    pieces = width // LANES
    total = rows + 2 * halo
    first = PAD + halo
    own = pl.ds(first, rows)
    fields = (s_ref, u_ref, v_ref, e_ref, h_ref, w_ref)
    near_at = pl.multiple_of(jnp.where(even, first + rows, PAD), 8)
    far_at = pl.multiple_of(jnp.where(even, PAD, first + rows), 8)
    edge = jnp.zeros((PAD, LANES), jnp.float32)
    for q in range(pieces):
        lanes = slice(q * LANES, (q + 1) * LANES)
        for i, field in enumerate(fields):
            field[q, pl.ds(near_at, halo), :] = near_ref[i * halo : (i + 1) * halo, lanes]
            field[q, pl.ds(far_at, halo), :] = far_ref[i * halo : (i + 1) * halo, lanes]
            if i < 4:
                field[q, own, :] = state_ref[i, :, lanes]
        h_ref[q, own, :] = depth_ref[:, lanes]
        s_ref[q, PAD : PAD + total, :] *= PRESSURE
        h_ref[q, PAD : PAD + total, :] *= PRESSURE * DIVERGE
        w_ref[q, own, :] = mask_ref[:, lanes].astype(jnp.float32)
        for field in (s_ref, e_ref, flux_ref):
            field[q, 0:PAD, :] = edge
            field[q, PAD + total : PAD + total + PAD, :] = edge

    lane = iota((8, LANES), 1)
    at_first, at_last = lane == 0, lane == LANES - 1

    def across(x):
        ahead = [pltpu.roll(piece, LANES - 1, 1) for piece in x] + [0.0]
        behind = [0.0] + [pltpu.roll(piece, 1, 1) for piece in x]
        return [
            jnp.where(at_last, ahead[q + 1], ahead[q]) - jnp.where(at_first, behind[q], behind[q + 1])
            for q in range(pieces)
        ]

    outer = (halo - obs_halo * CELLS_PER_OBS // width) // 8
    for step in range(STEPS):
        skip, skip_energy = (outer, halo // 8) if step == STEPS - 1 else (0, 0)
        for block in range(total // 8):
            r = PAD + 8 * block
            here, below, above = pl.ds(r, 8), pl.ds(r + 1, 8), pl.ds(r - 1, 8)
            inside = skip <= block < total // 8 - skip
            s = [s_ref[q, here, :] for q in range(pieces)]
            slope = across(s) if inside else None
            flux = []
            for q in range(pieces):
                w, h = w_ref[q, here, :], h_ref[q, here, :]
                u = w * (FRICTION * u_ref[q, here, :] - (s_ref[q, below, :] - s_ref[q, above, :]))
                u_ref[q, here, :] = u
                flux_ref[q, here, :] = h * u
                if inside:
                    v = w * (FRICTION * v_ref[q, here, :] - slope[q])
                    v_ref[q, here, :] = v
                    flux.append(h * v)
            if inside:
                rise = across(flux)
                for q in range(pieces):
                    part_ref[q, here, :] = s[q] - rise[q] + (PRESSURE * FORCING) * e_ref[q, here, :]
        for block in reversed(range(skip, total // 8 - skip)):
            r = PAD + 8 * block
            here, below, above = pl.ds(r, 8), pl.ds(r + 1, 8), pl.ds(r - 1, 8)
            for q in range(pieces):
                w = w_ref[q, here, :]
                rise = flux_ref[q, below, :] - flux_ref[q, above, :]
                s_ref[q, here, :] = w * (part_ref[q, here, :] - rise)
                if skip_energy <= block < total // 8 - skip_energy:
                    e = e_ref[q, here, :]
                    e_ref[q, here, :] = w * ((1.0 - UPWIND - DAMPING) * e + UPWIND * e_ref[q, above, :])

    me = lax.axis_index("member")
    for j in range(members):
        source = first + j * own_rows
        for i in range(PACKED):
            for q in range(pieces):
                target = (i * pieces + q) * own_rows
                block = fields[i][q, source : source + own_rows, :]
                pack_ref[j, target : target + own_rows, :] = block if i else block * (1.0 / PRESSURE)
    sent = pltpu.make_async_copy(pack_ref, out_ref, sem)
    sent.start()

    window = cell_win.shape[0]
    base = 6 * halo
    offsets = (cell_ref[...] % CELLS_PER_OBS).astype(jnp.float32)
    window_parts(cell_win, offsets, near_ref, far_ref, base, 0, even)
    window_parts(gain_win, gain_ref[...], near_ref, far_ref, base, 1, even)
    half = width // CELLS_PER_OBS
    top = first - obs_halo // half
    column = iota((LANES, 2 * width), 1)
    cell_at = column // (2 * LANES) * LANES + column % LANES
    parity = column // LANES % 2
    spread = jnp.where(
        iota((LANES, 2 * width), 0) == parity * half + cell_at // CELLS_PER_OBS, 1.0, 0.0
    ).astype(jnp.bfloat16)
    offset = jnp.dot(cell_win[...].astype(jnp.bfloat16), spread, preferred_element_type=jnp.float32)
    level = jnp.concatenate(
        [s_ref[q, pl.ds(top + side, window, stride=2), :] for q in range(pieces) for side in range(2)], axis=1
    )
    place = (iota((window, 2 * width), 1) % CELLS_PER_OBS).astype(jnp.float32)
    rest = jnp.where(jnp.abs(offset - place) < 0.5, level, 0.0)
    equiv = jnp.zeros((window, LANES), jnp.float32)
    parts = []
    for i in range(3):
        parts.append(rest.astype(jnp.bfloat16))
        rest = rest - parts[-1].astype(jnp.float32)
    for part in reversed(parts):
        equiv = equiv + lax.dot_general(
            part, spread, (((1,), (1,)), ((), ())), preferred_element_type=jnp.float32
        )
    equiv = equiv * ((1.0 / PRESSURE) * gain_win[...])
    equiv_ref[...] = equiv
    across_ref[across_ref.shape[0] - window :, :] = equiv

    for j in range(members):
        source = pl.multiple_of(first + (me ^ j) * own_rows, min(own_rows, 8))
        for i in range(PACKED, 4):
            for q in range(pieces):
                target = ((i - PACKED) * pieces + q) * own_rows
                block = fields[i][q, pl.ds(source, own_rows), :]
                if j % 2:
                    target += j // 2 * (4 - PACKED) * pieces * own_rows
                    across_ref[target : target + own_rows, :] = block
                else:
                    along_refs[j // 2][target : target + own_rows, :] = block
    sent.wait()


def group_columns(left, starts, members):
    return [jnp.take_along_axis(left, starts + k, axis=1, mode="promise_in_bounds") for k in range(members)]


def group_matmul(columns, right):
    terms = [column * right[k : k + 1, :] for k, column in enumerate(columns)]
    while len(terms) > 1:
        terms = [a + b for a, b in zip(terms[::2], terms[1::2])]
    return terms[0]


def precision_kernel(
    sizes, list_ref, count_ref, value_ref, error_ref, near_ref, far_ref, out_ref, spot_ref, value_win, error_win
):
    halo, rows, width, radius = sizes
    window = value_win.shape[0]
    per_dev, slots = list_ref.shape
    obs_tile = value_ref.shape[0] * LANES
    even = lax.axis_index("tile") % 2 == 0
    window_parts(value_win, value_ref[...], near_ref, far_ref, 6 * halo, 2, even)
    window_parts(error_win, error_ref[...], near_ref, far_ref, 6 * halo, 3, even)
    named = list_ref[...]
    patch = iota((per_dev, slots), 0)
    row_index = (lax.axis_index("member") * per_dev + patch) * REGION_POINTS // width
    dist = (named - (obs_tile + row_index * obs_tile // rows)).astype(jnp.float32) / radius
    counts = jnp.zeros((per_dev, slots), jnp.int32)
    for p in range(per_dev):
        counts = jnp.where(patch == p, count_ref[0, p], counts)
    live = jnp.where(iota((per_dev, slots), 1) < counts, 1.0, 0.0)
    live = side_by_side(live, per_dev // 2)
    damp = side_by_side(1.0 + 4.0 * dist * dist, per_dev // 2)
    spot = side_by_side(named - (obs_tile - radius), per_dev // 2)
    spot_ref[...] = spot
    row, lane = spot // LANES, spot % LANES
    value = jnp.zeros(spot.shape, jnp.float32)
    error = jnp.zeros(spot.shape, jnp.float32)
    for r in range(window):
        hit = row == r
        line = jnp.broadcast_to(value_win[r : r + 1, :], spot.shape)
        value = jnp.where(hit, jnp.take_along_axis(line, lane, axis=1, mode="promise_in_bounds"), value)
        line = jnp.broadcast_to(error_win[r : r + 1, :], spot.shape)
        error = jnp.where(hit, jnp.take_along_axis(line, lane, axis=1, mode="promise_in_bounds"), error)
    out_ref[0] = value
    out_ref[1] = jnp.where(live > 0.0, 1.0 / (damp * error), 0.0)


def weight_kernel(members, three_ref, last_ref, *refs):
    half = members // 2
    near_refs, (spot_ref, known_ref, mix_ref, equiv_win) = refs[: half // 2 - 1], refs[half // 2 - 1 :]
    window = equiv_win.shape[0] // (members + 1)
    for i, ref in enumerate((three_ref, *near_refs)):
        for j, place in enumerate((2 * i, 2 * i + 1, 2 * i + half)):
            equiv_win[place * window : (place + 1) * window, :] = ref[j * window : (j + 1) * window, :]
        place = 2 * i + half + 1
        equiv_win[place * window : (place + 1) * window, :] = last_ref[i * window : (i + 1) * window, :]
    value, precision = known_ref[0], known_ref[1]

    spot = spot_ref[...]
    pairs = spot.shape[0]
    row, lane = spot // LANES, spot % LANES
    rows_of = [jnp.broadcast_to(row[i : i + 1, :], (members, LANES)) for i in range(pairs)]
    lanes_of = [jnp.broadcast_to(lane[i : i + 1, :], (members, LANES)) for i in range(pairs)]
    picked = [jnp.zeros((members, LANES), jnp.float32) for i in range(pairs)]
    for r in range(window):
        source = equiv_win[pl.ds(r, members, stride=window), :]
        for i in range(pairs):
            got = jnp.take_along_axis(source, lanes_of[i], axis=1, mode="promise_in_bounds")
            picked[i] = jnp.where(rows_of[i] == r, got, picked[i])

    left_half = iota((members, LANES), 1) < LANES // 2
    weighted, spreads, innovations = [], [], []
    for i in range(pairs):
        mean = jnp.sum(picked[i], axis=0, keepdims=True) * (1.0 / members)
        spread = picked[i] - mean
        scaled = spread * precision[i : i + 1, :]
        innovation = jnp.broadcast_to(value[i : i + 1, :] - mean, (members, LANES))
        weighted.append(scaled)
        spreads.append(spread)
        innovations.append(innovation)
    every = lax.dot_general(
        jnp.concatenate(
            [jnp.where(left_half, x, 0.0) for x in weighted] + [jnp.where(left_half, 0.0, x) for x in weighted],
            axis=0,
        ),
        jnp.concatenate(spreads + spreads + innovations + innovations, axis=0),
        (((1,), (1,)), ((), ())),
        preferred_element_type=jnp.float32,
        precision=HIGH,
    )
    lane_at = iota((members, LANES), 1)
    patch_at = lane_at // members
    gram = jnp.zeros((members, LANES), jnp.float32)
    proj = jnp.zeros((members, LANES), jnp.float32)
    for p in range(2 * pairs):
        mine = patch_at == p
        block = every[p * members : (p + 1) * members, :]
        gram = jnp.where(mine, block[:, :LANES], gram)
        proj = jnp.where(mine, block[:, LANES:], proj)

    starts = lane_at - lane_at % members
    eye = (lane_at % members == iota((members, LANES), 0)).astype(jnp.float32)
    amat = gram + (members - 1.0) * eye
    diagonal = jnp.broadcast_to(jnp.sum(amat * eye, axis=0, keepdims=True), (members, LANES))
    trace = functools.reduce(jnp.add, group_columns(diagonal, starts, members))

    def iterate(sweep, carry):
        product, inverse = carry
        columns = group_columns(product, starts, members)
        square = group_matmul(columns, product)
        cube = group_matmul(columns, square)
        return (
            2.25 * product - 1.5 * square + 0.25 * cube,
            1.5 * inverse - 0.5 * group_matmul(columns, inverse),
        )

    product, inverse = lax.fori_loop(0, NS_ITERS, iterate, (amat / trace, eye), unroll=members <= 8)
    root = inverse / jnp.sqrt(trace)
    columns = group_columns(root, starts, members)
    wbar = group_matmul(columns, group_matmul(columns, proj))
    wtot = ((members - 1.0) ** 0.5) * root + wbar
    mix = wtot - jnp.sum(wtot, axis=0, keepdims=True) * (1.0 / members) + 1.0 / members
    mix_ref[...] = mix


def mix_kernel(sizes, recv_ref, mix_ref, *refs):
    members, own_rows, pieces = sizes
    half = members // 2
    rest_refs, (out_ref, table_ref) = refs[: half + 1], refs[half + 1 :]
    rest_rows = (4 - PACKED) * pieces * own_rows
    stride = recv_ref.shape[0] // members
    me = lax.axis_index("member")
    table_ref[0:LANES, :] = mix_ref[...].T
    bases = [pl.multiple_of((me ^ d) * stride, 8) for d in range(members)]

    def analyse(m, carry):
        for side in range(2):
            coefs = table_ref[pl.ds(side * members + m, own_rows, stride=2 * members), :]
            columns = [jnp.broadcast_to(coefs[:, d : d + 1], (own_rows, LANES)) for d in range(members)]
            for i in range(4):
                for q in range(side * pieces // 2, (side + 1) * pieces // 2):
                    total = None
                    for d in range(members):
                        if i < PACKED:
                            start = (i * pieces + q) * own_rows
                            block = recv_ref[pl.ds(bases[d] + start, own_rows), :]
                        else:
                            start = ((i - PACKED) * pieces + q) * own_rows
                            if d >= 2:
                                start += d % 2 * rest_rows
                            block = rest_refs[d if d < 2 else d // 2 + 1][start : start + own_rows, :]
                        term = columns[d] * block
                        total = term if total is None else total + term
                    out_ref[me ^ m, i, :, q * LANES : (q + 1) * LANES] = total
        return carry

    if members <= 8:
        for m in range(members):
            analyse(m, 0)
    else:
        lax.fori_loop(0, members, analyse, 0)


def trade(block, distance):
    members = lax.axis_size("member")
    return lax.ppermute(block, "member", [(i, i ^ distance) for i in range(members)])


def trade_blocks(equiv, across, along):
    half = len(along)
    size = along[0].shape[0]
    window = equiv.shape[0]
    passed = trade(across, 1)
    far = trade(equiv, half)
    three = jnp.concatenate([equiv, passed[half * size :], far], axis=0)
    near = [trade(three, 2 * i) for i in range(1, half // 2)]
    last = trade(jnp.concatenate([far] + [x[2 * window :] for x in near], axis=0), 1)
    pairs = [
        trade(jnp.concatenate([along[i], passed[i * size : (i + 1) * size]], axis=0), 2 * i)
        for i in range(1, half)
    ]
    return three, last, near, [along[0], passed, *pairs]


def swaps(near, far):
    count = lax.axis_size("tile")

    def pairs(start):
        twos = [(i, i + 1) for i in range(start, count - 1, 2)]
        return twos + [(b, a) for a, b in twos]

    far = lax.ppermute(far, "tile", pairs(1))
    near = lax.ppermute(near, "tile", pairs(0))
    return near, far


def vmem_specs(count):
    return [pl.BlockSpec(memory_space=pltpu.VMEM)] * count


def body(
    realization_array,
    water_depth,
    wet_mask,
    obs_cell,
    obs_value,
    obs_error,
    celer_gain,
    obs_list,
    obs_count,
):
    members = lax.axis_size("member")
    rows, width = water_depth.shape
    obs_tile = obs_cell.shape[0]
    radius = obs_tile // 8
    halo = radius * CELLS_PER_OBS // width + 2 * STEPS
    per_dev, slots = obs_list.shape[1:]
    own_rows = per_dev * REGION_POINTS // width
    pieces = width // LANES
    state = realization_array[0]
    panel = (obs_tile // LANES, LANES)
    pairs = per_dev * slots // LANES
    edges = pl.pallas_call(
        functools.partial(edge_kernel, halo),
        out_shape=[pltpu.VMEM((6 * halo + 8, width), jnp.float32)] * 2,
        in_specs=[pl.BlockSpec(memory_space=pl.ANY)] * 7,
        out_specs=vmem_specs(2),
        scratch_shapes=[
            pltpu.VMEM((2, halo, width), jnp.int32),
            pltpu.VMEM((2, 8, LANES), jnp.int32),
            pltpu.SemaphoreType.DMA((20,)),
        ],
        name="edges",
    )(
        state,
        water_depth,
        wet_mask,
        obs_cell.reshape(panel),
        celer_gain.reshape(panel),
        obs_value.reshape(panel),
        obs_error.reshape(panel),
    )
    near, far = swaps(*edges)

    window = (obs_tile + 2 * radius) // LANES
    packet = PACKED * pieces * own_rows
    grid = (pieces, rows + 2 * halo + 2 * PAD, LANES)
    half = members // 2
    rest_rows = (4 - PACKED) * pieces * own_rows
    sends, equiv, across, *along = pl.pallas_call(
        functools.partial(forecast_kernel, (members, own_rows, halo, radius)),
        out_shape=[
            jax.ShapeDtypeStruct((members, packet, LANES), jnp.float32),
            jax.ShapeDtypeStruct((window, LANES), jnp.float32),
            jax.ShapeDtypeStruct((half * rest_rows + window, LANES), jnp.float32),
        ]
        + [jax.ShapeDtypeStruct((rest_rows, LANES), jnp.float32)] * half,
        in_specs=vmem_specs(7),
        out_specs=[pl.BlockSpec(memory_space=pl.ANY)] + vmem_specs(2 + half),
        scratch_shapes=[pltpu.VMEM(grid, jnp.float32)] * 8
        + [pltpu.VMEM((window, LANES), jnp.float32)] * 2
        + [pltpu.VMEM((members, packet, LANES), jnp.float32), pltpu.SemaphoreType.DMA],
        compiler_params=pltpu.CompilerParams(vmem_limit_bytes=24 * 2**20),
        name="forecast",
    )(
        state,
        water_depth,
        wet_mask,
        obs_cell.reshape(panel),
        celer_gain.reshape(panel),
        near,
        far,
    )
    received = lax.all_to_all(sends, "member", split_axis=0, concat_axis=0, tiled=True)
    three, last, near_equivs, rest = trade_blocks(equiv, across, along)
    received = received.reshape(members * packet, LANES)

    known, spot = pl.pallas_call(
        functools.partial(precision_kernel, (halo, rows, width, radius)),
        out_shape=[pltpu.VMEM((2, pairs, LANES), jnp.float32), pltpu.VMEM((pairs, LANES), jnp.int32)],
        in_specs=vmem_specs(1) + [pl.BlockSpec(memory_space=pltpu.SMEM)] + vmem_specs(4),
        out_specs=vmem_specs(2),
        scratch_shapes=[pltpu.VMEM((window, LANES), jnp.float32)] * 2,
        name="precision",
    )(
        obs_list[0],
        obs_count,
        obs_value.reshape(panel),
        obs_error.reshape(panel),
        near,
        far,
    )
    mix = pl.pallas_call(
        functools.partial(weight_kernel, members),
        out_shape=jax.ShapeDtypeStruct((members, LANES), jnp.float32),
        in_specs=vmem_specs(4 + len(near_equivs)),
        out_specs=vmem_specs(1)[0],
        scratch_shapes=[pltpu.VMEM(((members + 1) * window, LANES), jnp.float32)],
        compiler_params=pltpu.CompilerParams(vmem_limit_bytes=24 * 2**20),
        name="weights",
    )(three, last, *near_equivs, spot, known)
    analysed = pl.pallas_call(
        functools.partial(mix_kernel, (members, own_rows, pieces)),
        out_shape=jax.ShapeDtypeStruct((members, 4, own_rows, width), jnp.float32),
        in_specs=vmem_specs(3 + half),
        out_specs=vmem_specs(1)[0],
        scratch_shapes=[pltpu.VMEM((LANES + 2 * members, members), jnp.float32)],
        compiler_params=pltpu.CompilerParams(vmem_limit_bytes=24 * 2**20),
        name="mix",
    )(received, mix, *rest)
    result = lax.all_to_all(analysed, "member", split_axis=0, concat_axis=0, tiled=True)
    return jnp.transpose(result, (1, 0, 2, 3)).reshape(1, 4, rows, width)


def solution(mesh):
    return jax.shard_map(
        body,
        mesh=mesh,
        in_specs=(
            P("member", None, "tile", None),
            P("tile", None),
            P("tile", None),
            P("tile"),
            P("tile"),
            P("tile"),
            P("tile"),
            P("tile", "member", None),
            P("tile", "member"),
        ),
        out_specs=P("member", None, "tile", None),
        check_vma=False,
    )
```

```python
import functools

import jax
import jax.numpy as jnp
from jax import lax
from jax.experimental import pallas as pl
from jax.experimental.pallas import tpu as pltpu
from jax.sharding import PartitionSpec as P

REGION_POINTS = 256
STEPS = 4
NS_ITERS = 14
CELLS_PER_OBS = 8
LANES = 128

FRICTION = 0.98
PRESSURE = 0.25
DIVERGE = 0.25
FORCING = 0.05
UPWIND = 0.4
DAMPING = 0.02
HIGH = lax.Precision.HIGHEST

PAD = 8
PACKED = 2


def iota(shape, dim):
    return lax.broadcasted_iota(jnp.int32, shape, dim)


def edge_kernel(halo, *refs):
    grids, obs, outs = refs[:3], refs[3:7], refs[7:9]
    wet_ref, cell_ref, sems = refs[9:]
    rows = grids[1].shape[0]
    inner = obs[0].shape[0]
    even = lax.axis_index("tile") % 2 == 0
    copies = []

    def fetch(source, target):
        copies.append(pltpu.make_async_copy(source, target, sems.at[len(copies)]))
        copies[-1].start()

    for side, out in enumerate(outs):
        is_last = even if side == 0 else jnp.logical_not(even)
        start = pl.multiple_of(jnp.where(is_last, rows - halo, 0), 8)
        for i in range(6):
            source = (grids[0].at[i] if i < 4 else grids[i - 3]).at[pl.ds(start, halo), :]
            fetch(source, out.at[pl.ds(i * halo, halo), :] if i < 5 else wet_ref.at[side])
        start = pl.multiple_of(jnp.where(is_last, inner - 8, 0), 8)
        for j in range(4):
            target = out.at[pl.ds(6 * halo, 8), pl.ds(j * LANES, LANES)] if j else cell_ref.at[side]
            fetch(obs[j].at[pl.ds(start, 8), :], target)
    for copy in copies:
        copy.wait()
    for side, out in enumerate(outs):
        out[5 * halo : 6 * halo, :] = wet_ref[side].astype(jnp.float32)
        out[6 * halo : 6 * halo + 8, 0:LANES] = (cell_ref[side] % CELLS_PER_OBS).astype(jnp.float32)


def side_by_side(x, pairs):
    return jnp.concatenate([x[:pairs], x[pairs:]], axis=1)


def window_parts(win, own, near_ref, far_ref, base, j, even):
    inner = own.shape[0]
    span = (win.shape[0] - inner) // 2
    lanes = slice(j * LANES, (j + 1) * LANES)
    near, far = near_ref[base : base + 8, lanes], far_ref[base : base + 8, lanes]
    win[0:span, :] = jnp.where(even, far, near)[8 - span :, :]
    win[span : span + inner, :] = own
    win[span + inner :, :] = jnp.where(even, near, far)[:span, :]


def forecast_kernel(
    sizes,
    state_ref,
    depth_ref,
    mask_ref,
    cell_ref,
    gain_ref,
    near_ref,
    far_ref,
    *refs,
):
    members, own_rows, halo, obs_halo = sizes
    half = members // 2
    out_ref, equiv_ref, across_ref = refs[:3]
    along_refs, scratch = refs[3 : half + 3], refs[half + 3 :]
    s_ref, u_ref, v_ref, e_ref, h_ref, w_ref, flux_ref, part_ref, cell_win, gain_win, pack_ref, sem = scratch
    even = lax.axis_index("tile") % 2 == 0
    rows, width = depth_ref.shape
    pieces = width // LANES
    total = rows + 2 * halo
    first = PAD + halo
    own = pl.ds(first, rows)
    fields = (s_ref, u_ref, v_ref, e_ref, h_ref, w_ref)
    near_at = pl.multiple_of(jnp.where(even, first + rows, PAD), 8)
    far_at = pl.multiple_of(jnp.where(even, PAD, first + rows), 8)
    edge = jnp.zeros((PAD, LANES), jnp.float32)
    for q in range(pieces):
        lanes = slice(q * LANES, (q + 1) * LANES)
        for i, field in enumerate(fields):
            field[q, pl.ds(near_at, halo), :] = near_ref[i * halo : (i + 1) * halo, lanes]
            field[q, pl.ds(far_at, halo), :] = far_ref[i * halo : (i + 1) * halo, lanes]
            if i < 4:
                field[q, own, :] = state_ref[i, :, lanes]
        h_ref[q, own, :] = depth_ref[:, lanes]
        s_ref[q, PAD : PAD + total, :] *= PRESSURE
        h_ref[q, PAD : PAD + total, :] *= PRESSURE * DIVERGE
        w_ref[q, own, :] = mask_ref[:, lanes].astype(jnp.float32)
        for field in (s_ref, e_ref, flux_ref):
            field[q, 0:PAD, :] = edge
            field[q, PAD + total : PAD + total + PAD, :] = edge

    lane = iota((8, LANES), 1)
    at_first, at_last = lane == 0, lane == LANES - 1

    def across(x):
        ahead = [pltpu.roll(piece, LANES - 1, 1) for piece in x] + [0.0]
        behind = [0.0] + [pltpu.roll(piece, 1, 1) for piece in x]
        return [
            jnp.where(at_last, ahead[q + 1], ahead[q]) - jnp.where(at_first, behind[q], behind[q + 1])
            for q in range(pieces)
        ]

    outer = (halo - obs_halo * CELLS_PER_OBS // width) // 8
    for step in range(STEPS):
        skip, skip_energy = (outer, halo // 8) if step == STEPS - 1 else (0, 0)
        for block in range(total // 8):
            r = PAD + 8 * block
            here, below, above = pl.ds(r, 8), pl.ds(r + 1, 8), pl.ds(r - 1, 8)
            inside = skip <= block < total // 8 - skip
            s = [s_ref[q, here, :] for q in range(pieces)]
            slope = across(s) if inside else None
            flux = []
            for q in range(pieces):
                w, h = w_ref[q, here, :], h_ref[q, here, :]
                u = w * (FRICTION * u_ref[q, here, :] - (s_ref[q, below, :] - s_ref[q, above, :]))
                u_ref[q, here, :] = u
                flux_ref[q, here, :] = h * u
                if inside:
                    v = w * (FRICTION * v_ref[q, here, :] - slope[q])
                    v_ref[q, here, :] = v
                    flux.append(h * v)
            if inside:
                rise = across(flux)
                for q in range(pieces):
                    part_ref[q, here, :] = s[q] - rise[q] + (PRESSURE * FORCING) * e_ref[q, here, :]
        for block in reversed(range(skip, total // 8 - skip)):
            r = PAD + 8 * block
            here, below, above = pl.ds(r, 8), pl.ds(r + 1, 8), pl.ds(r - 1, 8)
            for q in range(pieces):
                w = w_ref[q, here, :]
                rise = flux_ref[q, below, :] - flux_ref[q, above, :]
                s_ref[q, here, :] = w * (part_ref[q, here, :] - rise)
                if skip_energy <= block < total // 8 - skip_energy:
                    e = e_ref[q, here, :]
                    e_ref[q, here, :] = w * ((1.0 - UPWIND - DAMPING) * e + UPWIND * e_ref[q, above, :])

    me = lax.axis_index("member")
    for j in range(members):
        source = first + j * own_rows
        for i in range(PACKED):
            for q in range(pieces):
                target = (i * pieces + q) * own_rows
                block = fields[i][q, source : source + own_rows, :]
                pack_ref[j, target : target + own_rows, :] = block if i else block * (1.0 / PRESSURE)
    sent = pltpu.make_async_copy(pack_ref, out_ref, sem)
    sent.start()

    window = cell_win.shape[0]
    base = 6 * halo
    offsets = (cell_ref[...] % CELLS_PER_OBS).astype(jnp.float32)
    window_parts(cell_win, offsets, near_ref, far_ref, base, 0, even)
    window_parts(gain_win, gain_ref[...], near_ref, far_ref, base, 1, even)
    half = width // CELLS_PER_OBS
    top = first - obs_halo // half
    column = iota((LANES, 2 * width), 1)
    cell_at = column // (2 * LANES) * LANES + column % LANES
    parity = column // LANES % 2
    spread = jnp.where(
        iota((LANES, 2 * width), 0) == parity * half + cell_at // CELLS_PER_OBS, 1.0, 0.0
    ).astype(jnp.bfloat16)
    offset = jnp.dot(cell_win[...].astype(jnp.bfloat16), spread, preferred_element_type=jnp.float32)
    level = jnp.concatenate(
        [s_ref[q, pl.ds(top + side, window, stride=2), :] for q in range(pieces) for side in range(2)], axis=1
    )
    place = (iota((window, 2 * width), 1) % CELLS_PER_OBS).astype(jnp.float32)
    rest = jnp.where(jnp.abs(offset - place) < 0.5, level, 0.0)
    equiv = jnp.zeros((window, LANES), jnp.float32)
    parts = []
    for i in range(3):
        parts.append(rest.astype(jnp.bfloat16))
        rest = rest - parts[-1].astype(jnp.float32)
    for part in reversed(parts):
        equiv = equiv + lax.dot_general(
            part, spread, (((1,), (1,)), ((), ())), preferred_element_type=jnp.float32
        )
    equiv = equiv * ((1.0 / PRESSURE) * gain_win[...])
    equiv_ref[...] = equiv
    across_ref[across_ref.shape[0] - window :, :] = equiv

    for j in range(members):
        source = pl.multiple_of(first + (me ^ j) * own_rows, min(own_rows, 8))
        for i in range(PACKED, 4):
            for q in range(pieces):
                target = ((i - PACKED) * pieces + q) * own_rows
                block = fields[i][q, pl.ds(source, own_rows), :]
                if j % 2:
                    target += j // 2 * (4 - PACKED) * pieces * own_rows
                    across_ref[target : target + own_rows, :] = block
                else:
                    along_refs[j // 2][target : target + own_rows, :] = block
    sent.wait()


def group_columns(left, starts, members):
    return [jnp.take_along_axis(left, starts + k, axis=1, mode="promise_in_bounds") for k in range(members)]


def group_matmul(columns, right):
    terms = [column * right[k : k + 1, :] for k, column in enumerate(columns)]
    while len(terms) > 1:
        terms = [a + b for a, b in zip(terms[::2], terms[1::2])]
    return terms[0]


def precision_kernel(
    sizes, list_ref, count_ref, value_ref, error_ref, near_ref, far_ref, out_ref, spot_ref, value_win, error_win
):
    halo, rows, width, radius = sizes
    window = value_win.shape[0]
    per_dev, slots = list_ref.shape
    obs_tile = value_ref.shape[0] * LANES
    even = lax.axis_index("tile") % 2 == 0
    window_parts(value_win, value_ref[...], near_ref, far_ref, 6 * halo, 2, even)
    window_parts(error_win, error_ref[...], near_ref, far_ref, 6 * halo, 3, even)
    named = list_ref[...]
    patch = iota((per_dev, slots), 0)
    row_index = (lax.axis_index("member") * per_dev + patch) * REGION_POINTS // width
    dist = (named - (obs_tile + row_index * obs_tile // rows)).astype(jnp.float32) / radius
    counts = jnp.zeros((per_dev, slots), jnp.int32)
    for p in range(per_dev):
        counts = jnp.where(patch == p, count_ref[0, p], counts)
    live = jnp.where(iota((per_dev, slots), 1) < counts, 1.0, 0.0)
    live = side_by_side(live, per_dev // 2)
    damp = side_by_side(1.0 + 4.0 * dist * dist, per_dev // 2)
    spot = side_by_side(named - (obs_tile - radius), per_dev // 2)
    spot_ref[...] = spot
    row, lane = spot // LANES, spot % LANES
    value = jnp.zeros(spot.shape, jnp.float32)
    error = jnp.zeros(spot.shape, jnp.float32)
    for r in range(window):
        hit = row == r
        line = jnp.broadcast_to(value_win[r : r + 1, :], spot.shape)
        value = jnp.where(hit, jnp.take_along_axis(line, lane, axis=1, mode="promise_in_bounds"), value)
        line = jnp.broadcast_to(error_win[r : r + 1, :], spot.shape)
        error = jnp.where(hit, jnp.take_along_axis(line, lane, axis=1, mode="promise_in_bounds"), error)
    out_ref[0] = value
    out_ref[1] = jnp.where(live > 0.0, 1.0 / (damp * error), 0.0)


def weight_kernel(members, three_ref, last_ref, *refs):
    half = members // 2
    near_refs, (spot_ref, known_ref, mix_ref, equiv_win) = refs[: half // 2 - 1], refs[half // 2 - 1 :]
    window = equiv_win.shape[0] // (members + 1)
    for i, ref in enumerate((three_ref, *near_refs)):
        for j, place in enumerate((2 * i, 2 * i + 1, 2 * i + half)):
            equiv_win[place * window : (place + 1) * window, :] = ref[j * window : (j + 1) * window, :]
        place = 2 * i + half + 1
        equiv_win[place * window : (place + 1) * window, :] = last_ref[i * window : (i + 1) * window, :]
    value, precision = known_ref[0], known_ref[1]

    spot = spot_ref[...]
    pairs = spot.shape[0]
    row, lane = spot // LANES, spot % LANES
    rows_of = [jnp.broadcast_to(row[i : i + 1, :], (members, LANES)) for i in range(pairs)]
    lanes_of = [jnp.broadcast_to(lane[i : i + 1, :], (members, LANES)) for i in range(pairs)]
    picked = [jnp.zeros((members, LANES), jnp.float32) for i in range(pairs)]
    for r in range(window):
        source = equiv_win[pl.ds(r, members, stride=window), :]
        for i in range(pairs):
            got = jnp.take_along_axis(source, lanes_of[i], axis=1, mode="promise_in_bounds")
            picked[i] = jnp.where(rows_of[i] == r, got, picked[i])

    left_half = iota((members, LANES), 1) < LANES // 2
    weighted, spreads, innovations = [], [], []
    for i in range(pairs):
        mean = jnp.sum(picked[i], axis=0, keepdims=True) * (1.0 / members)
        spread = picked[i] - mean
        scaled = spread * precision[i : i + 1, :]
        innovation = jnp.broadcast_to(value[i : i + 1, :] - mean, (members, LANES))
        weighted.append(scaled)
        spreads.append(spread)
        innovations.append(innovation)
    every = lax.dot_general(
        jnp.concatenate(
            [jnp.where(left_half, x, 0.0) for x in weighted] + [jnp.where(left_half, 0.0, x) for x in weighted],
            axis=0,
        ),
        jnp.concatenate(spreads + spreads + innovations + innovations, axis=0),
        (((1,), (1,)), ((), ())),
        preferred_element_type=jnp.float32,
        precision=HIGH,
    )
    lane_at = iota((members, LANES), 1)
    patch_at = lane_at // members
    gram = jnp.zeros((members, LANES), jnp.float32)
    proj = jnp.zeros((members, LANES), jnp.float32)
    for p in range(2 * pairs):
        mine = patch_at == p
        block = every[p * members : (p + 1) * members, :]
        gram = jnp.where(mine, block[:, :LANES], gram)
        proj = jnp.where(mine, block[:, LANES:], proj)

    starts = lane_at - lane_at % members
    eye = (lane_at % members == iota((members, LANES), 0)).astype(jnp.float32)
    amat = gram + (members - 1.0) * eye
    diagonal = jnp.broadcast_to(jnp.sum(amat * eye, axis=0, keepdims=True), (members, LANES))
    trace = functools.reduce(jnp.add, group_columns(diagonal, starts, members))

    def iterate(sweep, carry):
        product, inverse = carry
        columns = group_columns(product, starts, members)
        square = group_matmul(columns, product)
        cube = group_matmul(columns, square)
        return (
            2.25 * product - 1.5 * square + 0.25 * cube,
            1.5 * inverse - 0.5 * group_matmul(columns, inverse),
        )

    product, inverse = lax.fori_loop(0, NS_ITERS, iterate, (amat / trace, eye), unroll=members <= 8)
    root = inverse / jnp.sqrt(trace)
    columns = group_columns(root, starts, members)
    wbar = group_matmul(columns, group_matmul(columns, proj))
    wtot = ((members - 1.0) ** 0.5) * root + wbar
    mix = wtot - jnp.sum(wtot, axis=0, keepdims=True) * (1.0 / members) + 1.0 / members
    mix_ref[...] = mix


def mix_kernel(sizes, recv_ref, mix_ref, *refs):
    members, own_rows, pieces = sizes
    half = members // 2
    rest_refs, (out_ref, table_ref) = refs[: half + 1], refs[half + 1 :]
    rest_rows = (4 - PACKED) * pieces * own_rows
    stride = recv_ref.shape[0] // members
    me = lax.axis_index("member")
    table_ref[0:LANES, :] = mix_ref[...].T
    bases = [pl.multiple_of((me ^ d) * stride, 8) for d in range(members)]

    def analyse(m, carry):
        for side in range(2):
            coefs = table_ref[pl.ds(side * members + m, own_rows, stride=2 * members), :]
            columns = [jnp.broadcast_to(coefs[:, d : d + 1], (own_rows, LANES)) for d in range(members)]
            for i in range(4):
                for q in range(side * pieces // 2, (side + 1) * pieces // 2):
                    total = None
                    for d in range(members):
                        if i < PACKED:
                            start = (i * pieces + q) * own_rows
                            block = recv_ref[pl.ds(bases[d] + start, own_rows), :]
                        else:
                            start = ((i - PACKED) * pieces + q) * own_rows
                            if d >= 2:
                                start += d % 2 * rest_rows
                            block = rest_refs[d if d < 2 else d // 2 + 1][start : start + own_rows, :]
                        term = columns[d] * block
                        total = term if total is None else total + term
                    out_ref[me ^ m, i, :, q * LANES : (q + 1) * LANES] = total
        return carry

    if members <= 8:
        for m in range(members):
            analyse(m, 0)
    else:
        lax.fori_loop(0, members, analyse, 0)


def trade(block, distance):
    members = lax.axis_size("member")
    return lax.ppermute(block, "member", [(i, i ^ distance) for i in range(members)])


def trade_blocks(equiv, across, along):
    half = len(along)
    size = along[0].shape[0]
    window = equiv.shape[0]
    passed = trade(across, 1)
    far = trade(equiv, half)
    three = jnp.concatenate([equiv, passed[half * size :], far], axis=0)
    near = [trade(three, 2 * i) for i in range(1, half // 2)]
    pairs = [jnp.concatenate([along[i], passed[i * size : (i + 1) * size]], axis=0) for i in range(1, half)]
    pairs[0], near[0] = lax.optimization_barrier((pairs[0], near[0]))
    last = trade(jnp.concatenate([far] + [x[2 * window :] for x in near], axis=0), 1)
    pairs = [trade(pair, 2 * i) for i, pair in enumerate(pairs, 1)]
    return three, last, near, [along[0], passed, *pairs]


def swaps(near, far):
    count = lax.axis_size("tile")

    def pairs(start):
        twos = [(i, i + 1) for i in range(start, count - 1, 2)]
        return twos + [(b, a) for a, b in twos]

    far = lax.ppermute(far, "tile", pairs(1))
    near = lax.ppermute(near, "tile", pairs(0))
    return near, far


def vmem_specs(count):
    return [pl.BlockSpec(memory_space=pltpu.VMEM)] * count


def body(
    realization_array,
    water_depth,
    wet_mask,
    obs_cell,
    obs_value,
    obs_error,
    celer_gain,
    obs_list,
    obs_count,
):
    members = lax.axis_size("member")
    rows, width = water_depth.shape
    obs_tile = obs_cell.shape[0]
    radius = obs_tile // 8
    halo = radius * CELLS_PER_OBS // width + 2 * STEPS
    per_dev, slots = obs_list.shape[1:]
    own_rows = per_dev * REGION_POINTS // width
    pieces = width // LANES
    state = realization_array[0]
    panel = (obs_tile // LANES, LANES)
    pairs = per_dev * slots // LANES
    edges = pl.pallas_call(
        functools.partial(edge_kernel, halo),
        out_shape=[pltpu.VMEM((6 * halo + 8, width), jnp.float32)] * 2,
        in_specs=[pl.BlockSpec(memory_space=pl.ANY)] * 7,
        out_specs=vmem_specs(2),
        scratch_shapes=[
            pltpu.VMEM((2, halo, width), jnp.int32),
            pltpu.VMEM((2, 8, LANES), jnp.int32),
            pltpu.SemaphoreType.DMA((20,)),
        ],
        name="edges",
    )(
        state,
        water_depth,
        wet_mask,
        obs_cell.reshape(panel),
        celer_gain.reshape(panel),
        obs_value.reshape(panel),
        obs_error.reshape(panel),
    )
    near, far = swaps(*edges)

    window = (obs_tile + 2 * radius) // LANES
    packet = PACKED * pieces * own_rows
    grid = (pieces, rows + 2 * halo + 2 * PAD, LANES)
    half = members // 2
    rest_rows = (4 - PACKED) * pieces * own_rows
    sends, equiv, across, *along = pl.pallas_call(
        functools.partial(forecast_kernel, (members, own_rows, halo, radius)),
        out_shape=[
            jax.ShapeDtypeStruct((members, packet, LANES), jnp.float32),
            jax.ShapeDtypeStruct((window, LANES), jnp.float32),
            jax.ShapeDtypeStruct((half * rest_rows + window, LANES), jnp.float32),
        ]
        + [jax.ShapeDtypeStruct((rest_rows, LANES), jnp.float32)] * half,
        in_specs=vmem_specs(7),
        out_specs=[pl.BlockSpec(memory_space=pl.ANY)] + vmem_specs(2 + half),
        scratch_shapes=[pltpu.VMEM(grid, jnp.float32)] * 8
        + [pltpu.VMEM((window, LANES), jnp.float32)] * 2
        + [pltpu.VMEM((members, packet, LANES), jnp.float32), pltpu.SemaphoreType.DMA],
        compiler_params=pltpu.CompilerParams(vmem_limit_bytes=24 * 2**20),
        name="forecast",
    )(
        state,
        water_depth,
        wet_mask,
        obs_cell.reshape(panel),
        celer_gain.reshape(panel),
        near,
        far,
    )
    received = lax.all_to_all(sends, "member", split_axis=0, concat_axis=0, tiled=True)
    three, last, near_equivs, rest = trade_blocks(equiv, across, along)
    received = received.reshape(members * packet, LANES)

    known, spot = pl.pallas_call(
        functools.partial(precision_kernel, (halo, rows, width, radius)),
        out_shape=[pltpu.VMEM((2, pairs, LANES), jnp.float32), pltpu.VMEM((pairs, LANES), jnp.int32)],
        in_specs=vmem_specs(1) + [pl.BlockSpec(memory_space=pltpu.SMEM)] + vmem_specs(4),
        out_specs=vmem_specs(2),
        scratch_shapes=[pltpu.VMEM((window, LANES), jnp.float32)] * 2,
        name="precision",
    )(
        obs_list[0],
        obs_count,
        obs_value.reshape(panel),
        obs_error.reshape(panel),
        near,
        far,
    )
    mix = pl.pallas_call(
        functools.partial(weight_kernel, members),
        out_shape=jax.ShapeDtypeStruct((members, LANES), jnp.float32),
        in_specs=vmem_specs(4 + len(near_equivs)),
        out_specs=vmem_specs(1)[0],
        scratch_shapes=[pltpu.VMEM(((members + 1) * window, LANES), jnp.float32)],
        compiler_params=pltpu.CompilerParams(vmem_limit_bytes=24 * 2**20),
        name="weights",
    )(three, last, *near_equivs, spot, known)
    analysed = pl.pallas_call(
        functools.partial(mix_kernel, (members, own_rows, pieces)),
        out_shape=jax.ShapeDtypeStruct((members, 4, own_rows, width), jnp.float32),
        in_specs=vmem_specs(3 + half),
        out_specs=vmem_specs(1)[0],
        scratch_shapes=[pltpu.VMEM((LANES + 2 * members, members), jnp.float32)],
        compiler_params=pltpu.CompilerParams(vmem_limit_bytes=24 * 2**20),
        name="mix",
    )(received, mix, *rest)
    result = lax.all_to_all(analysed, "member", split_axis=0, concat_axis=0, tiled=True)
    return jnp.transpose(result, (1, 0, 2, 3)).reshape(1, 4, rows, width)


def solution(mesh):
    return jax.shard_map(
        body,
        mesh=mesh,
        in_specs=(
            P("member", None, "tile", None),
            P("tile", None),
            P("tile", None),
            P("tile"),
            P("tile"),
            P("tile"),
            P("tile"),
            P("tile", "member", None),
            P("tile", "member"),
        ),
        out_specs=P("member", None, "tile", None),
        check_vma=False,
    )
```

```python
import functools

import jax
import jax.numpy as jnp
from jax import lax
from jax.experimental import pallas as pl
from jax.experimental.pallas import tpu as pltpu
from jax.sharding import PartitionSpec as P

REGION_POINTS = 256
STEPS = 4
NS_ITERS = 14
CELLS_PER_OBS = 8
LANES = 128

FRICTION = 0.98
PRESSURE = 0.25
DIVERGE = 0.25
FORCING = 0.05
UPWIND = 0.4
DAMPING = 0.02
HIGH = lax.Precision.HIGHEST

PAD = 8
PACKED = 2


def iota(shape, dim):
    return lax.broadcasted_iota(jnp.int32, shape, dim)


def edge_kernel(halo, *refs):
    grids, obs, outs = refs[:3], refs[3:7], refs[7:9]
    wet_ref, cell_ref, sems = refs[9:]
    rows = grids[1].shape[0]
    inner = obs[0].shape[0]
    even = lax.axis_index("tile") % 2 == 0
    copies = []

    def fetch(source, target):
        copies.append(pltpu.make_async_copy(source, target, sems.at[len(copies)]))
        copies[-1].start()

    for side, out in enumerate(outs):
        is_last = even if side == 0 else jnp.logical_not(even)
        start = pl.multiple_of(jnp.where(is_last, rows - halo, 0), 8)
        for i in range(6):
            source = (grids[0].at[i] if i < 4 else grids[i - 3]).at[pl.ds(start, halo), :]
            fetch(source, out.at[pl.ds(i * halo, halo), :] if i < 5 else wet_ref.at[side])
        start = pl.multiple_of(jnp.where(is_last, inner - 8, 0), 8)
        for j in range(4):
            target = out.at[pl.ds(6 * halo, 8), pl.ds(j * LANES, LANES)] if j else cell_ref.at[side]
            fetch(obs[j].at[pl.ds(start, 8), :], target)
    for copy in copies:
        copy.wait()
    for side, out in enumerate(outs):
        out[5 * halo : 6 * halo, :] = wet_ref[side].astype(jnp.float32)
        out[6 * halo : 6 * halo + 8, 0:LANES] = (cell_ref[side] % CELLS_PER_OBS).astype(jnp.float32)


def side_by_side(x, pairs):
    return jnp.concatenate([x[:pairs], x[pairs:]], axis=1)


def window_parts(win, own, near_ref, far_ref, base, j, even):
    inner = own.shape[0]
    span = (win.shape[0] - inner) // 2
    lanes = slice(j * LANES, (j + 1) * LANES)
    near, far = near_ref[base : base + 8, lanes], far_ref[base : base + 8, lanes]
    win[0:span, :] = jnp.where(even, far, near)[8 - span :, :]
    win[span : span + inner, :] = own
    win[span + inner :, :] = jnp.where(even, near, far)[:span, :]


def forecast_kernel(
    sizes,
    state_ref,
    depth_ref,
    mask_ref,
    cell_ref,
    gain_ref,
    near_ref,
    far_ref,
    *refs,
):
    members, own_rows, halo, obs_halo = sizes
    half = members // 2
    out_ref, equiv_ref, across_ref = refs[:3]
    along_refs, scratch = refs[3 : half + 3], refs[half + 3 :]
    s_ref, u_ref, v_ref, e_ref, h_ref, w_ref, flux_ref, part_ref, cell_win, gain_win, pack_ref, sem = scratch
    even = lax.axis_index("tile") % 2 == 0
    rows, width = depth_ref.shape
    pieces = width // LANES
    total = rows + 2 * halo
    first = PAD + halo
    own = pl.ds(first, rows)
    fields = (s_ref, u_ref, v_ref, e_ref, h_ref, w_ref)
    near_at = pl.multiple_of(jnp.where(even, first + rows, PAD), 8)
    far_at = pl.multiple_of(jnp.where(even, PAD, first + rows), 8)
    edge = jnp.zeros((PAD, LANES), jnp.float32)
    for q in range(pieces):
        lanes = slice(q * LANES, (q + 1) * LANES)
        for i, field in enumerate(fields):
            field[q, pl.ds(near_at, halo), :] = near_ref[i * halo : (i + 1) * halo, lanes]
            field[q, pl.ds(far_at, halo), :] = far_ref[i * halo : (i + 1) * halo, lanes]
            if i < 4:
                field[q, own, :] = state_ref[i, :, lanes]
        h_ref[q, own, :] = depth_ref[:, lanes]
        s_ref[q, PAD : PAD + total, :] *= PRESSURE
        h_ref[q, PAD : PAD + total, :] *= PRESSURE * DIVERGE
        w_ref[q, own, :] = mask_ref[:, lanes].astype(jnp.float32)
        for field in (s_ref, e_ref, flux_ref):
            field[q, 0:PAD, :] = edge
            field[q, PAD + total : PAD + total + PAD, :] = edge

    lane = iota((8, LANES), 1)
    at_first, at_last = lane == 0, lane == LANES - 1

    def across(x):
        ahead = [pltpu.roll(piece, LANES - 1, 1) for piece in x] + [0.0]
        behind = [0.0] + [pltpu.roll(piece, 1, 1) for piece in x]
        return [
            jnp.where(at_last, ahead[q + 1], ahead[q]) - jnp.where(at_first, behind[q], behind[q + 1])
            for q in range(pieces)
        ]

    outer = (halo - obs_halo * CELLS_PER_OBS // width) // 8
    for step in range(STEPS):
        skip, skip_energy = (outer, halo // 8) if step == STEPS - 1 else (0, 0)
        for block in range(total // 8):
            r = PAD + 8 * block
            here, below, above = pl.ds(r, 8), pl.ds(r + 1, 8), pl.ds(r - 1, 8)
            inside = skip <= block < total // 8 - skip
            s = [s_ref[q, here, :] for q in range(pieces)]
            slope = across(s) if inside else None
            flux = []
            for q in range(pieces):
                w, h = w_ref[q, here, :], h_ref[q, here, :]
                u = w * (FRICTION * u_ref[q, here, :] - (s_ref[q, below, :] - s_ref[q, above, :]))
                u_ref[q, here, :] = u
                flux_ref[q, here, :] = h * u
                if inside:
                    v = w * (FRICTION * v_ref[q, here, :] - slope[q])
                    v_ref[q, here, :] = v
                    flux.append(h * v)
            if inside:
                rise = across(flux)
                for q in range(pieces):
                    part_ref[q, here, :] = s[q] - rise[q] + (PRESSURE * FORCING) * e_ref[q, here, :]
        for block in reversed(range(skip, total // 8 - skip)):
            r = PAD + 8 * block
            here, below, above = pl.ds(r, 8), pl.ds(r + 1, 8), pl.ds(r - 1, 8)
            for q in range(pieces):
                w = w_ref[q, here, :]
                rise = flux_ref[q, below, :] - flux_ref[q, above, :]
                s_ref[q, here, :] = w * (part_ref[q, here, :] - rise)
                if skip_energy <= block < total // 8 - skip_energy:
                    e = e_ref[q, here, :]
                    e_ref[q, here, :] = w * ((1.0 - UPWIND - DAMPING) * e + UPWIND * e_ref[q, above, :])

    me = lax.axis_index("member")
    for j in range(members):
        source = first + j * own_rows
        for i in range(PACKED):
            for q in range(pieces):
                target = (i * pieces + q) * own_rows
                block = fields[i][q, source : source + own_rows, :]
                pack_ref[j, target : target + own_rows, :] = block if i else block * (1.0 / PRESSURE)
    sent = pltpu.make_async_copy(pack_ref, out_ref, sem)
    sent.start()

    window = cell_win.shape[0]
    base = 6 * halo
    offsets = (cell_ref[...] % CELLS_PER_OBS).astype(jnp.float32)
    window_parts(cell_win, offsets, near_ref, far_ref, base, 0, even)
    window_parts(gain_win, gain_ref[...], near_ref, far_ref, base, 1, even)
    half = width // CELLS_PER_OBS
    top = first - obs_halo // half
    column = iota((LANES, 2 * width), 1)
    cell_at = column // (2 * LANES) * LANES + column % LANES
    parity = column // LANES % 2
    spread = jnp.where(
        iota((LANES, 2 * width), 0) == parity * half + cell_at // CELLS_PER_OBS, 1.0, 0.0
    ).astype(jnp.bfloat16)
    offset = jnp.dot(cell_win[...].astype(jnp.bfloat16), spread, preferred_element_type=jnp.float32)
    level = jnp.concatenate(
        [s_ref[q, pl.ds(top + side, window, stride=2), :] for q in range(pieces) for side in range(2)], axis=1
    )
    place = (iota((window, 2 * width), 1) % CELLS_PER_OBS).astype(jnp.float32)
    rest = jnp.where(jnp.abs(offset - place) < 0.5, level, 0.0)
    equiv = jnp.zeros((window, LANES), jnp.float32)
    parts = []
    for i in range(3):
        parts.append(rest.astype(jnp.bfloat16))
        rest = rest - parts[-1].astype(jnp.float32)
    for part in reversed(parts):
        equiv = equiv + lax.dot_general(
            part, spread, (((1,), (1,)), ((), ())), preferred_element_type=jnp.float32
        )
    equiv = equiv * ((1.0 / PRESSURE) * gain_win[...])
    equiv_ref[...] = equiv
    across_ref[across_ref.shape[0] - window :, :] = equiv

    for j in range(members):
        source = pl.multiple_of(first + (me ^ j) * own_rows, min(own_rows, 8))
        for i in range(PACKED, 4):
            for q in range(pieces):
                target = ((i - PACKED) * pieces + q) * own_rows
                block = fields[i][q, pl.ds(source, own_rows), :]
                if j % 2:
                    target += j // 2 * (4 - PACKED) * pieces * own_rows
                    across_ref[target : target + own_rows, :] = block
                else:
                    along_refs[j // 2][target : target + own_rows, :] = block
    sent.wait()


def group_columns(left, starts, members):
    return [jnp.take_along_axis(left, starts + k, axis=1, mode="promise_in_bounds") for k in range(members)]


def group_matmul(columns, right):
    terms = [column * right[k : k + 1, :] for k, column in enumerate(columns)]
    while len(terms) > 1:
        terms = [a + b for a, b in zip(terms[::2], terms[1::2])]
    return terms[0]


def precision_kernel(
    sizes, list_ref, count_ref, value_ref, error_ref, near_ref, far_ref, out_ref, spot_ref, value_win, error_win
):
    halo, rows, width, radius = sizes
    window = value_win.shape[0]
    per_dev, slots = list_ref.shape
    obs_tile = value_ref.shape[0] * LANES
    even = lax.axis_index("tile") % 2 == 0
    window_parts(value_win, value_ref[...], near_ref, far_ref, 6 * halo, 2, even)
    window_parts(error_win, error_ref[...], near_ref, far_ref, 6 * halo, 3, even)
    named = list_ref[...]
    patch = iota((per_dev, slots), 0)
    row_index = (lax.axis_index("member") * per_dev + patch) * REGION_POINTS // width
    dist = (named - (obs_tile + row_index * obs_tile // rows)).astype(jnp.float32) / radius
    counts = jnp.zeros((per_dev, slots), jnp.int32)
    for p in range(per_dev):
        counts = jnp.where(patch == p, count_ref[0, p], counts)
    live = jnp.where(iota((per_dev, slots), 1) < counts, 1.0, 0.0)
    live = side_by_side(live, per_dev // 2)
    damp = side_by_side(1.0 + 4.0 * dist * dist, per_dev // 2)
    spot = side_by_side(named - (obs_tile - radius), per_dev // 2)
    spot_ref[...] = spot
    row, lane = spot // LANES, spot % LANES
    value = jnp.zeros(spot.shape, jnp.float32)
    error = jnp.zeros(spot.shape, jnp.float32)
    for r in range(window):
        hit = row == r
        line = jnp.broadcast_to(value_win[r : r + 1, :], spot.shape)
        value = jnp.where(hit, jnp.take_along_axis(line, lane, axis=1, mode="promise_in_bounds"), value)
        line = jnp.broadcast_to(error_win[r : r + 1, :], spot.shape)
        error = jnp.where(hit, jnp.take_along_axis(line, lane, axis=1, mode="promise_in_bounds"), error)
    out_ref[0] = value
    out_ref[1] = jnp.where(live > 0.0, 1.0 / (damp * error), 0.0)


def weight_kernel(members, three_ref, last_ref, *refs):
    half = members // 2
    near_refs, (spot_ref, known_ref, mix_ref, equiv_win) = refs[: half // 2 - 1], refs[half // 2 - 1 :]
    window = equiv_win.shape[0] // (members + 1)
    for i, ref in enumerate((three_ref, *near_refs)):
        for j, place in enumerate((2 * i, 2 * i + 1, 2 * i + half)):
            equiv_win[place * window : (place + 1) * window, :] = ref[j * window : (j + 1) * window, :]
        place = 2 * i + half + 1
        equiv_win[place * window : (place + 1) * window, :] = last_ref[i * window : (i + 1) * window, :]
    value, precision = known_ref[0], known_ref[1]

    spot = spot_ref[...]
    pairs = spot.shape[0]
    row, lane = spot // LANES, spot % LANES
    rows_of = [jnp.broadcast_to(row[i : i + 1, :], (members, LANES)) for i in range(pairs)]
    lanes_of = [jnp.broadcast_to(lane[i : i + 1, :], (members, LANES)) for i in range(pairs)]
    picked = [jnp.zeros((members, LANES), jnp.float32) for i in range(pairs)]
    for r in range(window):
        source = equiv_win[pl.ds(r, members, stride=window), :]
        for i in range(pairs):
            got = jnp.take_along_axis(source, lanes_of[i], axis=1, mode="promise_in_bounds")
            picked[i] = jnp.where(rows_of[i] == r, got, picked[i])

    left_half = iota((members, LANES), 1) < LANES // 2
    weighted, spreads, innovations = [], [], []
    for i in range(pairs):
        mean = jnp.sum(picked[i], axis=0, keepdims=True) * (1.0 / members)
        spread = picked[i] - mean
        scaled = spread * precision[i : i + 1, :]
        innovation = jnp.broadcast_to(value[i : i + 1, :] - mean, (members, LANES))
        weighted.append(scaled)
        spreads.append(spread)
        innovations.append(innovation)
    every = lax.dot_general(
        jnp.concatenate(
            [jnp.where(left_half, x, 0.0) for x in weighted] + [jnp.where(left_half, 0.0, x) for x in weighted],
            axis=0,
        ),
        jnp.concatenate(spreads + innovations, axis=0),
        (((1,), (1,)), ((), ())),
        preferred_element_type=jnp.float32,
        precision=HIGH,
    )
    lane_at = iota((members, LANES), 1)
    pair_at = lane_at // members % pairs
    sides = []
    for side in range(2):
        total = jnp.zeros((members, LANES), jnp.float32)
        for i in range(pairs):
            start = (side * pairs + i) * members
            total = jnp.where(pair_at == i, every[start : start + members, :], total)
        sides.append(total)
    gram = jnp.where(left_half, sides[0], pltpu.roll(sides[1], LANES // 2, 1))
    proj = jnp.where(left_half, pltpu.roll(sides[0], LANES // 2, 1), sides[1])

    starts = lane_at - lane_at % members
    eye = (lane_at % members == iota((members, LANES), 0)).astype(jnp.float32)
    amat = gram + (members - 1.0) * eye
    diagonal = jnp.broadcast_to(jnp.sum(amat * eye, axis=0, keepdims=True), (members, LANES))
    trace = functools.reduce(jnp.add, group_columns(diagonal, starts, members))

    def iterate(sweep, carry):
        product, inverse = carry
        columns = group_columns(product, starts, members)
        square = group_matmul(columns, product)
        cube = group_matmul(columns, square)
        return (
            2.25 * product - 1.5 * square + 0.25 * cube,
            1.5 * inverse - 0.5 * group_matmul(columns, inverse),
        )

    product, inverse = lax.fori_loop(0, NS_ITERS, iterate, (amat / trace, eye), unroll=members <= 8)
    root = inverse / jnp.sqrt(trace)
    columns = group_columns(root, starts, members)
    wbar = group_matmul(columns, group_matmul(columns, proj))
    wtot = ((members - 1.0) ** 0.5) * root + wbar
    mix = wtot - jnp.sum(wtot, axis=0, keepdims=True) * (1.0 / members) + 1.0 / members
    mix_ref[...] = mix


def mix_kernel(sizes, recv_ref, mix_ref, *refs):
    members, own_rows, pieces = sizes
    half = members // 2
    rest_refs, (out_ref, table_ref) = refs[: half + 1], refs[half + 1 :]
    rest_rows = (4 - PACKED) * pieces * own_rows
    stride = recv_ref.shape[0] // members
    me = lax.axis_index("member")
    table_ref[0:LANES, :] = mix_ref[...].T
    bases = [pl.multiple_of((me ^ d) * stride, 8) for d in range(members)]

    def analyse(m, carry):
        for side in range(2):
            coefs = table_ref[pl.ds(side * members + m, own_rows, stride=2 * members), :]
            columns = [jnp.broadcast_to(coefs[:, d : d + 1], (own_rows, LANES)) for d in range(members)]
            for i in range(4):
                for q in range(side * pieces // 2, (side + 1) * pieces // 2):
                    total = None
                    for d in range(members):
                        if i < PACKED:
                            start = (i * pieces + q) * own_rows
                            block = recv_ref[pl.ds(bases[d] + start, own_rows), :]
                        else:
                            start = ((i - PACKED) * pieces + q) * own_rows
                            if d >= 2:
                                start += d % 2 * rest_rows
                            block = rest_refs[d if d < 2 else d // 2 + 1][start : start + own_rows, :]
                        term = columns[d] * block
                        total = term if total is None else total + term
                    out_ref[me ^ m, i, :, q * LANES : (q + 1) * LANES] = total
        return carry

    if members <= 8:
        for m in range(members):
            analyse(m, 0)
    else:
        lax.fori_loop(0, members, analyse, 0)


def trade(block, distance):
    members = lax.axis_size("member")
    return lax.ppermute(block, "member", [(i, i ^ distance) for i in range(members)])


def trade_blocks(equiv, across, along):
    half = len(along)
    size = along[0].shape[0]
    window = equiv.shape[0]
    passed = trade(across, 1)
    far = trade(equiv, half)
    three = jnp.concatenate([equiv, passed[half * size :], far], axis=0)
    near = [trade(three, 2 * i) for i in range(1, half // 2)]
    last = trade(jnp.concatenate([far] + [x[2 * window :] for x in near], axis=0), 1)
    pairs = [
        trade(jnp.concatenate([along[i], passed[i * size : (i + 1) * size]], axis=0), 2 * i)
        for i in range(1, half)
    ]
    return three, last, near, [along[0], passed, *pairs]


def swaps(near, far):
    count = lax.axis_size("tile")

    def pairs(start):
        twos = [(i, i + 1) for i in range(start, count - 1, 2)]
        return twos + [(b, a) for a, b in twos]

    far = lax.ppermute(far, "tile", pairs(1))
    near = lax.ppermute(near, "tile", pairs(0))
    return near, far


def vmem_specs(count):
    return [pl.BlockSpec(memory_space=pltpu.VMEM)] * count


def body(
    realization_array,
    water_depth,
    wet_mask,
    obs_cell,
    obs_value,
    obs_error,
    celer_gain,
    obs_list,
    obs_count,
):
    members = lax.axis_size("member")
    rows, width = water_depth.shape
    obs_tile = obs_cell.shape[0]
    radius = obs_tile // 8
    halo = radius * CELLS_PER_OBS // width + 2 * STEPS
    per_dev, slots = obs_list.shape[1:]
    own_rows = per_dev * REGION_POINTS // width
    pieces = width // LANES
    state = realization_array[0]
    panel = (obs_tile // LANES, LANES)
    pairs = per_dev * slots // LANES
    edges = pl.pallas_call(
        functools.partial(edge_kernel, halo),
        out_shape=[pltpu.VMEM((6 * halo + 8, width), jnp.float32)] * 2,
        in_specs=[pl.BlockSpec(memory_space=pl.ANY)] * 7,
        out_specs=vmem_specs(2),
        scratch_shapes=[
            pltpu.VMEM((2, halo, width), jnp.int32),
            pltpu.VMEM((2, 8, LANES), jnp.int32),
            pltpu.SemaphoreType.DMA((20,)),
        ],
        name="edges",
    )(
        state,
        water_depth,
        wet_mask,
        obs_cell.reshape(panel),
        celer_gain.reshape(panel),
        obs_value.reshape(panel),
        obs_error.reshape(panel),
    )
    near, far = swaps(*edges)

    window = (obs_tile + 2 * radius) // LANES
    packet = PACKED * pieces * own_rows
    grid = (pieces, rows + 2 * halo + 2 * PAD, LANES)
    half = members // 2
    rest_rows = (4 - PACKED) * pieces * own_rows
    sends, equiv, across, *along = pl.pallas_call(
        functools.partial(forecast_kernel, (members, own_rows, halo, radius)),
        out_shape=[
            jax.ShapeDtypeStruct((members, packet, LANES), jnp.float32),
            jax.ShapeDtypeStruct((window, LANES), jnp.float32),
            jax.ShapeDtypeStruct((half * rest_rows + window, LANES), jnp.float32),
        ]
        + [jax.ShapeDtypeStruct((rest_rows, LANES), jnp.float32)] * half,
        in_specs=vmem_specs(7),
        out_specs=[pl.BlockSpec(memory_space=pl.ANY)] + vmem_specs(2 + half),
        scratch_shapes=[pltpu.VMEM(grid, jnp.float32)] * 8
        + [pltpu.VMEM((window, LANES), jnp.float32)] * 2
        + [pltpu.VMEM((members, packet, LANES), jnp.float32), pltpu.SemaphoreType.DMA],
        compiler_params=pltpu.CompilerParams(vmem_limit_bytes=24 * 2**20),
        name="forecast",
    )(
        state,
        water_depth,
        wet_mask,
        obs_cell.reshape(panel),
        celer_gain.reshape(panel),
        near,
        far,
    )
    received = lax.all_to_all(sends, "member", split_axis=0, concat_axis=0, tiled=True)
    three, last, near_equivs, rest = trade_blocks(equiv, across, along)
    received = received.reshape(members * packet, LANES)

    known, spot = pl.pallas_call(
        functools.partial(precision_kernel, (halo, rows, width, radius)),
        out_shape=[pltpu.VMEM((2, pairs, LANES), jnp.float32), pltpu.VMEM((pairs, LANES), jnp.int32)],
        in_specs=vmem_specs(1) + [pl.BlockSpec(memory_space=pltpu.SMEM)] + vmem_specs(4),
        out_specs=vmem_specs(2),
        scratch_shapes=[pltpu.VMEM((window, LANES), jnp.float32)] * 2,
        name="precision",
    )(
        obs_list[0],
        obs_count,
        obs_value.reshape(panel),
        obs_error.reshape(panel),
        near,
        far,
    )
    mix = pl.pallas_call(
        functools.partial(weight_kernel, members),
        out_shape=jax.ShapeDtypeStruct((members, LANES), jnp.float32),
        in_specs=vmem_specs(4 + len(near_equivs)),
        out_specs=vmem_specs(1)[0],
        scratch_shapes=[pltpu.VMEM(((members + 1) * window, LANES), jnp.float32)],
        compiler_params=pltpu.CompilerParams(vmem_limit_bytes=24 * 2**20),
        name="weights",
    )(three, last, *near_equivs, spot, known)
    analysed = pl.pallas_call(
        functools.partial(mix_kernel, (members, own_rows, pieces)),
        out_shape=jax.ShapeDtypeStruct((members, 4, own_rows, width), jnp.float32),
        in_specs=vmem_specs(3 + half),
        out_specs=vmem_specs(1)[0],
        scratch_shapes=[pltpu.VMEM((LANES + 2 * members, members), jnp.float32)],
        compiler_params=pltpu.CompilerParams(vmem_limit_bytes=24 * 2**20),
        name="mix",
    )(received, mix, *rest)
    result = lax.all_to_all(analysed, "member", split_axis=0, concat_axis=0, tiled=True)
    return jnp.transpose(result, (1, 0, 2, 3)).reshape(1, 4, rows, width)


def solution(mesh):
    return jax.shard_map(
        body,
        mesh=mesh,
        in_specs=(
            P("member", None, "tile", None),
            P("tile", None),
            P("tile", None),
            P("tile"),
            P("tile"),
            P("tile"),
            P("tile"),
            P("tile", "member", None),
            P("tile", "member"),
        ),
        out_specs=P("member", None, "tile", None),
        check_vma=False,
    )
```
